32 devices in a mesh: img: 8 (over z, x), win: 4 (over y, core).
Axes of the slice: x: 2, y: 2, z: 4, core: 2. Of those that a mesh axis runs over, the one named last changes fastest.
Arguments:
- inputs: bfloat16 [32, 4, 256, 512], P('img', 'win'), may hold values from -6 to 6
- query_key_value_weight: bfloat16 [512, 1536], replicated, may hold values from -0.25 to 0.25
- query_bias: float32 [512], replicated, may hold values from -3 to 3
- value_bias: float32 [512], replicated, may hold values from -3 to 3
- head_log_scale: float32 [16], replicated, may hold values from 1 to 2.5
- bias_net_first_weight: float32 [2, 512], replicated, may hold values from -5 to 5
- bias_net_first_bias: float32 [512], replicated, may hold values from -3 to 3
- bias_net_second_weight: float32 [512, 16], replicated, may hold values from -0.25 to 0.25
- attention_out_weight: bfloat16 [512, 512], replicated, may hold values from -0.25 to 0.25
- attention_out_bias: float32 [512], replicated, may hold values from -2 to 2
- attention_norm_gain: float32 [512], replicated, may hold values from 0.5 to 1.5
- attention_norm_bias: float32 [512], replicated, may hold values from -2 to 2
- expand_weight: bfloat16 [512, 2048], replicated, may hold values from -0.25 to 0.25
- expand_bias: float32 [2048], replicated, may hold values from -2 to 2
- contract_weight: bfloat16 [2048, 512], replicated, may hold values from -0.125 to 0.125
- contract_bias: float32 [512], replicated, may hold values from -2 to 2
- feedforward_norm_gain: float32 [512], replicated, may hold values from 0.5 to 1.5
- feedforward_norm_bias: float32 [512], replicated, may hold values from -2 to 2
- cotangent: bfloat16 [32, 4, 256, 512], P('img', 'win'), may hold values from -6 to 6
Outputs:
- result: bfloat16 [32, 4, 256, 512], P('img', 'win')
- grad_inputs: bfloat16 [32, 4, 256, 512], P('img', 'win')
- grad_w_qkv: float32 [512, 1536], replicated
- grad_q_bias: float32 [512], replicated
- grad_v_bias: float32 [512], replicated
- grad_logit_scale: float32 [16], replicated
- gradient_net_first_weight: float32 [2, 512], replicated
- gradient_net_first_bias: float32 [512], replicated
- gradient_net_second_weight: float32 [512, 16], replicated
- grad_w_proj: float32 [512, 512], replicated
- grad_b_proj: float32 [512], replicated
- grad_ln1_gain: float32 [512], replicated
- grad_ln1_bias: float32 [512], replicated
- grad_w_fc1: float32 [512, 2048], replicated
- grad_b_fc1: float32 [2048], replicated
- grad_w_fc2: float32 [2048, 512], replicated
- grad_b_fc2: float32 [512], replicated
- grad_ln2_gain: float32 [512], replicated
- grad_ln2_bias: float32 [512], replicated
The draws below stay inside these ranges and needn't reach their ends.
All inputs are finite; a program needn't handle non-finite values.
Results may differ from the reference program's by a relative error of at most 0.03.
Values may be sent and summed in bfloat16 or wider, within the bound.
A program may use at most 256 MiB of HBM per device.

```python
import jax
import jax.numpy as jnp
from jax import lax

WIDTH = 512
ATTENTION_HEADS = 16
HEAD_DIM = 32
HIDDEN_SIZE = 2048
BIAS_NET_UNITS = 512
WIN = 16
IMAGES = 32


def block_levels(key, shape, pieces, least, high):
    def one(axis_at, shards_of):
        steps = jax.random.uniform(jax.random.fold_in(jax.random.fold_in(key, 6), axis_at), (shards_of,), jnp.float32, least / len(pieces), high / len(pieces))
        return jnp.repeat(jnp.exp(steps), shape[axis_at] // shards_of).reshape((-1,) + (1,) * (len(shape) - axis_at - 1))

    level = one(*pieces[0])
    for cut in pieces[1:]:
        level = level * one(*cut)
    return level


def gaussian(own_key, shape, scale, limit, pieces=(), kind=jnp.bfloat16):
    values = jax.random.normal(own_key, shape, jnp.float32) * scale
    if len(pieces) > 0:
        values = block_levels(own_key, shape, pieces, -0.22, 0.18) * values
    return jnp.clip(values, min=-limit, max=limit).astype(kind)


def setup_inputs(seed: int = 0) -> dict:
    arg_keys = jax.random.split(jax.random.key(seed), 20)
    return {
        "inputs": gaussian(arg_keys[0], (IMAGES, 4, WIN * WIN, WIDTH), 1.0, 6.0, ((0, 8), (1, 4))),
        "query_key_value_weight": gaussian(arg_keys[1], (WIDTH, 3 * WIDTH), WIDTH ** -0.5, 0.25),
        "query_bias": gaussian(arg_keys[2], (WIDTH,), 0.5, 3.0, (), jnp.float32),
        "value_bias": gaussian(arg_keys[3], (WIDTH,), 0.5, 3.0, (), jnp.float32),
        "head_log_scale": jnp.clip(jax.random.uniform(arg_keys[4], (ATTENTION_HEADS,), jnp.float32, 1.0, 2.5), 1.0, 2.5),
        "bias_net_first_weight": gaussian(arg_keys[5], (2, BIAS_NET_UNITS), 1.0, 5.0, (), jnp.float32),
        "bias_net_first_bias": gaussian(arg_keys[6], (BIAS_NET_UNITS,), 0.5, 3.0, (), jnp.float32),
        "bias_net_second_weight": gaussian(arg_keys[7], (BIAS_NET_UNITS, ATTENTION_HEADS), BIAS_NET_UNITS ** -0.5, 0.25, (), jnp.float32),
        "attention_out_weight": gaussian(arg_keys[8], (WIDTH, WIDTH), WIDTH ** -0.5, 0.25),
        "attention_out_bias": gaussian(arg_keys[9], (WIDTH,), 0.3, 2.0, (), jnp.float32),
        "attention_norm_gain": jnp.clip(1.0 + 0.1 * jax.random.normal(arg_keys[10], (WIDTH,), jnp.float32), 0.5, 1.5),
        "attention_norm_bias": gaussian(arg_keys[11], (WIDTH,), 0.3, 2.0, (), jnp.float32),
        "expand_weight": gaussian(arg_keys[12], (WIDTH, HIDDEN_SIZE), WIDTH ** -0.5, 0.25),
        "expand_bias": gaussian(arg_keys[13], (HIDDEN_SIZE,), 0.3, 2.0, (), jnp.float32),
        "contract_weight": gaussian(arg_keys[14], (HIDDEN_SIZE, WIDTH), HIDDEN_SIZE ** -0.5, 0.125),
        "contract_bias": gaussian(arg_keys[15], (WIDTH,), 0.3, 2.0, (), jnp.float32),
        "feedforward_norm_gain": jnp.clip(1.0 + 0.1 * jax.random.normal(arg_keys[16], (WIDTH,), jnp.float32), 0.5, 1.5),
        "feedforward_norm_bias": gaussian(arg_keys[17], (WIDTH,), 0.3, 2.0, (), jnp.float32),
        "cotangent": gaussian(arg_keys[18], (IMAGES, 4, WIN * WIN, WIDTH), 1.0, 6.0, ((0, 8), (1, 4))),
    }


EPS_DIR = 1e-06
EPS_NORM = 1e-05
MASK_FILL = -100.0
BIAS_RANGE = 16.0
EXACT_PRECISION = lax.Precision.HIGHEST

@jax.custom_vjp
def low(v):
    return lax.optimization_barrier(v.astype(jnp.bfloat16)).astype(jnp.float32)

@jax.custom_vjp
def low_back(v):
    return v

def low_keep(v):
    return (low(v), None)

def low_pass(kept, grad):
    return (grad,)

def back_keep(v):
    return (v, None)

def back_low(kept, grad):
    return (low(grad),)
low.defvjp(low_keep, low_pass)
low_back.defvjp(back_keep, back_low)

def matmul(first_op, second_op):
    return jnp.matmul(first_op, second_op, precision=EXACT_PRECISION)

def gaussian_error_unit(values):
    return 0.5 * values * (1.0 + jax.scipy.special.erf(values * 0.7071067811865476))

def layer_norm(values, gain, shift_add):
    center = values - lax.optimization_barrier(jnp.mean(values, axis=-1, keepdims=True))
    spread = lax.optimization_barrier(jnp.mean(center * center, axis=-1, keepdims=True))
    return center * lax.rsqrt(spread + EPS_NORM) * gain + shift_add

def log_table():
    span_count = 2 * WIN - 1
    offsets = jnp.arange(-(WIN - 1), WIN).astype(jnp.float32) * (8.0 / (WIN - 1))
    spaced = jnp.sign(offsets) * jnp.log2(jnp.abs(offsets) + 1.0) / 3.0
    row_part = jnp.broadcast_to(spaced[:, None], (span_count, span_count))
    col_part = jnp.broadcast_to(spaced[None, :], (span_count, span_count))
    return jnp.stack([row_part, col_part], axis=-1)

def relative_position_bias(bias_net_first_weight, bias_net_first_bias, bias_net_second_weight):
    span_count = 2 * WIN - 1
    coordinates = log_table().reshape(span_count * span_count, 2)
    hidden_units = gaussian_error_unit(jnp.dot(coordinates, bias_net_first_weight, precision=EXACT_PRECISION) + bias_net_first_bias)
    score_logits = jnp.dot(hidden_units, bias_net_second_weight, precision=EXACT_PRECISION)
    lookup = BIAS_RANGE / (1.0 + jnp.exp(-score_logits))
    places = jnp.arange(WIN * WIN).astype(jnp.int32)
    row_ids = places // WIN
    col_ids = places % WIN
    index_pair = (row_ids[:, None] - row_ids[None, :] + WIN - 1) * span_count + (col_ids[:, None] - col_ids[None, :] + WIN - 1)
    return jnp.transpose(lookup[index_pair], (2, 0, 1))

def region(coord_ids):
    return (coord_ids >= WIN).astype(jnp.int32) + (coord_ids >= 3 * WIN // 2).astype(jnp.int32)

def shifted_window_masks():
    places = jnp.arange(WIN * WIN).astype(jnp.int32)
    blocks = []
    for window in range(4):
        row_ids = window // 2 * WIN + places // WIN
        col_ids = window % 2 * WIN + places % WIN
        labels = region(row_ids) * 3 + region(col_ids)
        blocks.append(jnp.where(labels[:, None] == labels[None, :], 0.0, MASK_FILL))
    return jnp.stack(blocks).astype(jnp.float32)

def to_grid(tokens):
    groups = tokens.shape[0]
    model_width = tokens.shape[-1]
    shaped = tokens.reshape(groups, 2, 2, WIN, WIN, model_width).transpose(0, 1, 3, 2, 4, 5)
    return shaped.reshape(groups, 2 * WIN, 2 * WIN, model_width)

def to_windows(grid):
    groups = grid.shape[0]
    model_width = grid.shape[-1]
    shaped = grid.reshape(groups, 2, WIN, 2, WIN, model_width).transpose(0, 1, 3, 2, 4, 5)
    return shaped.reshape(groups, 4, WIN * WIN, model_width)

def forward(tokens, block_parameters):
    query_key_value_weight, query_bias, value_bias, head_log_scale, bias_net_first_weight, bias_net_first_bias, bias_net_second_weight, attention_out_weight, attention_out_bias, attention_norm_gain, attention_norm_bias, expand_weight, expand_bias, contract_weight, contract_bias, feedforward_norm_gain, feedforward_norm_bias = block_parameters
    groups = tokens.shape[0]
    shift_by = WIN // 2
    moved = to_windows(jnp.roll(to_grid(tokens), (-shift_by, -shift_by), axis=(1, 2)))
    moved = low_back(moved)
    joint_qkv = matmul(moved, query_key_value_weight) + jnp.concatenate([query_bias, jnp.zeros_like(query_bias), value_bias])
    joint_qkv = low_back(joint_qkv).reshape(groups, 4, WIN * WIN, 3, ATTENTION_HEADS, HEAD_DIM)
    query_raw = joint_qkv[:, :, :, 0]
    key_raw = joint_qkv[:, :, :, 1]
    value_low = low(joint_qkv[:, :, :, 2])
    query_low = low(query_raw * lax.rsqrt(lax.optimization_barrier(jnp.sum(query_raw * query_raw, axis=-1, keepdims=True)) + EPS_DIR))
    key_low = low(key_raw * lax.rsqrt(lax.optimization_barrier(jnp.sum(key_raw * key_raw, axis=-1, keepdims=True)) + EPS_DIR))
    cosine_scores = jnp.einsum('gwnhd,gwmhd->gwhnm', query_low, key_low, precision=EXACT_PRECISION)
    attention_logits = cosine_scores * jnp.exp(head_log_scale)[:, None, None] + relative_position_bias(bias_net_first_weight, bias_net_first_bias, bias_net_second_weight) + shifted_window_masks()[:, None]
    attention_logits = low_back(attention_logits)
    row_peak = lax.optimization_barrier(jnp.max(attention_logits, axis=-1, keepdims=True))
    row_exp = jnp.exp(attention_logits - row_peak)
    soft_probs = low(row_exp / lax.optimization_barrier(jnp.sum(row_exp, axis=-1, keepdims=True)))
    mixed_heads = jnp.einsum('gwhnm,gwmhd->gwnhd', soft_probs, value_low, precision=EXACT_PRECISION)
    mixed_heads = low(low_back(mixed_heads)).reshape(groups, 4, WIN * WIN, WIDTH)
    branch = low(low_back(matmul(mixed_heads, attention_out_weight) + attention_out_bias))
    branch_back = to_windows(jnp.roll(to_grid(branch), (shift_by, shift_by), axis=(1, 2)))
    middle = tokens + layer_norm(branch_back, attention_norm_gain, attention_norm_bias)
    hidden_units = low_back(matmul(low(middle), expand_weight) + expand_bias)
    active = low(gaussian_error_unit(hidden_units))
    output = low_back(matmul(active, contract_weight) + contract_bias)
    return middle + layer_norm(output, feedforward_norm_gain, feedforward_norm_bias)

def reference(inputs, query_key_value_weight, query_bias, value_bias, head_log_scale, bias_net_first_weight, bias_net_first_bias, bias_net_second_weight, attention_out_weight, attention_out_bias, attention_norm_gain, attention_norm_bias, expand_weight, expand_bias, contract_weight, contract_bias, feedforward_norm_gain, feedforward_norm_bias, cotangent):
    block_parameters = tuple((window_member.astype(jnp.float32) for window_member in (query_key_value_weight, query_bias, value_bias, head_log_scale, bias_net_first_weight, bias_net_first_bias, bias_net_second_weight, attention_out_weight, attention_out_bias, attention_norm_gain, attention_norm_bias, expand_weight, expand_bias, contract_weight, contract_bias, feedforward_norm_gain, feedforward_norm_bias)))
    group_count = IMAGES // 4
    tokens_all = inputs.astype(jnp.float32).reshape(group_count, 4, 4, WIN * WIN, WIDTH)
    cot_all = cotangent.astype(jnp.float32).reshape(group_count, 4, 4, WIN * WIN, WIDTH)

    def group_step(grad_total, block_pair):
        block_in, block_cot = block_pair
        block_out, pullback = jax.vjp(forward, block_in, block_parameters)
        grad_in, grad_params = pullback(block_cot)
        grad_total = jax.tree.map(jnp.add, grad_total, grad_params)
        return (grad_total, (block_out.astype(jnp.bfloat16), grad_in.astype(jnp.bfloat16)))
    zero_grads = tuple((jnp.zeros_like(window_member) for window_member in block_parameters))
    grad_total, (outs_all, grads_in) = lax.scan(group_step, zero_grads, (tokens_all, cot_all))
    return (outs_all.reshape(inputs.shape), grads_in.reshape(inputs.shape), grad_total[0], grad_total[1], grad_total[2], grad_total[3], grad_total[4], grad_total[5], grad_total[6], grad_total[7], grad_total[8], grad_total[9], grad_total[10], grad_total[11], grad_total[12], grad_total[13], grad_total[14], grad_total[15], grad_total[16])
```

```python
import functools

import jax
import jax.numpy as jnp
import numpy as np
from jax import lax
from jax.experimental import pallas as pl
from jax.experimental.pallas import tpu as pltpu
from jax.sharding import PartitionSpec as P

WIN = 16
TOK = WIN * WIN
EPS_DIR = 1e-06
EPS_NORM = 1e-05
MASK_FILL = -100.0
BIAS_RANGE = 16.0
INV_ROOT_TWO = 0.7071067811865476
INV_ROOT_TWOPI = 0.3989422804014327
MESH = pl.DeviceIdType.MESH
BF = jnp.bfloat16
F32 = jnp.float32

(ROW_QB, ROW_VB, ROW_LS, ROW_W1, ROW_B1, ROW_W2, ROW_BP, ROW_G1, ROW_S1, ROW_B2, ROW_G2, ROW_S2,
 ROW_BE, SMALL_ROWS) = (0, 1, 2, 3, 5, 6, 22, 23, 24, 25, 26, 27, 28, 32)


def nn(a, b):
    return lax.dot_general(a, b, (((1,), (0,)), ((), ())), preferred_element_type=F32)


def nt(a, b):
    return lax.dot_general(a, b, (((1,), (1,)), ((), ())), preferred_element_type=F32)


def tn(a, b):
    return lax.dot_general(a, b, (((0,), (0,)), ((), ())), preferred_element_type=F32)


def split3(v):
    hi = v.astype(BF)
    rest = v - hi.astype(F32)
    mid = rest.astype(BF)
    return hi, mid, (rest - mid.astype(F32)).astype(BF)


def gelu_parts(v):
    ex = jnp.exp(-0.5 * v * v)
    d = 1.0 + (0.3275911 * INV_ROOT_TWO) * jnp.abs(v)
    t = pl.reciprocal(d, approx=True)
    t = t * (2.0 - d * t)
    poly = t * (
        0.127414796 + t * (-0.142248368 + t * (0.7107068705 + t * (-0.7265760135 + t * 0.5307027145)))
    )
    tail = poly * ex
    return jnp.where(v >= 0.0, 1.0 - tail, tail), ex * INV_ROOT_TWOPI


def col_sum(v):
    return jnp.sum(v.reshape(v.shape[0] // 8, 8, v.shape[1]), axis=0)


def to_blocks(v):
    n = v.shape[-1]
    t = v.reshape(2, 8, 2, 8, n)
    return [[t[qr, :, qc].reshape(64, n) for qc in range(2)] for qr in range(2)]


def from_blocks(quads):
    n = quads[0][0].shape[-1]
    rows = []
    for qr in range(2):
        a = quads[qr][0].reshape(8, 1, 8, n)
        b = quads[qr][1].reshape(8, 1, 8, n)
        rows.append(jnp.concatenate([a, b], axis=1).reshape(128, n))
    return jnp.concatenate(rows, axis=0)


def one_hot_places(c):
    l = lax.broadcasted_iota(jnp.int32, (256, 512), 0)
    k = lax.broadcasted_iota(jnp.int32, (256, 512), 1) + 512 * c
    return jnp.where(l == 8 * (15 - k // 128) + k % 128, 1.0, 0.0).astype(BF)


def one_hot_pick():
    k = lax.broadcasted_iota(jnp.int32, (1024, 256), 0)
    l = lax.broadcasted_iota(jnp.int32, (1024, 256), 1)
    return jnp.where(k == 32 * (l // 8) + l % 8, 1.0, 0.0).astype(BF)


def table_coords():
    k = np.arange(1024)
    out = np.zeros((2, 1024), np.float64)
    for i, off in enumerate((15 - k // 32, 15 - k % 32)):
        u = off * (8.0 / 15.0)
        out[i] = np.sign(u) * np.log2(np.abs(u) + 1.0) / 3.0
    rows = np.zeros((8, 1024), np.float32)
    rows[0:2] = out
    rows[2] = 1.0
    cols = np.zeros((1024, 8), np.float32)
    cols[:, 0:2] = out.T
    return rows, cols


def net_first(cols, w1, b1):
    return cols[:, 0:1] * w1[0:1, :] + cols[:, 1:2] * w1[1:2, :] + b1


def block_kernel(
    n_img, n_win,
    x_hbm, cot_hbm, wqkv, wproj, we, wc, qb, vb, hls, w1, b1, w2t, bproj, g1, s1, be, bc, g2, s2,
    crow, ccol,
    res_hbm, gin_hbm, sums_hbm, small_out,
    xr, cr, xroll, bias, ex, qs, kl, vl, qinv, kinv, isum, mixed, mixlo, blk, dmid, act, dhid, dout,
    mlow, slope, tab, part, acc_s, asum, rcore, rone, rtwo, rz, own, small_s, small_r,
    s_x, r_x, s_c, r_c, s_res, r_res, s_gin, r_gin, s_ar, r_ar, l_ar, s_sm, r_sm,
):
    img = lax.axis_index("img")
    me = lax.axis_index("win")
    extra = n_img // 8
    core = lax.rem(me, 2)
    ypos = me // 2
    xpos = lax.rem(img, 2)
    zpos = lax.rem(img // 2, 4)
    upper = img // 8

    def ring_to(k):
        return (img, lax.rem(me + k, n_win))

    def ring_from(k):
        return lax.rem(me + n_win - k, n_win)

    core_peer = (img, me + 1 - 2 * core)
    y_peer = (img, lax.rem(me + 2, 4))
    x_peer = (img + 1 - 2 * xpos, me)

    def z_peer(k):
        return (upper * 8 + lax.rem(zpos + k, 4) * 2 + xpos, me)

    def far_peer(k):
        return (lax.rem(upper + k, extra) * 8 + zpos * 2 + xpos, me)

    barrier = pltpu.get_barrier_semaphore()
    others = [ring_to(k) for k in range(1, n_win)] + [x_peer]
    others += [z_peer(k) for k in range(1, 4)] + [far_peer(k) for k in range(1, extra)]
    for peer in others:
        pl.semaphore_signal(barrier, inc=1, device_id=peer, device_id_type=MESH)
    pl.semaphore_wait(barrier, len(others))

    def remote(src, dst, ssem, rsem, peer):
        return pltpu.make_async_remote_copy(
            src_ref=src, dst_ref=dst, send_sem=ssem, recv_sem=rsem, device_id=peer, device_id_type=MESH
        )

    def spread(src_hbm, dst, ssem, rsem, k):
        to = lax.rem(me + k, n_win)
        return remote(src_hbm.at[to, 0], dst.at[me], ssem.at[k], rsem.at[k], ring_to(k))

    def spread_in(src_hbm, dst, ssem, rsem, k):
        frm = ring_from(k)
        return remote(src_hbm.at[frm, 0], dst.at[frm], ssem.at[k], rsem.at[k], ring_to(k))

    def own_part(src_hbm, dst, sem):
        return pltpu.make_async_copy(src_hbm.at[me, 0], dst.at[me], sem.at[0])

    for k in (2, 1, 3):
        spread(x_hbm, xr, s_x, r_x, k).start()
    own_part(x_hbm, xr, r_x).start()

    def net_piece(c):
        rows = pl.ds(pl.multiple_of(256 * c, 256), 256)
        return rows, net_first(ccol[rows, :], w1[...], b1[...][None, :])

    def look_up(c, _):
        cols, pre = net_piece(c)
        logits = lax.dot_general(
            w2t[...], pre * gelu_parts(pre)[0], (((1,), (1,)), ((), ())),
            precision=lax.Precision.HIGHEST, preferred_element_type=F32,
        )
        tab[:, cols] = BIAS_RANGE / (1.0 + jnp.exp(-logits))
        return 0

    lax.fori_loop(0, 4, look_up, 0)
    for u in range(24):
        part[:, u, :] = pltpu.roll(tab[...], 1001 + u, 1)
    pick = one_hot_pick()
    short = jnp.concatenate(
        [sum(nn(p, pick) for p in split3(part[4 * i : 4 * i + 4].reshape(96, 1024))) for i in range(4)], axis=0
    )
    short_parts = split3(short)
    for c in range(4):
        places = one_hot_places(c)
        wide = sum(nn(p, places) for p in short_parts)
        for r in range(4):
            row = 8 * (4 * c + r)
            bias[:, :, row : row + 8, :] = wide[:, 128 * r : 128 * r + 128].reshape(16, 3, 8, 128)

    lane = lax.broadcasted_iota(jnp.int32, (1, 128), 1)
    head_mask = [jnp.where(lane // 32 == hh, 1.0, 0.0).astype(BF) for hh in range(4)]
    l0 = lax.broadcasted_iota(jnp.int32, (256, 256), 0)
    l1 = lax.broadcasted_iota(jnp.int32, (256, 256), 1)
    head_ones = jnp.where(l0 // 32 == l1 // 32, 1.0, 0.0).astype(BF)

    def scale_lanes(p):
        wide = lax.broadcasted_iota(jnp.int32, (1, 256), 1) // 32
        out = jnp.zeros((1, 256), F32)
        for i in range(8):
            out = jnp.where(wide == i, hls[8 * p + i], out)
        return jnp.exp(out)

    for k in (0, 1, 2, 3):
        if k == 0:
            own_part(x_hbm, xr, r_x).wait()
        else:
            spread_in(x_hbm, xr, s_x, r_x, k).wait_recv()
    for k in (2, 1, 3):
        spread(cot_hbm, cr, s_c, r_c, k).start()
    own_part(cot_hbm, cr, r_c).start()

    def lay(w, _):
        quads = to_blocks(xr[w].astype(F32))
        for qr in range(2):
            for qc in range(2):
                br, bcol = 1 - qr, 1 - qc
                orow = w // 2 if br == 0 else 1 - w // 2
                ocol = lax.rem(w, 2) if bcol == 0 else 1 - lax.rem(w, 2)
                at = (bcol * 2 + br) * 64
                xroll[2 * orow + ocol, at : at + 64, :] = quads[qr][qc].astype(BF)
        return 0

    lax.fori_loop(0, 4, lay, 0)

    row_half = lax.broadcasted_iota(jnp.int32, (128, 128), 0) // 64
    col_half = lax.broadcasted_iota(jnp.int32, (128, 128), 1) // 64
    apart = jnp.where(row_half == col_half, 0.0, MASK_FILL)

    def home(o, bcol, br):
        return lax.rem(2 * (o // 2) + br + 1, 4), lax.rem(2 * lax.rem(o, 2) + bcol + 1, 4)

    def attend(o, _):
        xw = xroll[o]
        for p in range(2):
            cols = slice(256 * p, 256 * p + 256)
            q = nn(xw, wqkv[:, cols]) + qb[cols][None, :]
            qi = lax.rsqrt(nn((q * q).astype(BF), head_ones) + EPS_DIR)
            qsc = (q * qi * scale_lanes(p)).astype(BF)
            k = nn(xw, wqkv[:, 512 + 256 * p : 768 + 256 * p])
            ki = lax.rsqrt(nn((k * k).astype(BF), head_ones) + EPS_DIR)
            kn = (k * ki).astype(BF)
            v = (nn(xw, wqkv[:, 1024 + 256 * p : 1280 + 256 * p]) + vb[cols][None, :]).astype(BF)
            for i in range(2):
                half = slice(128 * i, 128 * i + 128)
                qs[o, 2 * p + i] = qsc[:, half]
                kl[o, 2 * p + i] = kn[:, half]
                vl[o, 2 * p + i] = v[:, half]
                qinv[o, 2 * p + i] = qi[:, half].astype(BF)
                kinv[o, 2 * p + i] = ki[:, half].astype(BF)
        rows_cut = jnp.where(o // 2 == 1, apart, 0.0)
        cols_cut = jnp.where(lax.rem(o, 2) == 1, jnp.full((128, 128), MASK_FILL, F32), rows_cut)

        for g in range(4):
            qg, kg, vg = qs[o, g], kl[o, g], vl[o, g]
            total = jnp.zeros((256, 256), F32)
            for hh in range(4):
                h = 4 * g + hh
                sc = nt(qg * head_mask[hh], kg)
                ex[o, g, hh, 0:128, 0:128] = jnp.exp(sc[0:128, 0:128] + bias[h, 1] + rows_cut).astype(BF)
                ex[o, g, hh, 0:128, 128:256] = jnp.exp(sc[0:128, 128:256] + bias[h, 0] + cols_cut).astype(BF)
                ex[o, g, hh, 128:256, 0:128] = jnp.exp(sc[128:256, 0:128] + bias[h, 2] + cols_cut).astype(BF)
                ex[o, g, hh, 128:256, 128:256] = jnp.exp(sc[128:256, 128:256] + bias[h, 1] + rows_cut).astype(BF)
                ones = jnp.broadcast_to(head_mask[hh], (256, 128))
                total = total + nn(ex[o, g, hh], jnp.concatenate([vg * head_mask[hh], ones], axis=1))
            inv = 1.0 / total[:, 128:256]
            isum[o, g] = inv
            mix = total[:, 0:128] * inv
            mix_hi = mix.astype(BF)
            mixed[o, :, 128 * g : 128 * g + 128] = mix_hi
            mixlo[o, :, 128 * g : 128 * g + 128] = (mix - mix_hi.astype(F32)).astype(BF)

        branch = (nn(mixed[o], wproj[...]) + bproj[...][None, :]).astype(BF)
        for bcol in range(2):
            for br in range(2):
                at = (bcol * 2 + br) * 64
                brow, bc_ = home(o, bcol, br)
                blk[brow, bc_] = branch[at : at + 64, :]
        return 0

    lax.fori_loop(0, 4, attend, 0)

    for k in (0, 1, 2, 3):
        if k == 0:
            own_part(cot_hbm, cr, r_c).wait()
        else:
            spread_in(cot_hbm, cr, s_c, r_c, k).wait_recv()
    acc_s[...] = jnp.zeros_like(acc_s)

    def res_copy(w):
        return remote(xr.at[w], res_hbm.at[me, 0], s_res.at[w], r_res.at[me], (img, w))

    def dense(w, _):
        wr, wcol = w // 2, lax.rem(w, 2)

        def flat(quads):
            return jnp.concatenate([quads[0][0], quads[0][1], quads[1][0], quads[1][1]], axis=0)

        x = flat(to_blocks(xr[w].astype(F32)))
        e = flat(to_blocks(cr[w].astype(F32)))
        back = jnp.concatenate(
            [blk[2 * wr + qr, 2 * wcol + qc] for qr in range(2) for qc in range(2)], axis=0
        ).astype(F32)
        ctr = back - jnp.mean(back, axis=1, keepdims=True)
        r1 = lax.rsqrt(jnp.mean(ctr * ctr, axis=1, keepdims=True) + EPS_NORM)
        z1 = ctr * r1
        middle = x + z1 * g1[...][None, :] + s1[...][None, :]
        ml = middle.astype(BF)
        rows = pl.ds(pl.multiple_of(w * TOK, TOK), TOK)
        mlow[rows, :] = ml
        out = jnp.zeros((TOK, 512), F32)
        for c in range(4):
            cols = slice(512 * c, 512 * c + 512)
            hid = nn(ml, we[:, cols]) + be[cols][None, :]
            cap, low = gelu_parts(hid)
            a = (hid * cap).astype(BF)
            act[c, rows, :] = a
            slope[c] = (cap + hid * low).astype(BF)
            out = out + nn(a, wc[cols, :])
        out = out + bc[...][None, :]
        ctr2 = out - jnp.mean(out, axis=1, keepdims=True)
        r2 = lax.rsqrt(jnp.mean(ctr2 * ctr2, axis=1, keepdims=True) + EPS_NORM)
        z2 = ctr2 * r2
        result = middle + z2 * g2[...][None, :] + s2[...][None, :]
        quads = [[result[128 * qr + 64 * qc : 128 * qr + 64 * qc + 64] for qc in range(2)] for qr in range(2)]
        xr[w] = from_blocks(quads).astype(BF)

        @pl.when(w != me)
        def _():
            res_copy(w).start()

        acc_s[0] += col_sum(e * z2)
        acc_s[1] += col_sum(e)
        dn = e * g2[...][None, :]
        dv = r2 * (
            dn - jnp.mean(dn, axis=1, keepdims=True) - z2 * jnp.mean(dn * z2, axis=1, keepdims=True)
        )
        do = dv.astype(BF)
        dout[rows, :] = do
        acc_s[2] += col_sum(do.astype(F32))
        dm = e
        for c in range(4):
            cols = slice(512 * c, 512 * c + 512)
            dh = (nt(do, wc[cols, :]) * slope[c].astype(F32)).astype(BF)
            dhid[c, rows, :] = dh
            acc_s[3 + c] += col_sum(dh.astype(F32))
            dm = dm + nt(dh, we[:, cols])
        acc_s[7] += col_sum(dm * z1)
        acc_s[8] += col_sum(dm)
        dn1 = dm * g1[...][None, :]
        db = r1 * (
            dn1 - jnp.mean(dn1, axis=1, keepdims=True) - z1 * jnp.mean(dn1 * z1, axis=1, keepdims=True)
        )
        db = db.astype(BF)
        for qr in range(2):
            for qc in range(2):
                at = 128 * qr + 64 * qc
                dmid[2 * wr + qr, 2 * wcol + qc] = dm[at : at + 64]
                blk[2 * wr + qr, 2 * wcol + qc] = db[at : at + 64]
        return 0

    lax.fori_loop(0, 4, dense, 0)
    own_res = pltpu.make_async_copy(xr.at[me], res_hbm.at[me, 0], r_res.at[me])
    own_res.start()

    def rows_of(c, s=0, b1=None, b2=None, z=None):
        at, size = 0, 1024
        if b1 is not None:
            at, size = at + s * 512 + b1 * 256, 256
        if b2 is not None:
            at, size = at + b2 * 128, 128
        if z is not None:
            at, size = at + z * 32, 32
        return c, pl.ds(pl.multiple_of(at, 32), size)

    first = (xpos, ypos)
    second = (ypos, xpos)
    first_peer = (x_peer, y_peer)
    second_peer = (y_peer, x_peer)

    def sum_plan(a, src, rcore):
        full = sums_hbm.at[a]

        def sems(i):
            return s_ar.at[a, i], r_ar.at[a, i]

        def core_send():
            return remote(src.at[rows_of(1 - core)], rcore, *sems(0), core_peer)

        def one_send(s):
            return remote(src.at[rows_of(core, s, 1 - first[s])], rone.at[a, s], *sems(1 + s), first_peer[s])

        def two_send(s):
            return remote(
                src.at[rows_of(core, s, first[s], 1 - second[s])], rtwo.at[a, s], *sems(3 + s), second_peer[s]
            )

        def z_send(s, k):
            return remote(
                src.at[rows_of(core, s, first[s], second[s], lax.rem(zpos + k, 4))],
                rz.at[a, s, k - 1], *sems(5 + 3 * s + k - 1), z_peer(k),
            )

        def far_send(s, k):
            return remote(
                own.at[a, s, 0], own.at[a, s, k], *sems(22 + (extra - 1) * s + k - 1), far_peer(k)
            )

        def out_z(s, k, z):
            at = rows_of(core, s, first[s], second[s], z)
            return remote(own.at[a, s, extra], full.at[at], *sems(11 + 3 * s + k - 1), z_peer(k))

        def out_own(s):
            at = rows_of(core, s, first[s], second[s], zpos)
            return pltpu.make_async_copy(own.at[a, s, extra], full.at[at], l_ar.at[a, s])

        def out_two(s, b2):
            at = rows_of(core, s, first[s], b2)
            return remote(full.at[at], full.at[at], *sems(17 + s), second_peer[s])

        def out_one(s, b1):
            at = rows_of(core, s, b1)
            return remote(full.at[at], full.at[at], *sems(19 + s), first_peer[s])

        def out_core(c):
            at = rows_of(c)
            return remote(full.at[at], full.at[at], *sems(21), core_peer)

        def step0():
            core_send().start()

        def step1():
            core_send().wait_recv()
            at = rows_of(core)
            src[at] = src[at] + rcore[...]
            for s in range(2):
                one_send(s).start()

        def step2():
            for s in range(2):
                one_send(s).wait_recv()
                at = rows_of(core, s, first[s])
                src[at] = src[at] + rone[a, s]
                two_send(s).start()

        def step3():
            for s in range(2):
                two_send(s).wait_recv()
                at = rows_of(core, s, first[s], second[s])
                src[at] = src[at] + rtwo[a, s]
                for k in (2, 1, 3):
                    z_send(s, k).start()

        def step4():
            for s in range(2):
                for k in (1, 2, 3):
                    z_send(s, k).wait_recv()
                at = rows_of(core, s, first[s], second[s], zpos)
                total = src[at].astype(F32)
                for k in range(3):
                    total = total + rz[a, s, k].astype(F32)
                own[a, s, 0] = total.astype(BF)
                for k in range(1, extra):
                    far_send(s, k).start()
            for s in range(2):
                total = own[a, s, 0].astype(F32)
                for k in range(1, extra):
                    far_send(s, k).wait_recv()
                    total = total + own[a, s, k].astype(F32)
                own[a, s, extra] = total.astype(BF)
                out_own(s).start()
                for k in (2, 1, 3):
                    out_z(s, k, zpos).start()

        def step5():
            for s in range(2):
                out_own(s).wait()
                for k in (1, 2, 3):
                    out_z(s, k, lax.rem(zpos + 4 - k, 4)).wait_recv()
                out_two(s, second[s]).start()

        def step6():
            for s in range(2):
                out_two(s, 1 - second[s]).wait_recv()
                out_one(s, first[s]).start()

        def step7():
            for s in range(2):
                out_one(s, 1 - first[s]).wait_recv()
            out_core(core).start()

        def step8():
            out_core(1 - core).wait_recv()
            core_send().wait_send()
            for s in range(2):
                one_send(s).wait_send()
                two_send(s).wait_send()
                out_two(s, second[s]).wait_send()
                out_one(s, first[s]).wait_send()
                for k in (1, 2, 3):
                    z_send(s, k).wait_send()
                    out_z(s, k, zpos).wait_send()
                for k in range(1, extra):
                    far_send(s, k).wait_send()
            out_core(core).wait_send()

        return [step0, step1, step2, step3, step4, step5, step6, step7, step8]

    plan_two = sum_plan(0, asum.at[0], rcore.at[0])
    plan_one = sum_plan(1, asum.at[1], rcore.at[1])
    plan_tail = sum_plan(2, act.at[0:2], act.at[2])

    for c in range(4):
        asum[0, c // 2, 512 * (c % 2) : 512 * (c % 2) + 512, :] = tn(act[c], dout[...]).astype(BF)
    plan_two[0]()
    for c in range(4):
        asum[1, c // 2, 512 * (c % 2) : 512 * (c % 2) + 512, :] = tn(mlow[...], dhid[c]).astype(BF)
    plan_one[0]()

    bias[...] = jnp.zeros_like(bias)
    acc_s[9] = jnp.zeros((8, 512), F32)

    def gather(o, _):
        for bcol in range(2):
            for br in range(2):
                at = (bcol * 2 + br) * 64
                brow, bc_ = home(o, bcol, br)
                cr[o, at : at + 64, :] = blk[brow, bc_]
        return 0

    lax.fori_loop(0, 4, gather, 0)
    head_ones_half = head_ones[0:128, 0:128]
    minus = jnp.full((256, 128), -1.0, BF)
    lane32 = lax.rem(lax.broadcasted_iota(jnp.int32, (256, 128), 1), 32)

    slots = {}
    for at, step in zip((0, 3, 5, 8, 11, 13, 15), plan_two[1:8]):
        slots.setdefault(at, []).append(step)
    for at, step in zip((1, 6, 9, 12, 15), plan_one[1:6]):
        slots.setdefault(at, []).append(step)

    def retreat(o, _):
        dmx = nt(cr[o], wproj[...])
        rows = pl.ds(pl.multiple_of(o * TOK, TOK), TOK)
        for g in range(4):
            lanes = slice(128 * g, 128 * g + 128)
            qg, kg, vg = qs[o, g], kl[o, g], vl[o, g]
            dmg = dmx[:, lanes] * isum[o, g]
            dmp = dmg.astype(BF)
            mix = mixed[o, :, lanes].astype(F32) + mixlo[o, :, lanes].astype(F32)
            prod = dmp.astype(F32) * mix
            delta = sum(nn(p, head_ones_half) for p in split3(prod)[:2])
            delta_hi, delta_lo, _ = split3(delta)
            prod = jnp.where(lane32 == 0, delta_hi, jnp.where(lane32 == 1, delta_lo, jnp.zeros_like(delta_lo)))
            vw = jnp.concatenate([vg, minus], axis=1)
            dmp_t = dmg.T.astype(BF)
            qg_t = qg.astype(F32).T.astype(BF)
            dq = jnp.zeros((256, 128), F32)
            dk_t, dv_t = [], []
            for hh in range(4):
                h = 4 * g + hh
                mask = head_mask[hh]
                left = jnp.concatenate([dmp * mask, prod * mask], axis=1)
                eh = ex[o, g, hh]
                dsf = nt(left, vw) * eh.astype(F32)
                ds = dsf.astype(BF)
                bias[h, 1] += dsf[0:128, 0:128] + dsf[128:256, 128:256]
                bias[h, 0] += dsf[0:128, 128:256]
                bias[h, 2] += dsf[128:256, 0:128]
                dq = dq + nn(ds, kg * mask)
                dk_t.append(nn(qg_t[32 * hh : 32 * hh + 32], ds))
                dv_t.append(nn(dmp_t[32 * hh : 32 * hh + 32], eh))
            dk = jnp.concatenate(dk_t, axis=0).T
            dv = jnp.concatenate(dv_t, axis=0).T
            qf, kf = qg.astype(F32), kg.astype(F32)
            scale = scale_lanes(g // 2)[:, 128 * (g % 2) : 128 * (g % 2) + 128]
            tq = dq * qf
            acc_s[9, :, lanes] += col_sum(tq)
            aq = nn(tq.astype(BF), head_ones_half)
            ak = nn((dk * kf).astype(BF), head_ones_half)
            dhid[0, rows, lanes] = (qinv[o, g].astype(F32) * (scale * dq - (1.0 / scale) * qf * aq)).astype(BF)
            dhid[1, rows, lanes] = (kinv[o, g].astype(F32) * (dk - kf * ak)).astype(BF)
            dhid[2, rows, lanes] = dv.astype(BF)
            for at, steps in slots.items():
                if at % 4 == g:

                    @pl.when(o == at // 4)
                    def _(steps=steps):
                        for step in steps:
                            step()

        moved = sum(nt(dhid[i, rows, :], wqkv[:, 512 * i : 512 * i + 512]) for i in range(3))
        for bcol in range(2):
            for br in range(2):
                at = (bcol * 2 + br) * 64
                brow, bc_ = home(o, bcol, br)
                dmid[brow, bc_] += moved[at : at + 64, :]
        return 0

    lax.fori_loop(0, 4, retreat, 0)

    xflat = xroll[...].reshape(1024, 512)
    for i in range(3):
        act[i // 2, 512 * (i % 2) : 512 * (i % 2) + 512, :] = tn(xflat, dhid[i]).astype(BF)
    act[1, 512:1024, :] = tn(mixed[...].reshape(1024, 512), cr[...].reshape(1024, 512)).astype(BF)
    plan_tail[0]()

    def gin_copy(w):
        return remote(slope.at[w], gin_hbm.at[me, 0], s_gin.at[w], r_gin.at[me], (img, w))

    def finish(w, _):
        wr, wcol = w // 2, lax.rem(w, 2)
        quads = [[dmid[2 * wr + qr, 2 * wcol + qc] for qc in range(2)] for qr in range(2)]
        slope[w] = from_blocks(quads).astype(BF)

        @pl.when(w != me)
        def _():
            gin_copy(w).start()

        return 0

    lax.fori_loop(0, 4, finish, 0)
    own_gin = pltpu.make_async_copy(slope.at[me], gin_hbm.at[me, 0], r_gin.at[me])
    own_gin.start()
    plan_one[6]()
    plan_tail[1]()

    row_ones = jnp.ones((8, 1024), BF)

    def put(row, v):
        small_s[0, row : row + v.shape[0], :] = v

    put(ROW_QB, nn(row_ones, dhid[0])[0:1])
    put(ROW_VB, nn(row_ones, dhid[2])[0:1])
    put(ROW_BP, nn(row_ones, cr[...].reshape(1024, 512))[0:1])
    for row, i in ((ROW_LS, 9), (ROW_G1, 7), (ROW_S1, 8), (ROW_B2, 2), (ROW_G2, 0), (ROW_S2, 1)):
        put(row, jnp.sum(acc_s[i], axis=0, keepdims=True))
    for c in range(4):
        put(ROW_BE + c, jnp.sum(acc_s[3 + c], axis=0, keepdims=True))
    short = jnp.zeros((384, 256), F32)
    for c in range(4):
        places = one_hot_places(c)
        left = jnp.concatenate(
            [bias[:, :, 8 * r : 8 * r + 8, :].reshape(384, 128) for r in range(4 * c, 4 * c + 4)], axis=1
        )
        for p in split3(left)[:2]:
            short = short + nt(p, places)
    pick = one_hot_pick()
    for i in range(4):
        piece = split3(short[96 * i : 96 * i + 96])[:2]
        part[4 * i : 4 * i + 4] = sum(nt(p, pick) for p in piece).reshape(4, 24, 1024)
    plan_tail[2]()
    dtab = jnp.zeros((16, 1024), F32)
    for u in range(24):
        dtab = dtab + pltpu.roll(part[:, u, :], 23 - u, 1)
    tab[...] = dtab * tab[...] * (1.0 - tab[...] * (1.0 / BIAS_RANGE))
    small_s[0, ROW_W1 : ROW_W2 + 16, :] = jnp.zeros((ROW_W2 + 16 - ROW_W1, 512), F32)

    def net_back(c, _):
        cols, pre = net_piece(c)
        cap, low = gelu_parts(pre)
        dlog, dlog_lo, _ = split3(tab[:, cols])
        units, units_lo, _ = split3(pre * cap)
        small_s[0, ROW_W2 : ROW_W2 + 16, :] += nn(dlog, units) + nn(dlog_lo, units) + nn(dlog, units_lo)
        w_hi, w_lo, _ = split3(w2t[...])
        back = tn(dlog, w_hi) + tn(dlog_lo, w_hi) + tn(dlog, w_lo)
        dpre, dpre_lo, _ = split3(back * (cap + pre * low))
        hi, mid, _ = split3(crow[:, cols])
        net = nn(hi, dpre) + nn(mid, dpre) + nn(hi, dpre_lo)
        small_s[0, ROW_W1 : ROW_W1 + 3, :] += net[0:3]
        return 0

    lax.fori_loop(0, 4, net_back, 0)
    plan_one[7]()
    plan_two[8]()
    plan_tail[3]()

    stages = [[core_peer], [y_peer], [x_peer], [z_peer(k) for k in range(1, 4)]]
    if extra > 1:
        stages.append([far_peer(k) for k in range(1, extra)])
    later = [plan_tail[4], plan_tail[5], plan_one[8], plan_tail[6], plan_tail[7]]
    slot = 0
    for i, peers in enumerate(stages):
        copies = [
            remote(small_s.at[i], small_r.at[slot + j], s_sm.at[slot + j], r_sm.at[slot + j], peer)
            for j, peer in enumerate(peers)
        ]
        slot += len(peers)
        for c in copies:
            c.start()
        if i < len(later):
            later[i]()
        total = small_s[i]
        for j, c in enumerate(copies):
            c.wait()
            total = total + small_r[slot - len(peers) + j]
        small_s[i + 1] = total
    for step in later[len(stages) :]:
        step()
    plan_tail[8]()
    small_out[...] = small_s[len(stages)]

    own_res.wait()
    own_gin.wait()
    for k in (1, 2, 3):
        frm, to = ring_from(k), lax.rem(me + k, n_win)
        spread(x_hbm, xr, s_x, r_x, k).wait_send()
        spread(cot_hbm, cr, s_c, r_c, k).wait_send()
        res_copy(to).wait_send()
        gin_copy(to).wait_send()
        remote(xr.at[frm], res_hbm.at[frm, 0], s_res.at[frm], r_res.at[frm], (img, frm)).wait_recv()
        remote(slope.at[frm], gin_hbm.at[frm, 0], s_gin.at[frm], r_gin.at[frm], (img, frm)).wait_recv()


def body(n_img, n_win, inputs, wqkv, qb, vb, hls, w1, b1, w2, wproj, bproj, g1, s1, we, be, wc, bc, g2, s2, cot):
    extra = n_img // 8
    crow, ccol = table_coords()
    dma = pltpu.SemaphoreType.DMA
    n_ar = 22 + 2 * (extra - 1)
    n_sm = 6 + (extra - 1)
    vmem = pl.BlockSpec(memory_space=pltpu.VMEM)
    hbm = pl.BlockSpec(memory_space=pl.ANY)
    smem = pl.BlockSpec(memory_space=pltpu.SMEM)
    scratch = [
        pltpu.VMEM((4, TOK, 512), BF),
        pltpu.VMEM((4, TOK, 512), BF),
        pltpu.VMEM((4, TOK, 512), BF),
        pltpu.VMEM((16, 3, 128, 128), F32),
        pltpu.VMEM((4, 4, 4, TOK, TOK), BF),
        pltpu.VMEM((4, 4, TOK, 128), BF),
        pltpu.VMEM((4, 4, TOK, 128), BF),
        pltpu.VMEM((4, 4, TOK, 128), BF),
        pltpu.VMEM((4, 4, TOK, 128), BF),
        pltpu.VMEM((4, 4, TOK, 128), BF),
        pltpu.VMEM((4, 4, TOK, 128), F32),
        pltpu.VMEM((4, TOK, 512), BF),
        pltpu.VMEM((4, TOK, 512), BF),
        pltpu.VMEM((4, 4, 64, 512), BF),
        pltpu.VMEM((4, 4, 64, 512), F32),
        pltpu.VMEM((4, 1024, 512), BF),
        pltpu.VMEM((4, 1024, 512), BF),
        pltpu.VMEM((1024, 512), BF),
        pltpu.VMEM((1024, 512), BF),
        pltpu.VMEM((4, TOK, 512), BF),
        pltpu.VMEM((16, 1024), F32),
        pltpu.VMEM((16, 24, 1024), F32),
        pltpu.VMEM((10, 8, 512), F32),
        pltpu.VMEM((2, 2, 1024, 512), BF),
        pltpu.VMEM((2, 1024, 512), BF),
        pltpu.VMEM((3, 2, 256, 512), BF),
        pltpu.VMEM((3, 2, 128, 512), BF),
        pltpu.VMEM((3, 2, 3, 32, 512), BF),
        pltpu.VMEM((3, 2, extra + 1, 32, 512), BF),
        pltpu.VMEM((6, SMALL_ROWS, 512), F32),
        pltpu.VMEM((n_sm, SMALL_ROWS, 512), F32),
        dma((4,)), dma((4,)), dma((4,)), dma((4,)),
        dma((4,)), dma((4,)), dma((4,)), dma((4,)),
        dma((3, n_ar)), dma((3, n_ar)), dma((3, 2)),
        dma((n_sm,)), dma((n_sm,)),
    ]
    block = jax.ShapeDtypeStruct(inputs.shape, BF)
    result, grad_inputs, sums, small = pl.pallas_call(
        functools.partial(block_kernel, n_img, n_win),
        out_shape=(
            block,
            block,
            jax.ShapeDtypeStruct((3, 2, 1024, 512), BF),
            jax.ShapeDtypeStruct((SMALL_ROWS, 512), F32),
        ),
        in_specs=[hbm, hbm] + [vmem] * 6 + [smem] + [vmem] * 12,
        out_specs=(hbm, hbm, hbm, vmem),
        scratch_shapes=scratch,
        compiler_params=pltpu.CompilerParams(
            collective_id=0, has_side_effects=True, vmem_limit_bytes=64 * 1024 * 1024
        ),
    )(
        inputs, cot, wqkv, wproj, we, wc, qb, vb, hls, w1, b1, w2.T, bproj, g1, s1, be, bc, g2, s2,
        jnp.asarray(crow), jnp.asarray(ccol),
    )
    sums = sums.astype(F32)
    fc2 = sums[0].reshape(2048, 512)
    fc1 = jnp.transpose(sums[1].reshape(4, 512, 512), (1, 0, 2)).reshape(512, 2048)
    qkv = jnp.transpose(sums[2].reshape(4, 512, 512)[:3], (1, 0, 2)).reshape(512, 1536)
    proj = sums[2, 1, 512:]
    return (
        result,
        grad_inputs,
        qkv,
        small[ROW_QB],
        small[ROW_VB],
        jnp.sum(small[ROW_LS].reshape(16, 32), axis=1),
        small[ROW_W1 : ROW_W1 + 2],
        small[ROW_B1],
        small[ROW_W2 : ROW_W2 + 16].T,
        proj,
        small[ROW_BP],
        small[ROW_G1],
        small[ROW_S1],
        fc1,
        small[ROW_BE : ROW_BE + 4].reshape(2048),
        fc2,
        small[ROW_B2],
        small[ROW_G2],
        small[ROW_S2],
    )


def solution(mesh):
    n_img, n_win = mesh.shape["img"], mesh.shape["win"]
    block = P("img", "win", None, None)
    return jax.shard_map(
        functools.partial(body, n_img, n_win),
        mesh=mesh,
        in_specs=(block,) + (P(),) * 17 + (block,),
        out_specs=(block, block) + (P(),) * 17,
        check_vma=False,
    )
```

```python
import functools

import jax
import jax.numpy as jnp
import numpy as np
from jax import lax
from jax.experimental import pallas as pl
from jax.experimental.pallas import tpu as pltpu
from jax.sharding import PartitionSpec as P

WIN = 16
TOK = WIN * WIN
EPS_DIR = 1e-06
EPS_NORM = 1e-05
MASK_FILL = -100.0
BIAS_RANGE = 16.0
INV_ROOT_TWO = 0.7071067811865476
INV_ROOT_TWOPI = 0.3989422804014327
LOG2_E = 1.4426950408889634
MESH = pl.DeviceIdType.MESH
BF = jnp.bfloat16
F32 = jnp.float32

(ROW_QB, ROW_VB, ROW_LS, ROW_W1, ROW_B1, ROW_W2, ROW_BP, ROW_G1, ROW_S1, ROW_B2, ROW_G2, ROW_S2,
 ROW_BE, SMALL_ROWS) = (0, 1, 2, 3, 5, 6, 22, 23, 24, 25, 26, 27, 28, 32)

SCHEDULE = {
    "a1": ((0, 0),),
    "a3": ((1, 0), (0, 1)),
    "d0": ((1, 1),),
    "d1": ((0, 2),),
    "d2": ((1, 2),),
    "d3": ((0, 3),),
    "b0": ((1, 3),),
    "b1": ((2, 0),),
    "b3": ((3, 0), (2, 1)),
    "gproj": ((4, 0), (3, 1), (0, 4), (4, 1)),
    "r0": ((1, 4), (2, 2), (3, 2), (0, 5)),
    "r1": ((4, 2), (2, 3), (1, 5), (3, 3)),
    "r2": ((0, 6), (4, 3), (1, 6), (2, 4)),
    "r3": ((3, 4), (0, 7)),
    "gq0": ((5, 0), (4, 4), (0, 8), (1, 7), (5, 1)),
    "r4": ((1, 8), (2, 5)),
    "r5": ((3, 5), (4, 5), (5, 2), (2, 6)),
    "r6": ((3, 6), (4, 6), (5, 3)),
    "r7": ((2, 7),),
    "gq1": ((6, 0), (5, 4), (3, 7), (2, 8), (6, 1), (4, 7), (3, 8), (4, 8)),
    "bb": ((5, 5),),
    "net": ((7, 0), (5, 6), (6, 2), (7, 1)),
    "end": ((6, 3), (6, 4), (7, 2), (6, 5), (7, 3), (6, 6), (7, 4)),
}


def nn(a, b):
    return lax.dot_general(a, b, (((1,), (0,)), ((), ())), preferred_element_type=F32)


def nt(a, b):
    return lax.dot_general(a, b, (((1,), (1,)), ((), ())), preferred_element_type=F32)


def tn(a, b):
    return lax.dot_general(a, b, (((0,), (0,)), ((), ())), preferred_element_type=F32)


def split3(v):
    hi = v.astype(BF)
    rest = v - hi.astype(F32)
    mid = rest.astype(BF)
    return hi, mid, (rest - mid.astype(F32)).astype(BF)


def gelu_parts(v):
    cap = 0.5 + 0.5 * lax.erf(v * INV_ROOT_TWO)
    return cap, INV_ROOT_TWOPI * jnp.exp2(v * v * (-0.5 * LOG2_E))


def col_sum(v):
    return jnp.sum(v.reshape(v.shape[0] // 8, 8, v.shape[1]), axis=0)


def to_blocks(v):
    n = v.shape[-1]
    t = v.reshape(2, 8, 2, 8, n)
    return [[t[qr, :, qc].reshape(64, n) for qc in range(2)] for qr in range(2)]


def from_blocks(quads):
    n = quads[0][0].shape[-1]
    rows = []
    for qr in range(2):
        a = quads[qr][0].reshape(8, 1, 8, n)
        b = quads[qr][1].reshape(8, 1, 8, n)
        rows.append(jnp.concatenate([a, b], axis=1).reshape(128, n))
    return jnp.concatenate(rows, axis=0)


def one_hot_places(c):
    l = lax.broadcasted_iota(jnp.int32, (256, 512), 0)
    k = lax.broadcasted_iota(jnp.int32, (256, 512), 1) + 512 * c
    return jnp.where(l == 8 * (15 - k // 128) + k % 128, 1.0, 0.0).astype(BF)


def one_hot_pick():
    k = lax.broadcasted_iota(jnp.int32, (1024, 256), 0)
    l = lax.broadcasted_iota(jnp.int32, (1024, 256), 1)
    return jnp.where(k == 32 * (l // 8) + l % 8, 1.0, 0.0).astype(BF)


def table_coords():
    k = np.arange(1024)
    out = np.zeros((2, 1024), np.float64)
    for i, off in enumerate((15 - k // 32, 15 - k % 32)):
        u = off * (8.0 / 15.0)
        out[i] = np.sign(u) * np.log2(np.abs(u) + 1.0) / 3.0
    rows = np.zeros((8, 1024), np.float32)
    rows[0:2] = out
    rows[2] = 1.0
    cols = np.zeros((1024, 8), np.float32)
    cols[:, 0:2] = out.T
    return rows, cols


def net_first(cols, w1, b1):
    return cols[:, 0:1] * w1[0:1, :] + cols[:, 1:2] * w1[1:2, :] + b1


def block_kernel(
    n_img, n_win,
    x_hbm, cot_hbm, wqkv_hbm, wproj_hbm, we_hbm, wc_hbm, qb, vb, hls, w1, b1, w2t, bproj, g1, s1, be, bc, g2, s2,
    crow, ccol,
    res_hbm, gin_hbm, wide_hbm, qkv_hbm, small_out,
    xr, cr, xroll, bias, ex, qs, kl, vl, qinv, kinv, isum, mixed, mixlo, blk, dmid, act, dhid, dout,
    mlow, slope, tab, part, acc_s, asum, rec, far, wqkv, wproj, we, wc,
    small_s, small_c, small_p, small_z, small_far, small_o,
    s_x, r_x, s_c, r_c, s_res, r_res, s_gin, r_gin, s_ar, r_ar, l_ar, s_sm, r_sm, s_w,
):
    img = lax.axis_index("img")
    me = lax.axis_index("win")
    extra = n_img // 8
    core = lax.rem(me, 2)
    ypos = me // 2
    xpos = lax.rem(img, 2)
    zpos = lax.rem(img // 2, 4)
    upper = img // 8

    def ring_to(k):
        return (img, lax.rem(me + k, n_win))

    def ring_from(k):
        return lax.rem(me + n_win - k, n_win)

    core_peer = (img, me + 1 - 2 * core)
    y_peer = (img, lax.rem(me + 2, 4))
    x_peer = (img + 1 - 2 * xpos, me)
    plane_pos = 2 * xpos + ypos

    def z_peer(k):
        return (upper * 8 + lax.rem(zpos + k, 4) * 2 + xpos, me)

    def plane_peer(k):
        to = lax.rem(plane_pos + k, 4)
        return (img + to // 2 - xpos, lax.rem(to, 2) * 2 + core)

    def far_peer(k):
        return (lax.rem(upper + k, extra) * 8 + zpos * 2 + xpos, me)

    weights = [
        pltpu.make_async_copy(a, b, s_w.at[i])
        for i, (a, b) in enumerate(((wqkv_hbm, wqkv), (wproj_hbm, wproj), (we_hbm, we), (wc_hbm, wc)))
    ]

    barrier = pltpu.get_barrier_semaphore()
    others = [ring_to(k) for k in range(1, n_win)] + [x_peer, (img + 1 - 2 * xpos, lax.rem(me + 2, 4))]
    others += [z_peer(k) for k in range(1, 4)] + [far_peer(k) for k in range(1, extra)]
    for peer in others:
        pl.semaphore_signal(barrier, inc=1, device_id=peer, device_id_type=MESH)
    pl.semaphore_wait(barrier, len(others))

    def remote(src, dst, ssem, rsem, peer):
        return pltpu.make_async_remote_copy(
            src_ref=src, dst_ref=dst, send_sem=ssem, recv_sem=rsem, device_id=peer, device_id_type=MESH
        )

    def spread(src_hbm, dst, ssem, rsem, k):
        to = lax.rem(me + k, n_win)
        return remote(src_hbm.at[to, 0], dst.at[me], ssem.at[k], rsem.at[k], ring_to(k))

    def spread_in(src_hbm, dst, ssem, rsem, k):
        frm = ring_from(k)
        return remote(src_hbm.at[frm, 0], dst.at[frm], ssem.at[k], rsem.at[k], ring_to(k))

    def own_part(src_hbm, dst, sem):
        return pltpu.make_async_copy(src_hbm.at[me, 0], dst.at[me], sem.at[0])

    def half_rows(w, half):
        return pl.ds(pl.multiple_of(128 * (1 - w // 2 if half == 0 else w // 2), 128), 128)

    def x_send(k, half):
        to, rows = lax.rem(me + k, n_win), half_rows(me, half)
        return remote(
            x_hbm.at[to, 0, rows], xr.at[me, rows], s_x.at[half, k], r_x.at[half, k], ring_to(k)
        )

    def x_arrival(k, half):
        frm = ring_from(k)
        rows = half_rows(frm, half)
        return remote(x_hbm.at[frm, 0, rows], xr.at[frm, rows], s_x.at[half, k], r_x.at[half, k], ring_to(k))

    for half in range(2):
        for k in (2, 1, 3):
            x_send(k, half).start()
    own_x = own_part(x_hbm, xr, r_x.at[0])
    own_x.start()
    for c in weights:
        c.start()

    def net_piece(c):
        rows = pl.ds(pl.multiple_of(256 * c, 256), 256)
        return rows, net_first(ccol[rows, :], w1[...], b1[...][None, :])

    def look_up(c, _):
        cols, pre = net_piece(c)
        logits = lax.dot_general(
            w2t[...], pre * gelu_parts(pre)[0], (((1,), (1,)), ((), ())),
            precision=lax.Precision.HIGHEST, preferred_element_type=F32,
        )
        tab[:, cols] = BIAS_RANGE / (1.0 + jnp.exp(-logits))
        return 0

    lax.fori_loop(0, 4, look_up, 0)
    for u in range(24):
        part[:, u, :] = pltpu.roll(tab[...], 1001 + u, 1)
    pick = one_hot_pick()
    short = jnp.concatenate(
        [sum(nn(p, pick) for p in split3(part[4 * i : 4 * i + 4].reshape(96, 1024))) for i in range(4)], axis=0
    )
    short_parts = split3(short)
    for c in range(4):
        places = one_hot_places(c)
        wide = sum(nn(p, places) for p in short_parts)
        for r in range(4):
            row = 8 * (4 * c + r)
            bias[:, :, row : row + 8, :] = wide[:, 128 * r : 128 * r + 128].reshape(16, 3, 8, 128)

    lane = lax.broadcasted_iota(jnp.int32, (1, 128), 1)
    head_mask = [jnp.where(lane // 32 == hh, 1.0, 0.0).astype(BF) for hh in range(4)]
    l0 = lax.broadcasted_iota(jnp.int32, (256, 256), 0)
    l1 = lax.broadcasted_iota(jnp.int32, (256, 256), 1)
    head_ones = jnp.where(l0 // 32 == l1 // 32, 1.0, 0.0).astype(BF)

    def scale_lanes(p):
        wide = lax.broadcasted_iota(jnp.int32, (1, 256), 1) // 32
        out = jnp.zeros((1, 256), F32)
        for i in range(8):
            out = jnp.where(wide == i, hls[8 * p + i], out)
        return jnp.exp(out)

    def lay(half):
        def one(w, _):
            late = w // 2 if half == 0 else 1 - w // 2
            rows = pl.ds(pl.multiple_of(128 * (1 - late), 128), 128)
            v = xr[w, rows, :].astype(F32).reshape(8, 2, 8, 512)
            for qc in range(2):
                bcol = 1 - qc
                ocol = lax.rem(w, 2) if bcol == 0 else 1 - lax.rem(w, 2)
                at = pl.ds(pl.multiple_of((bcol * 2 + late) * 64, 64), 64)
                xroll[2 * half + ocol, at, :] = v[:, qc].reshape(64, 512).astype(BF)
            return 0

        lax.fori_loop(0, 4, one, 0)

    own_x.wait()
    for k in (1, 2, 3):
        x_arrival(k, 0).wait_recv()
    lay(0)
    weights[0].wait()
    weights[1].wait()

    row_half = lax.broadcasted_iota(jnp.int32, (128, 128), 0) // 64
    col_half = lax.broadcasted_iota(jnp.int32, (128, 128), 1) // 64
    apart = jnp.where(row_half == col_half, 0.0, MASK_FILL)

    def home(o, bcol, br):
        return lax.rem(2 * (o // 2) + br + 1, 4), lax.rem(2 * lax.rem(o, 2) + bcol + 1, 4)

    def attend(o, _):
        @pl.when(o == 2)
        def _():
            for k in (1, 2, 3):
                x_arrival(k, 1).wait_recv()
            for k in (2, 1, 3):
                spread(cot_hbm, cr, s_c, r_c, k).start()
            own_part(cot_hbm, cr, r_c).start()
            lay(1)

        xw = xroll[o]
        for p in range(2):
            cols = slice(256 * p, 256 * p + 256)
            q = nn(xw, wqkv[:, cols]) + qb[cols][None, :]
            qi = lax.rsqrt(nn((q * q).astype(BF), head_ones) + EPS_DIR)
            qsc = (q * qi * scale_lanes(p)).astype(BF)
            k = nn(xw, wqkv[:, 512 + 256 * p : 768 + 256 * p])
            ki = lax.rsqrt(nn((k * k).astype(BF), head_ones) + EPS_DIR)
            kn = (k * ki).astype(BF)
            v = (nn(xw, wqkv[:, 1024 + 256 * p : 1280 + 256 * p]) + vb[cols][None, :]).astype(BF)
            for i in range(2):
                half = slice(128 * i, 128 * i + 128)
                qs[o, 2 * p + i] = qsc[:, half]
                kl[o, 2 * p + i] = kn[:, half]
                vl[o, 2 * p + i] = v[:, half]
                qinv[o, 2 * p + i] = qi[:, half].astype(BF)
                kinv[o, 2 * p + i] = ki[:, half].astype(BF)
        rows_cut = jnp.where(o // 2 == 1, apart, 0.0)
        cols_cut = jnp.where(lax.rem(o, 2) == 1, jnp.full((128, 128), MASK_FILL, F32), rows_cut)

        for g in range(4):
            qg, kg, vg = qs[o, g], kl[o, g], vl[o, g]
            sc = nt(jnp.concatenate([qg * mask for mask in head_mask], axis=0), kg)
            for hh in range(4):
                h, n = 4 * g + hh, 256 * hh
                ex[o, g, hh, 0:128, 0:128] = jnp.exp(sc[n : n + 128, 0:128] + bias[h, 1] + rows_cut).astype(BF)
                ex[o, g, hh, 0:128, 128:256] = jnp.exp(sc[n : n + 128, 128:256] + bias[h, 0] + cols_cut).astype(BF)
                ex[o, g, hh, 128:256, 0:128] = jnp.exp(sc[n + 128 : n + 256, 0:128] + bias[h, 2] + cols_cut).astype(BF)
                ex[o, g, hh, 128:256, 128:256] = jnp.exp(
                    sc[n + 128 : n + 256, 128:256] + bias[h, 1] + rows_cut
                ).astype(BF)
            ones = [jnp.broadcast_to(mask, (256, 128)) for mask in head_mask]
            total = nn(
                jnp.concatenate([ex[o, g, hh] for hh in range(4)], axis=1),
                jnp.concatenate(
                    [jnp.concatenate([vg * mask, one], axis=1) for mask, one in zip(head_mask, ones)], axis=0
                ),
            )
            inv = 1.0 / total[:, 128:256]
            isum[o, g] = inv
            mix = total[:, 0:128] * inv
            mix_hi = mix.astype(BF)
            mixed[o, :, 128 * g : 128 * g + 128] = mix_hi
            mixlo[o, :, 128 * g : 128 * g + 128] = (mix - mix_hi.astype(F32)).astype(BF)

        branch = (nn(mixed[o], wproj[...]) + bproj[...][None, :]).astype(BF)
        for bcol in range(2):
            for br in range(2):
                at = (bcol * 2 + br) * 64
                brow, bc_ = home(o, bcol, br)
                blk[brow, bc_] = branch[at : at + 64, :]
        return 0

    lax.fori_loop(0, 4, attend, 0)

    for k in (0, 1, 2, 3):
        if k == 0:
            own_part(cot_hbm, cr, r_c).wait()
        else:
            spread_in(cot_hbm, cr, s_c, r_c, k).wait_recv()
    weights[2].wait()
    weights[3].wait()
    acc_s[...] = jnp.zeros_like(acc_s)

    def res_copy(w):
        return remote(xr.at[w], res_hbm.at[me, 0], s_res.at[w], r_res.at[me], (img, w))

    def flat(quads):
        return jnp.concatenate([quads[0][0], quads[0][1], quads[1][0], quads[1][1]], axis=0)

    def first_norm(w):
        wr, wcol = w // 2, lax.rem(w, 2)
        back = jnp.concatenate(
            [blk[2 * wr + qr, 2 * wcol + qc] for qr in range(2) for qc in range(2)], axis=0
        ).astype(F32)
        ctr = back - jnp.mean(back, axis=1, keepdims=True)
        r1 = lax.rsqrt(jnp.mean(ctr * ctr, axis=1, keepdims=True) + EPS_NORM)
        return ctr * r1, r1

    def dense(w, _):
        e = flat(to_blocks(cr[w].astype(F32)))
        z1, _ = first_norm(w)
        middle = flat(to_blocks(xr[w].astype(F32))) + z1 * g1[...][None, :] + s1[...][None, :]
        ml = middle.astype(BF)
        rows = pl.ds(pl.multiple_of(w * TOK, TOK), TOK)
        mlow[rows, :] = ml
        out = jnp.zeros((TOK, 512), F32)
        for c in range(4):
            cols = slice(512 * c, 512 * c + 512)
            hid = nn(ml, we[:, cols]) + be[cols][None, :]
            cap, low = gelu_parts(hid)
            a = (hid * cap).astype(BF)
            act[c, rows, :] = a
            dhid[c, rows, :] = (cap + hid * low).astype(BF)
            out = out + nn(a, wc[cols, :])
        out = out + bc[...][None, :]
        ctr2 = out - jnp.mean(out, axis=1, keepdims=True)
        r2 = lax.rsqrt(jnp.mean(ctr2 * ctr2, axis=1, keepdims=True) + EPS_NORM)
        z2 = ctr2 * r2
        result = middle + z2 * g2[...][None, :] + s2[...][None, :]
        quads = [[result[128 * qr + 64 * qc : 128 * qr + 64 * qc + 64] for qc in range(2)] for qr in range(2)]
        xr[w] = from_blocks(quads).astype(BF)

        @pl.when(w != me)
        def _():
            res_copy(w).start()

        acc_s[0] += col_sum(e * z2)
        acc_s[1] += col_sum(e)
        dn = e * g2[...][None, :]
        dv = r2 * (
            dn - jnp.mean(dn, axis=1, keepdims=True) - z2 * jnp.mean(dn * z2, axis=1, keepdims=True)
        )
        do = dv.astype(BF)
        dout[rows, :] = do
        acc_s[2] += col_sum(do.astype(F32))
        return 0

    lax.fori_loop(0, 4, dense, 0)
    own_res = pltpu.make_async_copy(xr.at[me], res_hbm.at[me, 0], r_res.at[me])
    own_res.start()

    digits = {"x": (xpos, 2), "y": (ypos, 2), "z": (zpos, 4), "p": (plane_pos, 4)}

    def digit_peer(d, k):
        if d == "z":
            return z_peer(k)
        if d == "p":
            return plane_peer(k)
        return x_peer if d == "x" else y_peer

    def sum_unit(a, src, land, out, order):
        n = src.shape[1]
        levels, at, size, room, sem = [], core * 256, 256, 256, 1
        for d in order:
            pos, count = digits[d]
            part_size = size // count
            levels.append((d, pos, count, at, part_size, room, sem))
            at, room, sem = at + pos * part_size, room + (count - 1) * part_size, sem + count - 1
            size = part_size
        own_at, last = at, len(order) - 1

        def rows(start, length):
            return pl.ds(pl.multiple_of(start, 16), length)

        def copy(src_at, dst, length, i, peer):
            return remote(src.at[rows(src_at, length)], dst, s_ar.at[a, i], r_ar.at[a, i], peer)

        def core_send():
            return copy((1 - core) * 256, land.at[pl.ds(0, 256)], 256, 0, core_peer)

        def down(j, k):
            d, pos, count, at, length, room, sem = levels[j]
            dst = land.at[pl.ds(room + (k - 1) * length, length)]
            return copy(at + lax.rem(pos + k, count) * length, dst, length, sem + k - 1, digit_peer(d, k))

        def up(j, k, pos):
            d, _, count, at, length, _, sem = levels[j]
            here = out.at[rows(at + pos * length, length)]
            from_ = src.at[rows(own_at, length)] if j == last else here
            return remote(from_, here, s_ar.at[a, 6 + sem + k], r_ar.at[a, 6 + sem + k], digit_peer(d, k))

        def core_up(c):
            here = out.at[rows(c * 256, 256)]
            return remote(here, here, s_ar.at[a, 14], r_ar.at[a, 14], core_peer)

        def far_send(k):
            return copy(own_at, far.at[a, k - 1, :, 0:n], 16, 15 + k - 1, far_peer(k))

        def peers(j):
            return range(1, levels[j][2])

        def from_pos(j, k):
            return lax.rem(levels[j][1] + levels[j][2] - k, levels[j][2])

        def local():
            here = rows(own_at, 16)
            return pltpu.make_async_copy(src.at[here], out.at[here], l_ar.at[a])

        def step_core():
            core_send().start()

        def step_down(j):
            if j == 0:
                core_send().wait_recv()
                at = rows(core * 256, 256)
                src[at, :] = src[at, :] + land[0:256, :]
            else:
                take(j - 1)
            for k in peers(j):
                down(j, k).start()

        def take(j):
            d, pos, count, at, length, room, sem = levels[j]
            here = rows(at + pos * length, length)
            for k in peers(j):
                down(j, k).wait_recv()
            total = src[here, :].astype(F32)
            for k in peers(j):
                r = room + (k - 1) * length
                total = total + land[r : r + length, :].astype(F32)
            src[here, :] = total.astype(BF)

        def step_turn():
            take(last)
            if extra > 1:
                here = rows(own_at, 16)
                for k in range(1, extra):
                    far_send(k).start()
                total = src[here, :].astype(F32)
                for k in range(1, extra):
                    far_send(k).wait()
                    total = total + far[a, k - 1, :, 0:n].astype(F32)
                src[here, :] = total.astype(BF)
            for k in peers(last):
                up(last, k, levels[last][1]).start()
            local().start()

        def step_up(j):
            if j == last:
                local().wait()
            for k in peers(j):
                up(j, k, from_pos(j, k)).wait_recv()
            if j == 0:
                core_up(core).start()
            else:
                for k in peers(j - 1):
                    up(j - 1, k, levels[j - 1][1]).start()

        def step_last():
            core_up(1 - core).wait_recv()

        def step_sent():
            core_send().wait_send()
            core_up(core).wait_send()
            for j in range(last + 1):
                for k in peers(j):
                    down(j, k).wait_send()
                    up(j, k, levels[j][1]).wait_send()

        steps = [step_core] + [functools.partial(step_down, j) for j in range(last + 1)] + [step_turn]
        return steps + [functools.partial(step_up, j) for j in range(last, -1, -1)] + [step_last, step_sent]

    def together(units):
        return [lambda steps=steps: [step() for step in steps] for steps in zip(*units)]

    orders = ("xyz", "yxz")
    wide_units = [sum_unit(a, asum.at[a], rec.at[a], wide_hbm.at[a], orders[a % 2]) for a in range(9)]
    groups = [together(wide_units[2 * i : 2 * i + 2]) for i in range(4)] + [wide_units[8]]
    for p in range(2):
        part_units = []
        for i in range(3):
            place = (pl.ds(512 * (i // 2), 512), pl.ds(256 * (i % 2), 256))
            part_units.append(
                sum_unit(
                    9 + 3 * p + i, act.at[p].at[place], act.at[2 + p].at[place], qkv_hbm.at[p, i],
                    "pz",
                )
            )
        groups.append(together(part_units))

    def small_steps():
        mine, other = pl.ds(pl.multiple_of(16 * core, 16), 16), pl.ds(pl.multiple_of(16 - 16 * core, 16), 16)

        def copy(src, dst, i, peer):
            return remote(src, dst, s_sm.at[i], r_sm.at[i], peer)

        def core_send():
            return copy(small_s.at[0, other], small_c, 0, core_peer)

        def plane_send(k):
            return copy(small_s.at[1, mine], small_p.at[k - 1], k, plane_peer(k))

        def z_send(k):
            return copy(small_s.at[2, mine], small_z.at[k - 1], 3 + k, z_peer(k))

        def far_copy(k):
            return copy(small_s.at[3, mine], small_far.at[k - 1], 7 + k, far_peer(k))

        def core_up(rows):
            return copy(small_o.at[rows], small_o.at[rows], 7, core_peer)

        def step0():
            core_send().start()

        def step1():
            core_send().wait_recv()
            small_s[1, mine, :] = small_s[0, mine, :] + small_c[...]
            for k in range(1, 4):
                plane_send(k).start()

        def step2():
            total = small_s[1, mine, :]
            for k in range(1, 4):
                plane_send(k).wait_recv()
                total = total + small_p[k - 1]
            small_s[2, mine, :] = total
            for k in range(1, 4):
                z_send(k).start()

        def step3():
            total = small_s[2, mine, :]
            for k in range(1, 4):
                z_send(k).wait_recv()
                total = total + small_z[k - 1]
            if extra > 1:
                small_s[3, mine, :] = total
                for k in range(1, extra):
                    far_copy(k).start()
                for k in range(1, extra):
                    far_copy(k).wait()
                    total = total + small_far[k - 1]
            small_o[mine, :] = total
            core_up(mine).start()

        def step4():
            core_up(other).wait_recv()
            small_out[...] = small_o[...]

        def step5():
            core_send().wait_send()
            core_up(mine).wait_send()
            for k in range(1, 4):
                plane_send(k).wait_send()
                z_send(k).wait_send()

        return [step0, step1, step2, step3, step4, step5]

    groups.append(small_steps())

    def run(name):
        for at, j in SCHEDULE.get(name, ()):
            groups[at][j]()

    def run_in(prefix, i):
        for at in range(8):
            if SCHEDULE.get(f"{prefix}{at}"):

                @pl.when(i == at)
                def _(at=at):
                    run(f"{prefix}{at}")

    for c in range(4):
        asum[c] = tn(act[c], dout[...]).astype(BF)
        run(f"a{c}")

    def dense_back(w, _):
        wr, wcol = w // 2, lax.rem(w, 2)
        rows = pl.ds(pl.multiple_of(w * TOK, TOK), TOK)
        do = dout[rows, :]
        dm = flat(to_blocks(cr[w].astype(F32)))
        for c in range(4):
            cols = slice(512 * c, 512 * c + 512)
            dh = (nt(do, wc[cols, :]) * dhid[c, rows, :].astype(F32)).astype(BF)
            dhid[c, rows, :] = dh
            acc_s[3 + c] += col_sum(dh.astype(F32))
            dm = dm + nt(dh, we[:, cols])
        z1, r1 = first_norm(w)
        acc_s[7] += col_sum(dm * z1)
        acc_s[8] += col_sum(dm)
        dn1 = dm * g1[...][None, :]
        db = r1 * (
            dn1 - jnp.mean(dn1, axis=1, keepdims=True) - z1 * jnp.mean(dn1 * z1, axis=1, keepdims=True)
        )
        db = db.astype(BF)
        for qr in range(2):
            for qc in range(2):
                at = 128 * qr + 64 * qc
                dmid[2 * wr + qr, 2 * wcol + qc] = dm[at : at + 64]
                blk[2 * wr + qr, 2 * wcol + qc] = db[at : at + 64]
        run_in("d", w)
        return 0

    lax.fori_loop(0, 4, dense_back, 0)
    for c in range(4):
        asum[4 + c] = tn(mlow[...], dhid[c]).astype(BF)
        run(f"b{c}")

    bias[...] = jnp.zeros_like(bias)

    def gather(o, _):
        for bcol in range(2):
            for br in range(2):
                at = (bcol * 2 + br) * 64
                brow, bc_ = home(o, bcol, br)
                cr[o, at : at + 64, :] = blk[brow, bc_]
        return 0

    lax.fori_loop(0, 4, gather, 0)
    asum[8] = tn(mixed[...].reshape(1024, 512), cr[...].reshape(1024, 512)).astype(BF)
    run("gproj")
    head_ones_half = head_ones[0:128, 0:128]
    minus = jnp.full((256, 128), -1.0, BF)
    lane32 = lax.rem(lax.broadcasted_iota(jnp.int32, (256, 128), 1), 32)

    def retreat(it, _):
        p, o = it // 4, lax.rem(it, 4)
        half = pl.ds(pl.multiple_of(256 * p, 256), 256)
        dmx = nt(cr[o], wproj[half, :])
        rows = pl.ds(pl.multiple_of(o * TOK, TOK), TOK)
        scales = scale_lanes(p)
        for gi in range(2):
            g = 2 * p + gi
            lanes = pl.ds(pl.multiple_of(128 * g, 128), 128)
            qg, kg, vg = qs[o, g], kl[o, g], vl[o, g]
            dmg = dmx[:, 128 * gi : 128 * gi + 128] * isum[o, g]
            dmp = dmg.astype(BF)
            mix = mixed[o, :, lanes].astype(F32) + mixlo[o, :, lanes].astype(F32)
            prod = dmp.astype(F32) * mix
            delta = sum(nn(p, head_ones_half) for p in split3(prod)[:2])
            delta_hi, delta_lo, _ = split3(delta)
            prod = jnp.where(lane32 == 0, delta_hi, jnp.where(lane32 == 1, delta_lo, jnp.zeros_like(delta_lo)))
            vw = jnp.concatenate([vg, minus], axis=1)
            dmp4 = jnp.concatenate([dmp * mask for mask in head_mask], axis=0)
            left = jnp.concatenate([dmp4, jnp.concatenate([prod * mask for mask in head_mask], axis=0)], axis=1)
            e4 = ex[o, g].reshape(1024, 256)
            dsf = nt(left, vw) * e4.astype(F32)
            ds = dsf.astype(BF)
            for hh in range(4):
                h, n = 4 * g + hh, 256 * hh
                bias[h, 1] += dsf[n : n + 128, 0:128] + dsf[n + 128 : n + 256, 128:256]
                bias[h, 0] += dsf[n : n + 128, 128:256]
                bias[h, 2] += dsf[n + 128 : n + 256, 0:128]
            dq = nn(
                jnp.concatenate([ds[256 * hh : 256 * hh + 256] for hh in range(4)], axis=1),
                jnp.concatenate([kg * mask for mask in head_mask], axis=0),
            )
            dk = tn(ds, jnp.concatenate([qg * mask for mask in head_mask], axis=0))
            dv = tn(e4, dmp4)
            qf, kf = qg.astype(F32), kg.astype(F32)
            scale = scales[:, 128 * gi : 128 * gi + 128]
            tq = dq * qf
            acc_s[9, :, lanes] += col_sum(tq)
            aq = nn(tq.astype(BF), head_ones_half)
            ak = nn((dk * kf).astype(BF), head_ones_half)
            dhid[0, rows, lanes] = (qinv[o, g].astype(F32) * (scale * dq - (1.0 / scale) * qf * aq)).astype(BF)
            dhid[1, rows, lanes] = (kinv[o, g].astype(F32) * (dk - kf * ak)).astype(BF)
            dhid[2, rows, lanes] = dv.astype(BF)
        moved = sum(
            nt(dhid[i, rows, half], wqkv[:, pl.ds(pl.multiple_of(512 * i + 256 * p, 256), 256)])
            for i in range(3)
        )
        for bcol in range(2):
            for br in range(2):
                at = (bcol * 2 + br) * 64
                brow, bc_ = home(o, bcol, br)
                dmid[brow, bc_] += moved[at : at + 64, :]
        run_in("r", it)

        @pl.when(lax.rem(it, 4) == 3)
        def _():
            xflat = xroll[...].reshape(1024, 512)
            for i in range(3):
                grad = tn(xflat, dhid[i, :, half]).astype(BF)
                act[p, 512 * (i // 2) : 512 * (i // 2) + 512, 256 * (i % 2) : 256 * (i % 2) + 256] = grad

        run_in("gq", jnp.where(lax.rem(it, 4) == 3, p, -1))
        return 0

    lax.fori_loop(0, 8, retreat, 0)

    def gin_copy(w):
        return remote(slope.at[w], gin_hbm.at[me, 0], s_gin.at[w], r_gin.at[me], (img, w))

    def finish(w, _):
        wr, wcol = w // 2, lax.rem(w, 2)
        quads = [[dmid[2 * wr + qr, 2 * wcol + qc] for qc in range(2)] for qr in range(2)]
        slope[w] = from_blocks(quads).astype(BF)

        @pl.when(w != me)
        def _():
            gin_copy(w).start()

        return 0

    lax.fori_loop(0, 4, finish, 0)
    own_gin = pltpu.make_async_copy(slope.at[me], gin_hbm.at[me, 0], r_gin.at[me])
    own_gin.start()
    run("finish")

    row_ones = jnp.ones((8, 1024), BF)

    def put(row, v):
        small_s[0, row : row + v.shape[0], :] = v

    put(ROW_QB, nn(row_ones, dhid[0])[0:1])
    put(ROW_VB, nn(row_ones, dhid[2])[0:1])
    put(ROW_BP, nn(row_ones, cr[...].reshape(1024, 512))[0:1])
    for row, i in ((ROW_LS, 9), (ROW_G1, 7), (ROW_S1, 8), (ROW_B2, 2), (ROW_G2, 0), (ROW_S2, 1)):
        put(row, jnp.sum(acc_s[i], axis=0, keepdims=True))
    for c in range(4):
        put(ROW_BE + c, jnp.sum(acc_s[3 + c], axis=0, keepdims=True))
    run("puts")
    short = jnp.zeros((384, 256), F32)
    for c in range(4):
        places = one_hot_places(c)
        left = jnp.concatenate(
            [bias[:, :, 8 * r : 8 * r + 8, :].reshape(384, 128) for r in range(4 * c, 4 * c + 4)], axis=1
        )
        for p in split3(left)[:2]:
            short = short + nt(p, places)
    pick = one_hot_pick()
    for i in range(4):
        piece = split3(short[96 * i : 96 * i + 96])[:2]
        part[4 * i : 4 * i + 4] = sum(nt(p, pick) for p in piece).reshape(4, 24, 1024)
    run("bb")
    dtab = jnp.zeros((16, 1024), F32)
    for u in range(24):
        dtab = dtab + pltpu.roll(part[:, u, :], 23 - u, 1)
    tab[...] = dtab * tab[...] * (1.0 - tab[...] * (1.0 / BIAS_RANGE))
    small_s[0, ROW_W1 : ROW_W2 + 16, :] = jnp.zeros((ROW_W2 + 16 - ROW_W1, 512), F32)

    def net_back(c, _):
        cols, pre = net_piece(c)
        cap, low = gelu_parts(pre)
        dlog, dlog_lo, _ = split3(tab[:, cols])
        units, units_lo, _ = split3(pre * cap)
        small_s[0, ROW_W2 : ROW_W2 + 16, :] += nn(dlog, units) + nn(dlog_lo, units) + nn(dlog, units_lo)
        w_hi, w_lo, _ = split3(w2t[...])
        back = tn(dlog, w_hi) + tn(dlog_lo, w_hi) + tn(dlog, w_lo)
        dpre, dpre_lo, _ = split3(back * (cap + pre * low))
        hi, mid, _ = split3(crow[:, cols])
        net = nn(hi, dpre) + nn(mid, dpre) + nn(hi, dpre_lo)
        small_s[0, ROW_W1 : ROW_W1 + 3, :] += net[0:3]
        return 0

    lax.fori_loop(0, 4, net_back, 0)
    run("net")
    run("end")

    for group in groups:
        group[-1]()
    own_res.wait()
    own_gin.wait()
    for k in (1, 2, 3):
        frm, to = ring_from(k), lax.rem(me + k, n_win)
        x_send(k, 0).wait_send()
        x_send(k, 1).wait_send()
        spread(cot_hbm, cr, s_c, r_c, k).wait_send()
        res_copy(to).wait_send()
        gin_copy(to).wait_send()
        remote(xr.at[frm], res_hbm.at[frm, 0], s_res.at[frm], r_res.at[frm], (img, frm)).wait_recv()
        remote(slope.at[frm], gin_hbm.at[frm, 0], s_gin.at[frm], r_gin.at[frm], (img, frm)).wait_recv()


def widen_kernel(
    res, gin, wide, qkv, small,
    res_out, gin_out, w_qkv, g_qb, g_vb, g_ls, g_w1, g_b1, g_w2, w_proj, g_bp, g_g1, g_s1, w_fc1, g_be,
    w_fc2, g_b2, g_g2, g_s2,
    blocks, wide_in, qkv_in, wide_f, qkv_f, s_in, s_out, s_blocks,
):
    taken = [pltpu.make_async_copy(a, blocks.at[i], s_blocks.at[i]) for i, a in enumerate((res, gin))]
    passed = [pltpu.make_async_copy(blocks.at[i], a, s_blocks.at[2 + i]) for i, a in enumerate((res_out, gin_out))]
    pieces = []
    for i in range(9):
        if i < 4:
            place = w_fc2.at[pl.ds(512 * i, 512), :]
        elif i < 8:
            place = w_fc1.at[:, pl.ds(512 * (i - 4), 512)]
        else:
            place = w_proj
        pieces.append((wide.at[i], wide_in.at[i], wide_f.at[i], place))
    for i in range(6):
        place = w_qkv.at[:, pl.ds(512 * (i % 3) + 256 * (i // 3), 256)]
        pieces.append((qkv.at[i // 3, i % 3], qkv_in.at[i], qkv_f.at[i], place))
    loads = [pltpu.make_async_copy(a, b, s_in.at[i]) for i, (a, b, _, _) in enumerate(pieces)]
    stores = [pltpu.make_async_copy(c, d, s_out.at[i]) for i, (_, _, c, d) in enumerate(pieces)]
    for c in loads:
        c.start()
    for c in taken:
        c.start()
    for i, (_, b, c, _) in enumerate(pieces):
        loads[i].wait()
        c[...] = b[...].astype(F32)
        stores[i].start()
    for a, b in zip(taken, passed):
        a.wait()
        b.start()
    for row, out in (
        (ROW_QB, g_qb), (ROW_VB, g_vb), (ROW_B1, g_b1), (ROW_BP, g_bp), (ROW_G1, g_g1), (ROW_S1, g_s1),
        (ROW_B2, g_b2), (ROW_G2, g_g2), (ROW_S2, g_s2),
    ):
        out[...] = small[row, :]
    for c in range(4):
        g_be[512 * c : 512 * c + 512] = small[ROW_BE + c, :]
    g_w1[...] = small[ROW_W1 : ROW_W1 + 2, :]
    g_w2[...] = small[ROW_W2 : ROW_W2 + 16, :].T
    h0 = lax.broadcasted_iota(jnp.int32, (512, 16), 0) // 32
    h1 = lax.broadcasted_iota(jnp.int32, (512, 16), 1)
    heads = jnp.where(h0 == h1, 1.0, 0.0).astype(BF)
    per_head = sum(nn(jnp.broadcast_to(p, (8, 512)), heads) for p in split3(small[ROW_LS : ROW_LS + 1, :]))
    g_ls[...] = per_head[0, :]
    for c in passed + stores:
        c.wait()


def body(n_img, n_win, inputs, wqkv, qb, vb, hls, w1, b1, w2, wproj, bproj, g1, s1, we, be, wc, bc, g2, s2, cot):
    extra = n_img // 8
    crow, ccol = table_coords()
    dma = pltpu.SemaphoreType.DMA
    n_ar = 15 + (extra - 1)
    n_sm = 8 + (extra - 1)
    vmem = pl.BlockSpec(memory_space=pltpu.VMEM)
    hbm = pl.BlockSpec(memory_space=pl.ANY)
    smem = pl.BlockSpec(memory_space=pltpu.SMEM)
    scratch = [
        pltpu.VMEM((4, TOK, 512), BF),
        pltpu.VMEM((4, TOK, 512), BF),
        pltpu.VMEM((4, TOK, 512), BF),
        pltpu.VMEM((16, 3, 128, 128), F32),
        pltpu.VMEM((4, 4, 4, TOK, TOK), BF),
        pltpu.VMEM((4, 4, TOK, 128), BF),
        pltpu.VMEM((4, 4, TOK, 128), BF),
        pltpu.VMEM((4, 4, TOK, 128), BF),
        pltpu.VMEM((4, 4, TOK, 128), BF),
        pltpu.VMEM((4, 4, TOK, 128), BF),
        pltpu.VMEM((4, 4, TOK, 128), F32),
        pltpu.VMEM((4, TOK, 512), BF),
        pltpu.VMEM((4, TOK, 512), BF),
        pltpu.VMEM((4, 4, 64, 512), BF),
        pltpu.VMEM((4, 4, 64, 512), F32),
        pltpu.VMEM((4, 1024, 512), BF),
        pltpu.VMEM((4, 1024, 512), BF),
        pltpu.VMEM((1024, 512), BF),
        pltpu.VMEM((1024, 512), BF),
        pltpu.VMEM((4, TOK, 512), BF),
        pltpu.VMEM((16, 1024), F32),
        pltpu.VMEM((16, 24, 1024), F32),
        pltpu.VMEM((10, 8, 512), F32),
        pltpu.VMEM((9, 512, 512), BF),
        pltpu.VMEM((9, 496, 512), BF),
        pltpu.VMEM((15, extra - 1, 16, 512) if extra > 1 else (1, 1, 16, 512), BF),
        pltpu.VMEM((512, 1536), BF),
        pltpu.VMEM((512, 512), BF),
        pltpu.VMEM((512, 2048), BF),
        pltpu.VMEM((2048, 512), BF),
        pltpu.VMEM((4, SMALL_ROWS, 512), F32),
        pltpu.VMEM((16, 512), F32),
        pltpu.VMEM((3, 16, 512), F32),
        pltpu.VMEM((3, 16, 512), F32),
        pltpu.VMEM((max(extra - 1, 1), 16, 512), F32),
        pltpu.VMEM((SMALL_ROWS, 512), F32),
        dma((2, 4)), dma((2, 4)), dma((4,)), dma((4,)),
        dma((4,)), dma((4,)), dma((4,)), dma((4,)),
        dma((15, n_ar)), dma((15, n_ar)), dma((15,)),
        dma((n_sm,)), dma((n_sm,)),
        dma((4,)),
    ]
    block = jax.ShapeDtypeStruct(inputs.shape, BF)
    result, grad_inputs, wide, qkv, small = pl.pallas_call(
        functools.partial(block_kernel, n_img, n_win),
        out_shape=(
            block,
            block,
            jax.ShapeDtypeStruct((9, 512, 512), BF),
            jax.ShapeDtypeStruct((2, 3, 512, 256), BF),
            jax.ShapeDtypeStruct((SMALL_ROWS, 512), F32),
        ),
        in_specs=[hbm] * 6 + [vmem] * 2 + [smem] + [vmem] * 12,
        out_specs=(hbm, hbm, hbm, hbm, vmem),
        scratch_shapes=scratch,
        compiler_params=pltpu.CompilerParams(
            collective_id=0, has_side_effects=True, vmem_limit_bytes=64 * 1024 * 1024
        ),
    )(
        inputs, cot, wqkv, wproj, we, wc, qb, vb, hls, w1, b1, w2.T, bproj, g1, s1, be, bc, g2, s2,
        jnp.asarray(crow), jnp.asarray(ccol),
    )
    any_ = lambda shape: jax.ShapeDtypeStruct(shape, F32)
    outs = pl.pallas_call(
        widen_kernel,
        out_shape=(
            block, block, any_((512, 1536)), any_((512,)), any_((512,)), any_((16,)), any_((2, 512)),
            any_((512,)), any_((512, 16)), any_((512, 512)), any_((512,)), any_((512,)), any_((512,)),
            any_((512, 2048)), any_((2048,)), any_((2048, 512)), any_((512,)), any_((512,)), any_((512,)),
        ),
        in_specs=[hbm] * 4 + [vmem],
        out_specs=tuple(hbm if i in (0, 1, 2, 9, 13, 15) else vmem for i in range(19)),
        scratch_shapes=[
            pltpu.VMEM((2,) + inputs.shape, BF),
            pltpu.VMEM((9, 512, 512), BF),
            pltpu.VMEM((6, 512, 256), BF),
            pltpu.VMEM((9, 512, 512), F32),
            pltpu.VMEM((6, 512, 256), F32),
            dma((15,)), dma((15,)), dma((4,)),
        ],
        compiler_params=pltpu.CompilerParams(vmem_limit_bytes=63 * 1024 * 1024),
    )(result, grad_inputs, wide, qkv, small)
    return outs


def solution(mesh):
    n_img, n_win = mesh.shape["img"], mesh.shape["win"]
    block = P("img", "win", None, None)
    return jax.shard_map(
        functools.partial(body, n_img, n_win),
        mesh=mesh,
        in_specs=(block,) + (P(),) * 17 + (block,),
        out_specs=(block, block) + (P(),) * 17,
        check_vma=False,
    )
```

```python
import functools

import jax
import jax.numpy as jnp
import numpy as np
from jax import lax
from jax.experimental import pallas as pl
from jax.experimental.pallas import tpu as pltpu
from jax.sharding import PartitionSpec as P

WIN = 16
TOK = WIN * WIN
EPS_DIR = 1e-06
EPS_NORM = 1e-05
MASK_FILL = -100.0
BIAS_RANGE = 16.0
INV_ROOT_TWO = 0.7071067811865476
INV_ROOT_TWOPI = 0.3989422804014327
LOG2_E = 1.4426950408889634
MESH = pl.DeviceIdType.MESH
BF = jnp.bfloat16
F32 = jnp.float32

(ROW_QB, ROW_VB, ROW_LS, ROW_W1, ROW_B1, ROW_W2, ROW_BP, ROW_G1, ROW_S1, ROW_B2, ROW_G2, ROW_S2,
 ROW_BE, SMALL_ROWS) = (0, 1, 2, 3, 5, 6, 22, 23, 24, 25, 26, 27, 28, 32)

SCHEDULE = {
    "a1": ((0, 0),),
    "a3": ((1, 0),),
    "d0": ((0, 1), (1, 1)),
    "d1": ((2, 0),),
    "d2": ((2, 1),),
    "d3": ((3, 0),),
    "nb": ((1, 2), (0, 2)),
    "gproj": ((4, 0), (3, 1)),
    "r0": ((4, 1), (0, 3), (1, 3)),
    "r1": ((2, 2), (3, 2)),
    "r2": ((4, 2), (0, 4)),
    "r3": ((2, 3), (1, 4)),
    "gq0": ((5, 0), (4, 3), (3, 3)),
    "r4": ((5, 1), (0, 5), (2, 4)),
    "r6": ((1, 5), (4, 4)),
    "r7": ((3, 4), (5, 2), (2, 5), (0, 6)),
    "gq1": ((6, 0), (4, 5), (1, 6)),
    "puts": ((6, 1), (2, 6), (3, 5)),
    "bb": ((5, 3), (4, 6)),
    "net": ((7, 0),),
    "end": (
        (7, 1), (1, 7), (0, 7), (1, 8), (0, 8), (6, 2), (3, 6), (5, 4), (2, 7), (4, 7), (6, 3), (2, 8), (7, 2),
        (4, 8), (3, 7), (6, 4), (3, 8), (5, 5), (7, 3), (5, 6), (7, 4), (6, 5), (6, 6),
    ),
}
ORDERS = (
    "zxy", "yxz", "xyz", "xyz", "zxy", "xyz", "yzx", "xyz", "yxz",
    "pz", "pz", "pz", "pz", "pz", "pz",
)


def nn(a, b):
    return lax.dot_general(a, b, (((1,), (0,)), ((), ())), preferred_element_type=F32)


def nt(a, b):
    return lax.dot_general(a, b, (((1,), (1,)), ((), ())), preferred_element_type=F32)


def tn(a, b):
    return lax.dot_general(a, b, (((0,), (0,)), ((), ())), preferred_element_type=F32)


def split3(v):
    hi = v.astype(BF)
    rest = v - hi.astype(F32)
    mid = rest.astype(BF)
    return hi, mid, (rest - mid.astype(F32)).astype(BF)


def gelu_parts(v):
    cap = 0.5 + 0.5 * lax.erf(v * INV_ROOT_TWO)
    return cap, INV_ROOT_TWOPI * jnp.exp2(v * v * (-0.5 * LOG2_E))


def col_sum(v):
    return jnp.sum(v.reshape(v.shape[0] // 8, 8, v.shape[1]), axis=0)


def to_blocks(v):
    n = v.shape[-1]
    t = v.reshape(2, 8, 2, 8, n)
    return [[t[qr, :, qc].reshape(64, n) for qc in range(2)] for qr in range(2)]


def from_blocks(quads):
    n = quads[0][0].shape[-1]
    rows = []
    for qr in range(2):
        a = quads[qr][0].reshape(8, 1, 8, n)
        b = quads[qr][1].reshape(8, 1, 8, n)
        rows.append(jnp.concatenate([a, b], axis=1).reshape(128, n))
    return jnp.concatenate(rows, axis=0)


def one_hot_places(c):
    l = lax.broadcasted_iota(jnp.int32, (256, 512), 0)
    k = lax.broadcasted_iota(jnp.int32, (256, 512), 1) + 512 * c
    return jnp.where(l == 8 * (15 - k // 128) + k % 128, 1.0, 0.0).astype(BF)


def one_hot_pick():
    k = lax.broadcasted_iota(jnp.int32, (1024, 256), 0)
    l = lax.broadcasted_iota(jnp.int32, (1024, 256), 1)
    return jnp.where(k == 32 * (l // 8) + l % 8, 1.0, 0.0).astype(BF)


def table_coords():
    k = np.arange(1024)
    out = np.zeros((2, 1024), np.float64)
    for i, off in enumerate((15 - k // 32, 15 - k % 32)):
        u = off * (8.0 / 15.0)
        out[i] = np.sign(u) * np.log2(np.abs(u) + 1.0) / 3.0
    rows = np.zeros((8, 1024), np.float32)
    rows[0:2] = out
    rows[2] = 1.0
    cols = np.zeros((1024, 8), np.float32)
    cols[:, 0:2] = out.T
    return rows, cols


def net_first(cols, w1, b1):
    return cols[:, 0:1] * w1[0:1, :] + cols[:, 1:2] * w1[1:2, :] + b1


def block_kernel(
    n_img, n_win,
    x_hbm, cot_hbm, wqkv_hbm, wproj_hbm, we_hbm, wc_hbm, qb, vb, hls, w1, b1, w2t, bproj, g1, s1, be, bc, g2, s2,
    crow, ccol,
    res_hbm, gin_hbm, wide_hbm, qkv_hbm, small_out,
    xr, cr, xroll, bias, ex, qs, kl, vl, qinv, kinv, isum, mixed, mixlo, blk, dmid, act, dhid, dout,
    mlow, slope, tab, part, acc_s, asum, rec, far, wqkv, wproj, we, wc,
    small_s, small_c, small_p, small_z, small_far, small_o,
    s_x, r_x, s_c, r_c, s_res, r_res, s_gin, r_gin, s_ar, r_ar, l_ar, s_sm, r_sm, s_w,
):
    img = lax.axis_index("img")
    me = lax.axis_index("win")
    extra = n_img // 8
    core = lax.rem(me, 2)
    ypos = me // 2
    xpos = lax.rem(img, 2)
    zpos = lax.rem(img // 2, 4)
    upper = img // 8

    def ring_to(k):
        return (img, lax.rem(me + k, n_win))

    def ring_from(k):
        return lax.rem(me + n_win - k, n_win)

    core_peer = (img, me + 1 - 2 * core)
    y_peer = (img, lax.rem(me + 2, 4))
    x_peer = (img + 1 - 2 * xpos, me)
    plane_pos = 2 * xpos + ypos

    def z_peer(k):
        return (upper * 8 + lax.rem(zpos + k, 4) * 2 + xpos, me)

    def plane_peer(k):
        to = lax.rem(plane_pos + k, 4)
        return (img + to // 2 - xpos, lax.rem(to, 2) * 2 + core)

    def far_peer(k):
        return (lax.rem(upper + k, extra) * 8 + zpos * 2 + xpos, me)

    weights = [
        pltpu.make_async_copy(a, b, s_w.at[i])
        for i, (a, b) in enumerate(((wqkv_hbm, wqkv), (wproj_hbm, wproj), (we_hbm, we), (wc_hbm, wc)))
    ]

    own_x = pltpu.make_async_copy(x_hbm.at[me, 0], xr.at[me], r_x.at[0, 0])
    own_c = pltpu.make_async_copy(cot_hbm.at[me, 0], cr.at[me], r_c.at[0])
    for c in [own_x] + weights + [own_c]:
        c.start()

    barrier = pltpu.get_barrier_semaphore()
    others = [ring_to(k) for k in range(1, n_win)] + [x_peer, (img + 1 - 2 * xpos, lax.rem(me + 2, 4))]
    others += [z_peer(k) for k in range(1, 4)] + [far_peer(k) for k in range(1, extra)]
    for peer in others:
        pl.semaphore_signal(barrier, inc=1, device_id=peer, device_id_type=MESH)
    pl.semaphore_wait(barrier, len(others))

    def remote(src, dst, ssem, rsem, peer):
        return pltpu.make_async_remote_copy(
            src_ref=src, dst_ref=dst, send_sem=ssem, recv_sem=rsem, device_id=peer, device_id_type=MESH
        )

    def spread(src_hbm, dst, ssem, rsem, k):
        to = lax.rem(me + k, n_win)
        return remote(src_hbm.at[to, 0], dst.at[me], ssem.at[k], rsem.at[k], ring_to(k))

    def spread_in(src_hbm, dst, ssem, rsem, k):
        frm = ring_from(k)
        return remote(src_hbm.at[frm, 0], dst.at[frm], ssem.at[k], rsem.at[k], ring_to(k))

    def half_rows(w, half):
        return pl.ds(pl.multiple_of(128 * (1 - w // 2 if half == 0 else w // 2), 128), 128)

    def x_send(k, half):
        to, rows = lax.rem(me + k, n_win), half_rows(me, half)
        return remote(
            x_hbm.at[to, 0, rows], xr.at[me, rows], s_x.at[half, k], r_x.at[half, k], ring_to(k)
        )

    def x_arrival(k, half):
        frm = ring_from(k)
        rows = half_rows(frm, half)
        return remote(x_hbm.at[frm, 0, rows], xr.at[frm, rows], s_x.at[half, k], r_x.at[half, k], ring_to(k))

    for half in range(2):
        for k in (2, 1, 3):
            x_send(k, half).start()
    for k in (2, 1, 3):
        spread(cot_hbm, cr, s_c, r_c, k).start()

    def net_piece(c):
        rows = pl.ds(pl.multiple_of(256 * c, 256), 256)
        return rows, net_first(ccol[rows, :], w1[...], b1[...][None, :])

    def look_up(c, _):
        cols, pre = net_piece(c)
        logits = lax.dot_general(
            w2t[...], pre * gelu_parts(pre)[0], (((1,), (1,)), ((), ())),
            precision=lax.Precision.HIGHEST, preferred_element_type=F32,
        )
        tab[:, cols] = BIAS_RANGE / (1.0 + jnp.exp(-logits))
        return 0

    lax.fori_loop(0, 4, look_up, 0)
    for u in range(24):
        part[:, u, :] = pltpu.roll(tab[...], 1001 + u, 1)
    pick = one_hot_pick()
    short = jnp.concatenate(
        [sum(nn(p, pick) for p in split3(part[4 * i : 4 * i + 4].reshape(96, 1024))) for i in range(4)], axis=0
    )
    short_parts = split3(short)
    for c in range(4):
        places = one_hot_places(c)
        wide = sum(nn(p, places) for p in short_parts)
        for r in range(4):
            row = 8 * (4 * c + r)
            bias[:, :, row : row + 8, :] = wide[:, 128 * r : 128 * r + 128].reshape(16, 3, 8, 128)

    lane = lax.broadcasted_iota(jnp.int32, (1, 128), 1)
    head_mask = [jnp.where(lane // 32 == hh, 1.0, 0.0).astype(BF) for hh in range(4)]
    l0 = lax.broadcasted_iota(jnp.int32, (256, 256), 0)
    l1 = lax.broadcasted_iota(jnp.int32, (256, 256), 1)
    head_ones = jnp.where(l0 // 32 == l1 // 32, 1.0, 0.0).astype(BF)

    def scale_lanes(p):
        wide = lax.broadcasted_iota(jnp.int32, (1, 256), 1) // 32
        out = jnp.zeros((1, 256), F32)
        for i in range(8):
            out = jnp.where(wide == i, hls[8 * p + i], out)
        return jnp.exp(out)

    def lay(half):
        def one(w, _):
            late = w // 2 if half == 0 else 1 - w // 2
            rows = pl.ds(pl.multiple_of(128 * (1 - late), 128), 128)
            v = xr[w, rows, :].astype(F32).reshape(8, 2, 8, 512)
            for qc in range(2):
                bcol = 1 - qc
                ocol = lax.rem(w, 2) if bcol == 0 else 1 - lax.rem(w, 2)
                at = pl.ds(pl.multiple_of((bcol * 2 + late) * 64, 64), 64)
                xroll[2 * half + ocol, at, :] = v[:, qc].reshape(64, 512).astype(BF)
            return 0

        lax.fori_loop(0, 4, one, 0)

    def project(half):
        xw = xroll[2 * half : 2 * half + 2].reshape(512, 512)

        def one(p, _):
            def cols(i):
                return pl.ds(pl.multiple_of(512 * i + 256 * p, 256), 256)

            q = nn(xw, wqkv[:, cols(0)]) + qb[cols(0)][None, :]
            qi = lax.rsqrt(nn((q * q).astype(BF), head_ones) + EPS_DIR)
            qsc = (q * qi * scale_lanes(p)).astype(BF)
            k = nn(xw, wqkv[:, cols(1)])
            ki = lax.rsqrt(nn((k * k).astype(BF), head_ones) + EPS_DIR)
            kn = (k * ki).astype(BF)
            v = (nn(xw, wqkv[:, cols(2)]) + vb[cols(0)][None, :]).astype(BF)
            for w in range(2):
                rows = slice(256 * w, 256 * w + 256)
                for i in range(2):
                    lanes = slice(128 * i, 128 * i + 128)
                    at = (2 * half + w, 2 * p + i)
                    qs[at] = qsc[rows, lanes]
                    kl[at] = kn[rows, lanes]
                    vl[at] = v[rows, lanes]
                    qinv[at] = qi[rows, lanes].astype(BF)
                    kinv[at] = ki[rows, lanes].astype(BF)
            return 0

        lax.fori_loop(0, 2, one, 0)

    own_x.wait()
    for k in (1, 2, 3):
        x_arrival(k, 0).wait_recv()
    lay(0)
    weights[0].wait()
    project(0)
    weights[1].wait()

    row_half = lax.broadcasted_iota(jnp.int32, (128, 128), 0) // 64
    col_half = lax.broadcasted_iota(jnp.int32, (128, 128), 1) // 64
    apart = jnp.where(row_half == col_half, 0.0, MASK_FILL)

    def home(o, bcol, br):
        row, col = lax.rem(2 * (o // 2) + br + 1, 4), lax.rem(2 * lax.rem(o, 2) + bcol + 1, 4)
        return 2 * (row // 2) + col // 2, 2 * lax.rem(row, 2) + lax.rem(col, 2)

    def attend(o, _):
        @pl.when(o == 2)
        def _():
            for k in (1, 2, 3):
                x_arrival(k, 1).wait_recv()
            lay(1)
            project(1)

        rows_cut = jnp.where(o // 2 == 1, apart, 0.0)
        cols_cut = jnp.where(lax.rem(o, 2) == 1, jnp.full((128, 128), MASK_FILL, F32), rows_cut)

        for g in range(4):
            qg, kg, vg = qs[o, g], kl[o, g], vl[o, g]
            sc = nt(jnp.concatenate([qg * mask for mask in head_mask], axis=0), kg)
            for hh in range(4):
                h, n = 4 * g + hh, 256 * hh
                ex[o, g, hh, 0:128, 0:128] = jnp.exp(sc[n : n + 128, 0:128] + bias[h, 1] + rows_cut).astype(BF)
                ex[o, g, hh, 0:128, 128:256] = jnp.exp(sc[n : n + 128, 128:256] + bias[h, 0] + cols_cut).astype(BF)
                ex[o, g, hh, 128:256, 0:128] = jnp.exp(sc[n + 128 : n + 256, 0:128] + bias[h, 2] + cols_cut).astype(BF)
                ex[o, g, hh, 128:256, 128:256] = jnp.exp(
                    sc[n + 128 : n + 256, 128:256] + bias[h, 1] + rows_cut
                ).astype(BF)
            ones = [jnp.broadcast_to(mask, (256, 128)) for mask in head_mask]
            total = nn(
                jnp.concatenate([ex[o, g, hh] for hh in range(4)], axis=1),
                jnp.concatenate(
                    [jnp.concatenate([vg * mask, one], axis=1) for mask, one in zip(head_mask, ones)], axis=0
                ),
            )
            inv = 1.0 / total[:, 128:256]
            isum[o, g] = inv
            mix = total[:, 0:128] * inv
            mix_hi = mix.astype(BF)
            mixed[o, :, 128 * g : 128 * g + 128] = mix_hi
            mixlo[o, :, 128 * g : 128 * g + 128] = (mix - mix_hi.astype(F32)).astype(BF)

        branch = (nn(mixed[o], wproj[...]) + bproj[...][None, :]).astype(BF)
        for bcol in range(2):
            for br in range(2):
                at = (bcol * 2 + br) * 64
                blk[home(o, bcol, br)] = branch[at : at + 64, :]
        return 0

    lax.fori_loop(0, 4, attend, 0)

    weights[2].wait()
    weights[3].wait()
    acc_s[...] = jnp.zeros_like(acc_s)

    def res_copy(w):
        return remote(xr.at[w], res_hbm.at[me, 0], s_res.at[w], r_res.at[me], (img, w))

    def flat(quads):
        return jnp.concatenate([quads[0][0], quads[0][1], quads[1][0], quads[1][1]], axis=0)

    def first_norm(pair):
        back = blk[pl.ds(2 * pair, 2)].reshape(512, 512).astype(F32)
        ctr = back - jnp.mean(back, axis=1, keepdims=True)
        r1 = lax.rsqrt(jnp.mean(ctr * ctr, axis=1, keepdims=True) + EPS_NORM)
        return ctr * r1, r1

    def laid(ref, pair):
        return jnp.concatenate([flat(to_blocks(ref[2 * pair + i].astype(F32))) for i in range(2)], axis=0)

    def dense(turn, _):
        pair = lax.rem(ypos + turn, 2)
        z1, _ = first_norm(pair)
        middle = laid(xr, pair) + z1 * g1[...][None, :] + s1[...][None, :]
        ml = middle.astype(BF)
        rows = pl.ds(pl.multiple_of(pair * 512, 512), 512)
        mlow[rows, :] = ml
        out = jnp.zeros((512, 512), F32)
        for c in range(8):
            cols = slice(256 * c, 256 * c + 256)
            part_cols = slice(256 * (c % 2), 256 * (c % 2) + 256)
            hid = nn(ml, we[:, cols]) + be[cols][None, :]
            cap, low = gelu_parts(hid)
            a = (hid * cap).astype(BF)
            act[c // 2, rows, part_cols] = a
            dhid[c // 2, rows, part_cols] = (cap + hid * low).astype(BF)
            out = out + nn(a, wc[cols, :])
        out = out + bc[...][None, :]
        ctr2 = out - jnp.mean(out, axis=1, keepdims=True)
        r2 = lax.rsqrt(jnp.mean(ctr2 * ctr2, axis=1, keepdims=True) + EPS_NORM)
        z2 = ctr2 * r2
        result = middle + z2 * g2[...][None, :] + s2[...][None, :]
        for i in range(2):
            quads = [[result[256 * i + 64 * (2 * qr + qc) :][:64] for qc in range(2)] for qr in range(2)]
            w = 2 * pair + i
            xr[w] = from_blocks(quads).astype(BF)

            @pl.when(w != me)
            def _(w=w):
                res_copy(w).start()

        @pl.when(turn == 0)
        def _():
            own_c.wait()
            spread_in(cot_hbm, cr, s_c, r_c, 3 - 2 * core).wait_recv()

        @pl.when(turn == 1)
        def _():
            spread_in(cot_hbm, cr, s_c, r_c, 2).wait_recv()
            spread_in(cot_hbm, cr, s_c, r_c, 1 + 2 * core).wait_recv()

        e = laid(cr, pair)
        acc_s[0] += col_sum(e * z2)
        acc_s[1] += col_sum(e)
        dn = e * g2[...][None, :]
        dv = r2 * (
            dn - jnp.mean(dn, axis=1, keepdims=True) - z2 * jnp.mean(dn * z2, axis=1, keepdims=True)
        )
        do = dv.astype(BF)
        dout[rows, :] = do
        acc_s[2] += col_sum(do.astype(F32))
        return 0

    lax.fori_loop(0, 2, dense, 0)
    own_res = pltpu.make_async_copy(xr.at[me], res_hbm.at[me, 0], r_res.at[me])
    own_res.start()

    digits = {"x": (xpos, 2), "y": (ypos, 2), "z": (zpos, 4), "p": (plane_pos, 4)}

    def digit_peer(d, k):
        if d == "z":
            return z_peer(k)
        if d == "p":
            return plane_peer(k)
        return x_peer if d == "x" else y_peer

    def sum_unit(a, src, land, out, order):
        n = src.shape[1]
        levels, at, size, room, sem = [], core * 256, 256, 256, 1
        for d in order:
            pos, count = digits[d]
            part_size = size // count
            levels.append((d, pos, count, at, part_size, room, sem))
            at, room, sem = at + pos * part_size, room + (count - 1) * part_size, sem + count - 1
            size = part_size
        own_at, last = at, len(order) - 1

        def rows(start, length):
            return pl.ds(pl.multiple_of(start, 16), length)

        def copy(src_at, dst, length, i, peer):
            return remote(src.at[rows(src_at, length)], dst, s_ar.at[a, i], r_ar.at[a, i], peer)

        def core_send():
            return copy((1 - core) * 256, land.at[pl.ds(0, 256)], 256, 0, core_peer)

        def down(j, k):
            d, pos, count, at, length, room, sem = levels[j]
            dst = land.at[pl.ds(room + (k - 1) * length, length)]
            return copy(at + lax.rem(pos + k, count) * length, dst, length, sem + k - 1, digit_peer(d, k))

        def up(j, k, pos):
            d, _, count, at, length, _, sem = levels[j]
            here = out.at[rows(at + pos * length, length)]
            from_ = src.at[rows(own_at, length)] if j == last else here
            return remote(from_, here, s_ar.at[a, 6 + sem + k], r_ar.at[a, 6 + sem + k], digit_peer(d, k))

        def core_up(c):
            here = out.at[rows(c * 256, 256)]
            return remote(here, here, s_ar.at[a, 14], r_ar.at[a, 14], core_peer)

        def far_send(k):
            return copy(own_at, far.at[a, k - 1, :, 0:n], 16, 15 + k - 1, far_peer(k))

        def peers(j):
            return range(1, levels[j][2])

        def from_pos(j, k):
            return lax.rem(levels[j][1] + levels[j][2] - k, levels[j][2])

        def local():
            here = rows(own_at, 16)
            return pltpu.make_async_copy(src.at[here], out.at[here], l_ar.at[a])

        def step_core():
            core_send().start()

        def step_down(j):
            if j == 0:
                core_send().wait_recv()
                at = rows(core * 256, 256)
                src[at, :] = src[at, :] + land[0:256, :]
            else:
                take(j - 1)
            for k in peers(j):
                down(j, k).start()

        def take(j):
            d, pos, count, at, length, room, sem = levels[j]
            here = rows(at + pos * length, length)
            for k in peers(j):
                down(j, k).wait_recv()
            total = src[here, :].astype(F32)
            for k in peers(j):
                r = room + (k - 1) * length
                total = total + land[r : r + length, :].astype(F32)
            src[here, :] = total.astype(BF)

        def step_turn():
            take(last)
            if extra > 1:
                here = rows(own_at, 16)
                for k in range(1, extra):
                    far_send(k).start()
                total = src[here, :].astype(F32)
                for k in range(1, extra):
                    far_send(k).wait()
                    total = total + far[a, k - 1, :, 0:n].astype(F32)
                src[here, :] = total.astype(BF)
            for k in peers(last):
                up(last, k, levels[last][1]).start()
            local().start()

        def step_up(j):
            if j == last:
                local().wait()
            for k in peers(j):
                up(j, k, from_pos(j, k)).wait_recv()
            if j == 0:
                core_up(core).start()
            else:
                for k in peers(j - 1):
                    up(j - 1, k, levels[j - 1][1]).start()

        def step_last():
            core_up(1 - core).wait_recv()

        def step_sent():
            core_send().wait_send()
            core_up(core).wait_send()
            for j in range(last + 1):
                for k in peers(j):
                    down(j, k).wait_send()
                    up(j, k, levels[j][1]).wait_send()

        steps = [step_core] + [functools.partial(step_down, j) for j in range(last + 1)] + [step_turn]
        return steps + [functools.partial(step_up, j) for j in range(last, -1, -1)] + [step_last, step_sent]

    def together(units):
        return [lambda steps=steps: [step() for step in steps] for steps in zip(*units)]

    wide_units = [sum_unit(a, asum.at[a], rec.at[a], wide_hbm.at[a], ORDERS[a]) for a in range(9)]
    groups = [together(wide_units[2 * i : 2 * i + 2]) for i in range(4)] + [wide_units[8]]
    for p in range(2):
        part_units = []
        for i in range(3):
            place = (pl.ds(512 * (i // 2), 512), pl.ds(256 * (i % 2), 256))
            part_units.append(
                sum_unit(
                    9 + 3 * p + i, act.at[p].at[place], act.at[2 + p].at[place], qkv_hbm.at[p, i],
                    ORDERS[9 + 3 * p + i],
                )
            )
        groups.append(together(part_units))

    def small_steps():
        mine, other = pl.ds(pl.multiple_of(16 * core, 16), 16), pl.ds(pl.multiple_of(16 - 16 * core, 16), 16)

        def copy(src, dst, i, peer):
            return remote(src, dst, s_sm.at[i], r_sm.at[i], peer)

        def core_send():
            return copy(small_s.at[0, other], small_c, 0, core_peer)

        def plane_send(k):
            return copy(small_s.at[1, mine], small_p.at[k - 1], k, plane_peer(k))

        def z_send(k):
            return copy(small_s.at[2, mine], small_z.at[k - 1], 3 + k, z_peer(k))

        def far_copy(k):
            return copy(small_s.at[3, mine], small_far.at[k - 1], 7 + k, far_peer(k))

        def core_up(rows):
            return copy(small_o.at[rows], small_o.at[rows], 7, core_peer)

        def step0():
            core_send().start()

        def step1():
            core_send().wait_recv()
            small_s[1, mine, :] = small_s[0, mine, :] + small_c[...]
            for k in range(1, 4):
                plane_send(k).start()

        def step2():
            total = small_s[1, mine, :]
            for k in range(1, 4):
                plane_send(k).wait_recv()
                total = total + small_p[k - 1]
            small_s[2, mine, :] = total
            for k in range(1, 4):
                z_send(k).start()

        def step3():
            total = small_s[2, mine, :]
            for k in range(1, 4):
                z_send(k).wait_recv()
                total = total + small_z[k - 1]
            if extra > 1:
                small_s[3, mine, :] = total
                for k in range(1, extra):
                    far_copy(k).start()
                for k in range(1, extra):
                    far_copy(k).wait()
                    total = total + small_far[k - 1]
            small_o[mine, :] = total
            core_up(mine).start()

        def step4():
            core_up(other).wait_recv()
            small_out[...] = small_o[...]

        def step5():
            core_send().wait_send()
            core_up(mine).wait_send()
            for k in range(1, 4):
                plane_send(k).wait_send()
                z_send(k).wait_send()

        return [step0, step1, step2, step3, step4, step5]

    groups.append(small_steps())

    def run(name):
        for at, j in SCHEDULE.get(name, ()):
            groups[at][j]()

    def run_in(prefix, i):
        for at in range(8):
            if SCHEDULE.get(f"{prefix}{at}"):

                @pl.when(i == at)
                def _(at=at):
                    run(f"{prefix}{at}")

    for c in range(4):
        asum[c] = tn(act[c], dout[...]).astype(BF)
        run(f"a{c}")

    for w in range(4):
        dmid[w] = flat(to_blocks(cr[w].astype(F32))).reshape(4, 64, 512)

    def dense_back(c, _):
        cols = pl.ds(pl.multiple_of(512 * c, 512), 512)
        dh = (nt(dout[...], wc[cols, :]) * dhid[c].astype(F32)).astype(BF)
        dhid[c] = dh
        acc_s[3 + c] = col_sum(dh.astype(F32))
        dmid[...] += nt(dh, we[:, cols]).reshape(4, 4, 64, 512)
        asum[4 + c] = tn(mlow[...], dh).astype(BF)
        run_in("d", c)
        return 0

    lax.fori_loop(0, 4, dense_back, 0)

    def norm_back(pair, _):
        z1, r1 = first_norm(pair)
        dm = dmid[pl.ds(2 * pair, 2)].reshape(512, 512)
        acc_s[7] += col_sum(dm * z1)
        acc_s[8] += col_sum(dm)
        dn1 = dm * g1[...][None, :]
        db = r1 * (
            dn1 - jnp.mean(dn1, axis=1, keepdims=True) - z1 * jnp.mean(dn1 * z1, axis=1, keepdims=True)
        )
        blk[pl.ds(2 * pair, 2)] = db.astype(BF).reshape(2, 4, 64, 512)
        return 0

    lax.fori_loop(0, 2, norm_back, 0)
    run("nb")

    bias[...] = jnp.zeros_like(bias)

    def gather(o, _):
        for bcol in range(2):
            for br in range(2):
                at = (bcol * 2 + br) * 64
                cr[o, at : at + 64, :] = blk[home(o, bcol, br)]
        return 0

    lax.fori_loop(0, 4, gather, 0)
    asum[8] = tn(mixed[...].reshape(1024, 512), cr[...].reshape(1024, 512)).astype(BF)
    run("gproj")
    head_ones_half = head_ones[0:128, 0:128]
    minus = jnp.full((256, 128), -1.0, BF)
    lane32 = lax.rem(lax.broadcasted_iota(jnp.int32, (256, 128), 1), 32)

    def retreat(it, _):
        p, o = it // 4, lax.rem(it, 4)
        half = pl.ds(pl.multiple_of(256 * p, 256), 256)
        dmx = nt(cr[o], wproj[half, :])
        rows = pl.ds(pl.multiple_of(o * TOK, TOK), TOK)
        scales = scale_lanes(p)
        for gi in range(2):
            g = 2 * p + gi
            lanes = pl.ds(pl.multiple_of(128 * g, 128), 128)
            qg, kg, vg = qs[o, g], kl[o, g], vl[o, g]
            dmg = dmx[:, 128 * gi : 128 * gi + 128] * isum[o, g]
            dmp = dmg.astype(BF)
            mix = mixed[o, :, lanes].astype(F32) + mixlo[o, :, lanes].astype(F32)
            prod = dmp.astype(F32) * mix
            delta = sum(nn(p, head_ones_half) for p in split3(prod)[:2])
            delta_hi, delta_lo, _ = split3(delta)
            prod = jnp.where(lane32 == 0, delta_hi, jnp.where(lane32 == 1, delta_lo, jnp.zeros_like(delta_lo)))
            vw = jnp.concatenate([vg, minus], axis=1)
            dmp4 = jnp.concatenate([dmp * mask for mask in head_mask], axis=0)
            left = jnp.concatenate([dmp4, jnp.concatenate([prod * mask for mask in head_mask], axis=0)], axis=1)
            e4 = ex[o, g].reshape(1024, 256)
            dsf = nt(left, vw) * e4.astype(F32)
            ds = dsf.astype(BF)
            for hh in range(4):
                h, n = 4 * g + hh, 256 * hh
                bias[h, 1] += dsf[n : n + 128, 0:128] + dsf[n + 128 : n + 256, 128:256]
                bias[h, 0] += dsf[n : n + 128, 128:256]
                bias[h, 2] += dsf[n + 128 : n + 256, 0:128]
            dq = nn(
                jnp.concatenate([ds[256 * hh : 256 * hh + 256] for hh in range(4)], axis=1),
                jnp.concatenate([kg * mask for mask in head_mask], axis=0),
            )
            dk = tn(ds, jnp.concatenate([qg * mask for mask in head_mask], axis=0))
            dv = tn(e4, dmp4)
            qf, kf = qg.astype(F32), kg.astype(F32)
            scale = scales[:, 128 * gi : 128 * gi + 128]
            tq = dq * qf
            acc_s[9, :, lanes] += col_sum(tq)
            aq = nn(tq.astype(BF), head_ones_half)
            ak = nn((dk * kf).astype(BF), head_ones_half)
            dhid[0, rows, lanes] = (qinv[o, g].astype(F32) * (scale * dq - (1.0 / scale) * qf * aq)).astype(BF)
            dhid[1, rows, lanes] = (kinv[o, g].astype(F32) * (dk - kf * ak)).astype(BF)
            dhid[2, rows, lanes] = dv.astype(BF)
        run_in("r", it)

        @pl.when(lax.rem(it, 4) == 3)
        def _():
            moved = sum(
                nt(dhid[i, :, half], wqkv[:, pl.ds(pl.multiple_of(512 * i + 256 * p, 256), 256)])
                for i in range(3)
            )
            for w in range(4):
                for bcol in range(2):
                    for br in range(2):
                        at = 256 * w + (bcol * 2 + br) * 64
                        dmid[home(w, bcol, br)] += moved[at : at + 64, :]
            xflat = xroll[...].reshape(1024, 512)
            for i in range(3):
                grad = tn(xflat, dhid[i, :, half]).astype(BF)
                act[p, 512 * (i // 2) : 512 * (i // 2) + 512, 256 * (i % 2) : 256 * (i % 2) + 256] = grad

        run_in("gq", jnp.where(lax.rem(it, 4) == 3, p, -1))
        return 0

    lax.fori_loop(0, 8, retreat, 0)

    def gin_copy(w):
        return remote(slope.at[w], gin_hbm.at[me, 0], s_gin.at[w], r_gin.at[me], (img, w))

    def finish(w, _):
        quads = [[dmid[w, 2 * qr + qc] for qc in range(2)] for qr in range(2)]
        slope[w] = from_blocks(quads).astype(BF)

        @pl.when(w != me)
        def _():
            gin_copy(w).start()

        return 0

    lax.fori_loop(0, 4, finish, 0)
    own_gin = pltpu.make_async_copy(slope.at[me], gin_hbm.at[me, 0], r_gin.at[me])
    own_gin.start()
    run("finish")

    row_ones = jnp.ones((8, 1024), BF)

    def put(row, v):
        small_s[0, row : row + v.shape[0], :] = v

    put(ROW_QB, nn(row_ones, dhid[0])[0:1])
    put(ROW_VB, nn(row_ones, dhid[2])[0:1])
    put(ROW_BP, nn(row_ones, cr[...].reshape(1024, 512))[0:1])
    for row, i in ((ROW_LS, 9), (ROW_G1, 7), (ROW_S1, 8), (ROW_B2, 2), (ROW_G2, 0), (ROW_S2, 1)):
        put(row, jnp.sum(acc_s[i], axis=0, keepdims=True))
    for c in range(4):
        put(ROW_BE + c, jnp.sum(acc_s[3 + c], axis=0, keepdims=True))
    run("puts")
    short = jnp.zeros((384, 256), F32)
    for c in range(4):
        places = one_hot_places(c)
        left = jnp.concatenate(
            [bias[:, :, 8 * r : 8 * r + 8, :].reshape(384, 128) for r in range(4 * c, 4 * c + 4)], axis=1
        )
        for p in split3(left)[:2]:
            short = short + nt(p, places)
    pick = one_hot_pick()
    for i in range(4):
        piece = split3(short[96 * i : 96 * i + 96])[:2]
        part[4 * i : 4 * i + 4] = sum(nt(p, pick) for p in piece).reshape(4, 24, 1024)
    run("bb")
    dtab = jnp.zeros((16, 1024), F32)
    for u in range(24):
        dtab = dtab + pltpu.roll(part[:, u, :], 23 - u, 1)
    tab[...] = dtab * tab[...] * (1.0 - tab[...] * (1.0 / BIAS_RANGE))
    small_s[0, ROW_W1 : ROW_W2 + 16, :] = jnp.zeros((ROW_W2 + 16 - ROW_W1, 512), F32)

    def net_back(c, _):
        cols, pre = net_piece(c)
        cap, low = gelu_parts(pre)
        dlog, dlog_lo, _ = split3(tab[:, cols])
        units, units_lo, _ = split3(pre * cap)
        small_s[0, ROW_W2 : ROW_W2 + 16, :] += nn(dlog, units) + nn(dlog_lo, units) + nn(dlog, units_lo)
        w_hi, w_lo, _ = split3(w2t[...])
        back = tn(dlog, w_hi) + tn(dlog_lo, w_hi) + tn(dlog, w_lo)
        dpre, dpre_lo, _ = split3(back * (cap + pre * low))
        hi, mid, _ = split3(crow[:, cols])
        net = nn(hi, dpre) + nn(mid, dpre) + nn(hi, dpre_lo)
        small_s[0, ROW_W1 : ROW_W1 + 3, :] += net[0:3]
        return 0

    lax.fori_loop(0, 4, net_back, 0)
    run("net")
    run("end")

    for group in groups:
        group[-1]()
    own_res.wait()
    own_gin.wait()
    for k in (1, 2, 3):
        frm, to = ring_from(k), lax.rem(me + k, n_win)
        x_send(k, 0).wait_send()
        x_send(k, 1).wait_send()
        spread(cot_hbm, cr, s_c, r_c, k).wait_send()
        res_copy(to).wait_send()
        gin_copy(to).wait_send()
        remote(xr.at[frm], res_hbm.at[frm, 0], s_res.at[frm], r_res.at[frm], (img, frm)).wait_recv()
        remote(slope.at[frm], gin_hbm.at[frm, 0], s_gin.at[frm], r_gin.at[frm], (img, frm)).wait_recv()


def widen_kernel(
    res, gin, wide, qkv, small,
    res_out, gin_out, w_qkv, g_qb, g_vb, g_ls, g_w1, g_b1, g_w2, w_proj, g_bp, g_g1, g_s1, w_fc1, g_be,
    w_fc2, g_b2, g_g2, g_s2,
    blocks, wide_in, qkv_in, wide_f, qkv_f, s_in, s_out, s_blocks,
):
    taken = [pltpu.make_async_copy(a, blocks.at[i], s_blocks.at[i]) for i, a in enumerate((res, gin))]
    passed = [pltpu.make_async_copy(blocks.at[i], a, s_blocks.at[2 + i]) for i, a in enumerate((res_out, gin_out))]
    pieces = []
    for i in range(9):
        if i < 4:
            place = w_fc2.at[pl.ds(512 * i, 512), :]
        elif i < 8:
            place = w_fc1.at[:, pl.ds(512 * (i - 4), 512)]
        else:
            place = w_proj
        pieces.append((wide.at[i], wide_in.at[i], wide_f.at[i], place))
    for i in range(6):
        place = w_qkv.at[:, pl.ds(512 * (i % 3) + 256 * (i // 3), 256)]
        pieces.append((qkv.at[i // 3, i % 3], qkv_in.at[i], qkv_f.at[i], place))
    loads = [pltpu.make_async_copy(a, b, s_in.at[i]) for i, (a, b, _, _) in enumerate(pieces)]
    stores = [pltpu.make_async_copy(c, d, s_out.at[i]) for i, (_, _, c, d) in enumerate(pieces)]
    for c in loads:
        c.start()
    for c in taken:
        c.start()
    for i, (_, b, c, _) in enumerate(pieces):
        loads[i].wait()
        c[...] = b[...].astype(F32)
        stores[i].start()
    for a, b in zip(taken, passed):
        a.wait()
        b.start()
    for row, out in (
        (ROW_QB, g_qb), (ROW_VB, g_vb), (ROW_B1, g_b1), (ROW_BP, g_bp), (ROW_G1, g_g1), (ROW_S1, g_s1),
        (ROW_B2, g_b2), (ROW_G2, g_g2), (ROW_S2, g_s2),
    ):
        out[...] = small[row, :]
    for c in range(4):
        g_be[512 * c : 512 * c + 512] = small[ROW_BE + c, :]
    g_w1[...] = small[ROW_W1 : ROW_W1 + 2, :]
    g_w2[...] = small[ROW_W2 : ROW_W2 + 16, :].T
    h0 = lax.broadcasted_iota(jnp.int32, (512, 16), 0) // 32
    h1 = lax.broadcasted_iota(jnp.int32, (512, 16), 1)
    heads = jnp.where(h0 == h1, 1.0, 0.0).astype(BF)
    per_head = sum(nn(jnp.broadcast_to(p, (8, 512)), heads) for p in split3(small[ROW_LS : ROW_LS + 1, :]))
    g_ls[...] = per_head[0, :]
    for c in passed + stores:
        c.wait()


def body(n_img, n_win, inputs, wqkv, qb, vb, hls, w1, b1, w2, wproj, bproj, g1, s1, we, be, wc, bc, g2, s2, cot):
    extra = n_img // 8
    crow, ccol = table_coords()
    dma = pltpu.SemaphoreType.DMA
    n_ar = 15 + (extra - 1)
    n_sm = 8 + (extra - 1)
    vmem = pl.BlockSpec(memory_space=pltpu.VMEM)
    hbm = pl.BlockSpec(memory_space=pl.ANY)
    smem = pl.BlockSpec(memory_space=pltpu.SMEM)
    scratch = [
        pltpu.VMEM((4, TOK, 512), BF),
        pltpu.VMEM((4, TOK, 512), BF),
        pltpu.VMEM((4, TOK, 512), BF),
        pltpu.VMEM((16, 3, 128, 128), F32),
        pltpu.VMEM((4, 4, 4, TOK, TOK), BF),
        pltpu.VMEM((4, 4, TOK, 128), BF),
        pltpu.VMEM((4, 4, TOK, 128), BF),
        pltpu.VMEM((4, 4, TOK, 128), BF),
        pltpu.VMEM((4, 4, TOK, 128), BF),
        pltpu.VMEM((4, 4, TOK, 128), BF),
        pltpu.VMEM((4, 4, TOK, 128), F32),
        pltpu.VMEM((4, TOK, 512), BF),
        pltpu.VMEM((4, TOK, 512), BF),
        pltpu.VMEM((4, 4, 64, 512), BF),
        pltpu.VMEM((4, 4, 64, 512), F32),
        pltpu.VMEM((4, 1024, 512), BF),
        pltpu.VMEM((4, 1024, 512), BF),
        pltpu.VMEM((1024, 512), BF),
        pltpu.VMEM((1024, 512), BF),
        pltpu.VMEM((4, TOK, 512), BF),
        pltpu.VMEM((16, 1024), F32),
        pltpu.VMEM((16, 24, 1024), F32),
        pltpu.VMEM((10, 8, 512), F32),
        pltpu.VMEM((9, 512, 512), BF),
        pltpu.VMEM((9, 496, 512), BF),
        pltpu.VMEM((15, extra - 1, 16, 512) if extra > 1 else (1, 1, 16, 512), BF),
        pltpu.VMEM((512, 1536), BF),
        pltpu.VMEM((512, 512), BF),
        pltpu.VMEM((512, 2048), BF),
        pltpu.VMEM((2048, 512), BF),
        pltpu.VMEM((4, SMALL_ROWS, 512), F32),
        pltpu.VMEM((16, 512), F32),
        pltpu.VMEM((3, 16, 512), F32),
        pltpu.VMEM((3, 16, 512), F32),
        pltpu.VMEM((max(extra - 1, 1), 16, 512), F32),
        pltpu.VMEM((SMALL_ROWS, 512), F32),
        dma((2, 4)), dma((2, 4)), dma((4,)), dma((4,)),
        dma((4,)), dma((4,)), dma((4,)), dma((4,)),
        dma((15, n_ar)), dma((15, n_ar)), dma((15,)),
        dma((n_sm,)), dma((n_sm,)),
        dma((4,)),
    ]
    block = jax.ShapeDtypeStruct(inputs.shape, BF)
    result, grad_inputs, wide, qkv, small = pl.pallas_call(
        functools.partial(block_kernel, n_img, n_win),
        out_shape=(
            block,
            block,
            jax.ShapeDtypeStruct((9, 512, 512), BF),
            jax.ShapeDtypeStruct((2, 3, 512, 256), BF),
            jax.ShapeDtypeStruct((SMALL_ROWS, 512), F32),
        ),
        in_specs=[hbm] * 6 + [vmem] * 2 + [smem] + [vmem] * 12,
        out_specs=(hbm, hbm, hbm, hbm, vmem),
        scratch_shapes=scratch,
        compiler_params=pltpu.CompilerParams(
            collective_id=0, has_side_effects=True, vmem_limit_bytes=64 * 1024 * 1024
        ),
    )(
        inputs, cot, wqkv, wproj, we, wc, qb, vb, hls, w1, b1, w2.T, bproj, g1, s1, be, bc, g2, s2,
        jnp.asarray(crow), jnp.asarray(ccol),
    )
    any_ = lambda shape: jax.ShapeDtypeStruct(shape, F32)
    outs = pl.pallas_call(
        widen_kernel,
        out_shape=(
            block, block, any_((512, 1536)), any_((512,)), any_((512,)), any_((16,)), any_((2, 512)),
            any_((512,)), any_((512, 16)), any_((512, 512)), any_((512,)), any_((512,)), any_((512,)),
            any_((512, 2048)), any_((2048,)), any_((2048, 512)), any_((512,)), any_((512,)), any_((512,)),
        ),
        in_specs=[hbm] * 4 + [vmem],
        out_specs=tuple(hbm if i in (0, 1, 2, 9, 13, 15) else vmem for i in range(19)),
        scratch_shapes=[
            pltpu.VMEM((2,) + inputs.shape, BF),
            pltpu.VMEM((9, 512, 512), BF),
            pltpu.VMEM((6, 512, 256), BF),
            pltpu.VMEM((9, 512, 512), F32),
            pltpu.VMEM((6, 512, 256), F32),
            dma((15,)), dma((15,)), dma((4,)),
        ],
        compiler_params=pltpu.CompilerParams(vmem_limit_bytes=63 * 1024 * 1024),
    )(result, grad_inputs, wide, qkv, small)
    return outs


def solution(mesh):
    n_img, n_win = mesh.shape["img"], mesh.shape["win"]
    block = P("img", "win", None, None)
    return jax.shard_map(
        functools.partial(body, n_img, n_win),
        mesh=mesh,
        in_specs=(block,) + (P(),) * 17 + (block,),
        out_specs=(block, block) + (P(),) * 17,
        check_vma=False,
    )
```

```python
import functools

import jax
import jax.numpy as jnp
import numpy as np
from jax import lax
from jax.experimental import pallas as pl
from jax.experimental.pallas import tpu as pltpu
from jax.sharding import PartitionSpec as P

WIN = 16
TOK = WIN * WIN
EPS_DIR = 1e-06
EPS_NORM = 1e-05
MASK_FILL = -100.0
BIAS_RANGE = 16.0
INV_ROOT_TWO = 0.7071067811865476
INV_ROOT_TWOPI = 0.3989422804014327
LOG2_E = 1.4426950408889634
MESH = pl.DeviceIdType.MESH
BF = jnp.bfloat16
F32 = jnp.float32

(ROW_QB, ROW_VB, ROW_LS, ROW_W1, ROW_B1, ROW_W2, ROW_BP, ROW_G1, ROW_S1, ROW_B2, ROW_G2, ROW_S2,
 ROW_BE, SMALL_ROWS) = (0, 1, 2, 3, 5, 6, 22, 23, 24, 25, 26, 27, 28, 32)

SCHEDULE = {
    "a1": ((0, 0),),
    "a3": ((1, 0), (0, 1)),
    "d0": ((1, 1),),
    "d1": ((2, 0), (0, 2)),
    "d2": ((2, 1), (1, 2)),
    "d3": ((3, 0), (0, 3)),
    "nb": ((3, 1), (2, 2)),
    "gproj": ((4, 0), (1, 3), (0, 4)),
    "r0": ((4, 1), (0, 5), (2, 3), (1, 4)),
    "r1": ((3, 2),),
    "r2": ((1, 5), (4, 2), (2, 4), (0, 6)),
    "r3": ((3, 3),),
    "gq0": ((5, 0), (1, 6), (4, 3), (2, 5), (5, 1), (3, 4)),
    "r4": ((0, 7), (1, 7)),
    "r5": ((4, 4), (5, 2), (2, 6), (3, 5), (1, 8)),
    "r6": ((0, 8),),
    "r7": ((4, 5), (5, 3), (2, 7)),
    "gq1": ((6, 0), (3, 6), (4, 6), (1, 9), (6, 1), (5, 4), (1, 10), (0, 9), (3, 7)),
    "finish": ((2, 8), (0, 10)),
    "bb": ((6, 2), (5, 5), (3, 8)),
    "net": ((7, 0), (2, 9), (7, 1)),
    "end": ((6, 3), (2, 10), (3, 9), (5, 6), (3, 10), (6, 4), (7, 2), (5, 7), (5, 8), (7, 3), (6, 5), (7, 4), (6, 6)),
}
ORDERS = (
    "wvxy", "xwvy", "xywv", "yxwv", "xywv", "wvxy", "xwyv", "xwyv", "pz",
    "xzy", "yxz", "xzy", "pz", "pz", "pz",
)


def nn(a, b):
    return lax.dot_general(a, b, (((1,), (0,)), ((), ())), preferred_element_type=F32)


def nt(a, b):
    return lax.dot_general(a, b, (((1,), (1,)), ((), ())), preferred_element_type=F32)


def tn(a, b):
    return lax.dot_general(a, b, (((0,), (0,)), ((), ())), preferred_element_type=F32)


def split3(v):
    hi = v.astype(BF)
    rest = v - hi.astype(F32)
    mid = rest.astype(BF)
    return hi, mid, (rest - mid.astype(F32)).astype(BF)


def gelu_parts(v):
    cap = 0.5 + 0.5 * lax.erf(v * INV_ROOT_TWO)
    return cap, INV_ROOT_TWOPI * jnp.exp2(v * v * (-0.5 * LOG2_E))


def col_sum(v):
    return jnp.sum(v.reshape(v.shape[0] // 8, 8, v.shape[1]), axis=0)


def to_blocks(v):
    n = v.shape[-1]
    t = v.reshape(2, 8, 2, 8, n)
    return [[t[qr, :, qc].reshape(64, n) for qc in range(2)] for qr in range(2)]


def from_blocks(quads):
    n = quads[0][0].shape[-1]
    rows = []
    for qr in range(2):
        a = quads[qr][0].reshape(8, 1, 8, n)
        b = quads[qr][1].reshape(8, 1, 8, n)
        rows.append(jnp.concatenate([a, b], axis=1).reshape(128, n))
    return jnp.concatenate(rows, axis=0)


def one_hot_places(c):
    l = lax.broadcasted_iota(jnp.int32, (256, 512), 0)
    k = lax.broadcasted_iota(jnp.int32, (256, 512), 1) + 512 * c
    return jnp.where(l == 8 * (15 - k // 128) + k % 128, 1.0, 0.0).astype(BF)


def one_hot_pick():
    k = lax.broadcasted_iota(jnp.int32, (1024, 256), 0)
    l = lax.broadcasted_iota(jnp.int32, (1024, 256), 1)
    return jnp.where(k == 32 * (l // 8) + l % 8, 1.0, 0.0).astype(BF)


def table_coords():
    k = np.arange(1024)
    out = np.zeros((2, 1024), np.float64)
    for i, off in enumerate((15 - k // 32, 15 - k % 32)):
        u = off * (8.0 / 15.0)
        out[i] = np.sign(u) * np.log2(np.abs(u) + 1.0) / 3.0
    rows = np.zeros((8, 1024), np.float32)
    rows[0:2] = out
    rows[2] = 1.0
    return rows


def net_first(cols, w1, b1):
    return cols[:, 0:1] * w1[0:1, :] + cols[:, 1:2] * w1[1:2, :] + b1


def block_kernel(
    n_img, n_win,
    x_hbm, cot_hbm, wqkv_hbm, wproj_hbm, we_hbm, wc_hbm, hls, qb_hbm, vb_hbm, w1_hbm, b1_hbm,
    w2t_hbm, bproj_hbm, g1_hbm, s1_hbm, be_hbm, bc_hbm, g2_hbm, s2_hbm, crow_hbm,
    res_hbm, gin_hbm, wide_hbm, qkv_hbm, small_out,
    xr, cr, xroll, bias, ex, qs, kl, vl, qinv, kinv, isum, mixed, mixlo, blk, dmid, act, dhid, dout,
    mlow, slope, tab, part, acc_s, asum, rec, far, wqkv, wproj, we, wc,
    qb, vb, w1, b1, w2t, bproj, g1, s1, be, bc, g2, s2, crow,
    small_s, small_c, small_p, small_z, small_far, small_o,
    s_x, r_x, s_c, r_c, s_res, r_res, s_gin, r_gin, s_ar, r_ar, l_ar, s_sm, r_sm, s_w, s_v,
):
    img = lax.axis_index("img")
    me = lax.axis_index("win")
    extra = n_img // 8
    core = lax.rem(me, 2)
    ypos = me // 2
    xpos = lax.rem(img, 2)
    zpos = lax.rem(img // 2, 4)
    upper = img // 8

    def ring_to(k):
        return (img, lax.rem(me + k, n_win))

    def ring_from(k):
        return lax.rem(me + n_win - k, n_win)

    core_peer = (img, me + 1 - 2 * core)
    y_peer = (img, lax.rem(me + 2, 4))
    x_peer = (img + 1 - 2 * xpos, me)
    plane_pos = 2 * xpos + ypos

    def z_peer(k):
        return (upper * 8 + lax.rem(zpos + k, 4) * 2 + xpos, me)

    def plane_peer(k):
        to = lax.rem(plane_pos + k, 4)
        return (img + to // 2 - xpos, lax.rem(to, 2) * 2 + core)

    def far_peer(k):
        return (lax.rem(upper + k, extra) * 8 + zpos * 2 + xpos, me)

    weights = [
        pltpu.make_async_copy(a, b, s_w.at[i])
        for i, (a, b) in enumerate(((wqkv_hbm, wqkv), (wproj_hbm, wproj), (we_hbm, we), (wc_hbm, wc)))
    ]

    own_x = pltpu.make_async_copy(x_hbm.at[me, 0], xr.at[me], r_x.at[0, 0])
    own_c = pltpu.make_async_copy(cot_hbm.at[me, 0], cr.at[me], r_c.at[0])
    vectors = [
        pltpu.make_async_copy(a, b, s_v.at[i])
        for i, (a, b) in enumerate(
            (
                (w1_hbm, w1), (b1_hbm, b1), (w2t_hbm, w2t), (crow_hbm, crow), (qb_hbm, qb), (vb_hbm, vb),
                (bproj_hbm, bproj), (g1_hbm, g1), (s1_hbm, s1), (be_hbm, be), (bc_hbm, bc), (g2_hbm, g2),
                (s2_hbm, s2),
            )
        )
    ]
    for c in vectors + [own_x] + weights + [own_c]:
        c.start()

    barrier = pltpu.get_barrier_semaphore()
    others = [ring_to(k) for k in range(1, n_win)] + [x_peer, (img + 1 - 2 * xpos, lax.rem(me + 2, 4))]
    others += [z_peer(k) for k in range(1, 4)] + [far_peer(k) for k in range(1, extra)]
    for peer in others:
        pl.semaphore_signal(barrier, inc=1, device_id=peer, device_id_type=MESH)
    pl.semaphore_wait(barrier, len(others))

    def remote(src, dst, ssem, rsem, peer):
        return pltpu.make_async_remote_copy(
            src_ref=src, dst_ref=dst, send_sem=ssem, recv_sem=rsem, device_id=peer, device_id_type=MESH
        )

    def spread(src_hbm, dst, ssem, rsem, k):
        to = lax.rem(me + k, n_win)
        return remote(src_hbm.at[to, 0], dst.at[me], ssem.at[k], rsem.at[k], ring_to(k))

    def spread_in(src_hbm, dst, ssem, rsem, k):
        frm = ring_from(k)
        return remote(src_hbm.at[frm, 0], dst.at[frm], ssem.at[k], rsem.at[k], ring_to(k))

    def half_rows(w, half):
        return pl.ds(pl.multiple_of(128 * (1 - w // 2 if half == 0 else w // 2), 128), 128)

    def x_send(k, half):
        to, rows = lax.rem(me + k, n_win), half_rows(me, half)
        return remote(
            x_hbm.at[to, 0, rows], xr.at[me, rows], s_x.at[half, k], r_x.at[half, k], ring_to(k)
        )

    def x_arrival(k, half):
        frm = ring_from(k)
        rows = half_rows(frm, half)
        return remote(x_hbm.at[frm, 0, rows], xr.at[frm, rows], s_x.at[half, k], r_x.at[half, k], ring_to(k))

    for half in range(2):
        for k in (2, 1, 3):
            x_send(k, half).start()
    for k in (2, 1, 3):
        spread(cot_hbm, cr, s_c, r_c, k).start()

    for c in vectors:
        c.wait()
    def net_piece(c):
        rows = pl.ds(pl.multiple_of(256 * c, 256), 256)
        return rows, net_first(crow[:, rows].T, w1[...], b1[...][None, :])

    def look_up(c, _):
        cols, pre = net_piece(c)
        logits = lax.dot_general(
            w2t[...], pre * gelu_parts(pre)[0], (((1,), (1,)), ((), ())),
            precision=lax.Precision.HIGHEST, preferred_element_type=F32,
        )
        tab[:, cols] = BIAS_RANGE / (1.0 + jnp.exp(-logits))
        return 0

    lax.fori_loop(0, 4, look_up, 0)
    for u in range(24):
        part[:, u, :] = pltpu.roll(tab[...], 1001 + u, 1)
    pick = one_hot_pick()
    short = jnp.concatenate(
        [sum(nn(p, pick) for p in split3(part[4 * i : 4 * i + 4].reshape(96, 1024))) for i in range(4)], axis=0
    )
    short_parts = split3(short)
    for c in range(4):
        places = one_hot_places(c)
        wide = sum(nn(p, places) for p in short_parts)
        for r in range(4):
            row = 8 * (4 * c + r)
            bias[:, :, row : row + 8, :] = wide[:, 128 * r : 128 * r + 128].reshape(16, 3, 8, 128)

    lane = lax.broadcasted_iota(jnp.int32, (1, 128), 1)
    head_mask = [jnp.where(lane // 32 == hh, 1.0, 0.0).astype(BF) for hh in range(4)]
    l0 = lax.broadcasted_iota(jnp.int32, (256, 256), 0)
    l1 = lax.broadcasted_iota(jnp.int32, (256, 256), 1)
    head_ones = jnp.where(l0 // 32 == l1 // 32, 1.0, 0.0).astype(BF)

    def scale_lanes(p):
        wide = lax.broadcasted_iota(jnp.int32, (1, 256), 1) // 32
        out = jnp.zeros((1, 256), F32)
        for i in range(8):
            out = jnp.where(wide == i, hls[8 * p + i], out)
        return jnp.exp(out)

    def lay(half):
        def one(w, _):
            late = w // 2 if half == 0 else 1 - w // 2
            rows = pl.ds(pl.multiple_of(128 * (1 - late), 128), 128)
            v = xr[w, rows, :].astype(F32).reshape(8, 2, 8, 512)
            for qc in range(2):
                bcol = 1 - qc
                ocol = lax.rem(w, 2) if bcol == 0 else 1 - lax.rem(w, 2)
                at = pl.ds(pl.multiple_of((bcol * 2 + late) * 64, 64), 64)
                xroll[2 * half + ocol, at, :] = v[:, qc].reshape(64, 512).astype(BF)
            return 0

        lax.fori_loop(0, 4, one, 0)

    def project(half):
        xw = xroll[2 * half : 2 * half + 2].reshape(512, 512)

        def one(p, _):
            def cols(i):
                return pl.ds(pl.multiple_of(512 * i + 256 * p, 256), 256)

            q = nn(xw, wqkv[:, cols(0)]) + qb[cols(0)][None, :]
            qi = lax.rsqrt(nn((q * q).astype(BF), head_ones) + EPS_DIR)
            qsc = (q * qi * scale_lanes(p)).astype(BF)
            k = nn(xw, wqkv[:, cols(1)])
            ki = lax.rsqrt(nn((k * k).astype(BF), head_ones) + EPS_DIR)
            kn = (k * ki).astype(BF)
            v = (nn(xw, wqkv[:, cols(2)]) + vb[cols(0)][None, :]).astype(BF)
            for w in range(2):
                rows = slice(256 * w, 256 * w + 256)
                for i in range(2):
                    lanes = slice(128 * i, 128 * i + 128)
                    at = (2 * half + w, 2 * p + i)
                    qs[at] = qsc[rows, lanes]
                    kl[at] = kn[rows, lanes]
                    vl[at] = v[rows, lanes]
                    qinv[at] = qi[rows, lanes].astype(BF)
                    kinv[at] = ki[rows, lanes].astype(BF)
            return 0

        lax.fori_loop(0, 2, one, 0)

    own_x.wait()
    for k in (1, 2, 3):
        x_arrival(k, 0).wait_recv()
    lay(0)
    weights[0].wait()
    project(0)
    weights[1].wait()

    row_half = lax.broadcasted_iota(jnp.int32, (128, 128), 0) // 64
    col_half = lax.broadcasted_iota(jnp.int32, (128, 128), 1) // 64
    apart = jnp.where(row_half == col_half, 0.0, MASK_FILL)

    def home(o, bcol, br):
        row, col = lax.rem(2 * (o // 2) + br + 1, 4), lax.rem(2 * lax.rem(o, 2) + bcol + 1, 4)
        return 2 * (row // 2) + col // 2, 2 * lax.rem(row, 2) + lax.rem(col, 2)

    def attend(o, _):
        @pl.when(o == 2)
        def _():
            for k in (1, 2, 3):
                x_arrival(k, 1).wait_recv()
            lay(1)
            project(1)

        rows_cut = jnp.where(o // 2 == 1, apart, 0.0)
        cols_cut = jnp.where(lax.rem(o, 2) == 1, jnp.full((128, 128), MASK_FILL, F32), rows_cut)

        for g in range(4):
            qg, kg, vg = qs[o, g], kl[o, g], vl[o, g]
            sc = nt(jnp.concatenate([qg * mask for mask in head_mask], axis=0), kg)
            for hh in range(4):
                h, n = 4 * g + hh, 256 * hh
                ex[o, g, hh, 0:128, 0:128] = jnp.exp(sc[n : n + 128, 0:128] + bias[h, 1] + rows_cut).astype(BF)
                ex[o, g, hh, 0:128, 128:256] = jnp.exp(sc[n : n + 128, 128:256] + bias[h, 0] + cols_cut).astype(BF)
                ex[o, g, hh, 128:256, 0:128] = jnp.exp(sc[n + 128 : n + 256, 0:128] + bias[h, 2] + cols_cut).astype(BF)
                ex[o, g, hh, 128:256, 128:256] = jnp.exp(
                    sc[n + 128 : n + 256, 128:256] + bias[h, 1] + rows_cut
                ).astype(BF)
            ones = [jnp.broadcast_to(mask, (256, 128)) for mask in head_mask]
            total = nn(
                jnp.concatenate([ex[o, g, hh] for hh in range(4)], axis=1),
                jnp.concatenate(
                    [jnp.concatenate([vg * mask, one], axis=1) for mask, one in zip(head_mask, ones)], axis=0
                ),
            )
            inv = 1.0 / total[:, 128:256]
            isum[o, g] = inv
            mix = total[:, 0:128] * inv
            mix_hi = mix.astype(BF)
            mixed[o, :, 128 * g : 128 * g + 128] = mix_hi
            mixlo[o, :, 128 * g : 128 * g + 128] = (mix - mix_hi.astype(F32)).astype(BF)

        branch = (nn(mixed[o], wproj[...]) + bproj[...][None, :]).astype(BF)
        for bcol in range(2):
            for br in range(2):
                at = (bcol * 2 + br) * 64
                blk[home(o, bcol, br)] = branch[at : at + 64, :]
        return 0

    lax.fori_loop(0, 4, attend, 0)

    weights[2].wait()
    weights[3].wait()
    acc_s[...] = jnp.zeros_like(acc_s)

    def res_copy(w):
        return remote(xr.at[w], res_hbm.at[me, 0], s_res.at[w], r_res.at[me], (img, w))

    def flat(quads):
        return jnp.concatenate([quads[0][0], quads[0][1], quads[1][0], quads[1][1]], axis=0)

    def first_norm(pair):
        back = blk[pl.ds(2 * pair, 2)].reshape(512, 512).astype(F32)
        ctr = back - jnp.mean(back, axis=1, keepdims=True)
        r1 = lax.rsqrt(jnp.mean(ctr * ctr, axis=1, keepdims=True) + EPS_NORM)
        return ctr * r1, r1

    def laid(ref, pair):
        return jnp.concatenate([flat(to_blocks(ref[2 * pair + i].astype(F32))) for i in range(2)], axis=0)

    def dense(turn, _):
        pair = lax.rem(ypos + turn, 2)
        z1, _ = first_norm(pair)
        middle = laid(xr, pair) + z1 * g1[...][None, :] + s1[...][None, :]
        ml = middle.astype(BF)
        rows = pl.ds(pl.multiple_of(pair * 512, 512), 512)
        mlow[rows, :] = ml
        out = jnp.zeros((512, 512), F32)
        for c in range(8):
            cols = slice(256 * c, 256 * c + 256)
            part_cols = slice(256 * (c % 2), 256 * (c % 2) + 256)
            hid = nn(ml, we[:, cols]) + be[cols][None, :]
            cap, low = gelu_parts(hid)
            a = (hid * cap).astype(BF)
            act[c // 2, rows, part_cols] = a
            dhid[c // 2, rows, part_cols] = (cap + hid * low).astype(BF)
            out = out + nn(a, wc[cols, :])
        out = out + bc[...][None, :]
        ctr2 = out - jnp.mean(out, axis=1, keepdims=True)
        r2 = lax.rsqrt(jnp.mean(ctr2 * ctr2, axis=1, keepdims=True) + EPS_NORM)
        z2 = ctr2 * r2
        result = middle + z2 * g2[...][None, :] + s2[...][None, :]
        for i in range(2):
            quads = [[result[256 * i + 64 * (2 * qr + qc) :][:64] for qc in range(2)] for qr in range(2)]
            w = 2 * pair + i
            xr[w] = from_blocks(quads).astype(BF)

            @pl.when(w != me)
            def _(w=w):
                res_copy(w).start()

        @pl.when(turn == 0)
        def _():
            own_c.wait()
            spread_in(cot_hbm, cr, s_c, r_c, 3 - 2 * core).wait_recv()

        @pl.when(turn == 1)
        def _():
            spread_in(cot_hbm, cr, s_c, r_c, 2).wait_recv()
            spread_in(cot_hbm, cr, s_c, r_c, 1 + 2 * core).wait_recv()

        e = laid(cr, pair)
        acc_s[0] += col_sum(e * z2)
        acc_s[1] += col_sum(e)
        dn = e * g2[...][None, :]
        dv = r2 * (
            dn - jnp.mean(dn, axis=1, keepdims=True) - z2 * jnp.mean(dn * z2, axis=1, keepdims=True)
        )
        do = dv.astype(BF)
        dout[rows, :] = do
        acc_s[2] += col_sum(do.astype(F32))
        return 0

    lax.fori_loop(0, 2, dense, 0)
    own_res = pltpu.make_async_copy(xr.at[me], res_hbm.at[me, 0], r_res.at[me])
    own_res.start()

    digits = {
        "x": (xpos, 2), "y": (ypos, 2), "z": (zpos, 4), "p": (plane_pos, 4),
        "w": (lax.rem(zpos, 2), 2), "v": (zpos // 2, 2),
    }

    def digit_peer(d, k):
        if d == "z":
            return z_peer(k)
        if d == "p":
            return plane_peer(k)
        z_step = {"w": 1 - 2 * lax.rem(zpos, 2), "v": 2 - 4 * (zpos // 2)}
        if d in z_step:
            return (img + 2 * z_step[d], me)
        return x_peer if d == "x" else y_peer

    def sum_unit(a, src, land, out, order):
        n = src.shape[1]
        levels, at, size, room = [], core * 256, 256, 256
        for d in order:
            pos, count = digits[d]
            part_size = size // count
            levels.append((d, pos, count, at, part_size, room))
            at, room = at + pos * part_size, room + (count - 1) * part_size
            size = part_size
        own_at, last = at, len(order) - 1

        def rows(start, length):
            return pl.ds(pl.multiple_of(start, 16), length)

        def copy(src_at, dst, length, i, peer):
            return remote(src.at[rows(src_at, length)], dst, s_ar.at[a, 0], r_ar.at[a, i], peer)

        def core_send():
            return copy((1 - core) * 256, land.at[pl.ds(0, 256)], 256, 0, core_peer)

        def down(j, k):
            d, pos, count, at, length, room = levels[j]
            dst = land.at[pl.ds(room + (k - 1) * length, length)]
            return copy(at + lax.rem(pos + k, count) * length, dst, length, 1 + j, digit_peer(d, k))

        def all_down(j):
            d, _, count, _, length, room = levels[j]
            dst = land.at[pl.ds(room, (count - 1) * length)]
            return copy(0, dst, (count - 1) * length, 1 + j, digit_peer(d, 1))

        def up(j, k):
            d, pos, count, at, length, _ = levels[j]
            here = out.at[rows(at + pos * length, length)]
            from_ = src.at[rows(own_at, length)] if j == last else here
            return remote(from_, here, s_ar.at[a, 1], r_ar.at[a, 5 + j], digit_peer(d, k))

        def all_up(j):
            d, _, count, _, length, _ = levels[j]
            some = out.at[pl.ds(0, (count - 1) * length)]
            return remote(some, some, s_ar.at[a, 1], r_ar.at[a, 5 + j], digit_peer(d, 1))

        def core_up(c):
            here = out.at[rows(c * 256, 256)]
            return remote(here, here, s_ar.at[a, 1], r_ar.at[a, 9], core_peer)

        def all_sent(i):
            some = out.at[pl.ds(0, 496)]
            return remote(some, some, s_ar.at[a, i], r_ar.at[a, 0], core_peer)

        def far_send(k):
            return remote(
                src.at[rows(own_at, 16)], far.at[a, k - 1, :, 0:n], s_ar.at[a, 1 + k], r_ar.at[a, 9 + k],
                far_peer(k),
            )

        def peers(j):
            return range(1, levels[j][2])

        def local():
            here = rows(own_at, 16)
            return pltpu.make_async_copy(src.at[here], out.at[here], l_ar.at[a])

        def step_core():
            core_send().start()

        def step_down(j):
            if j == 0:
                core_send().wait_recv()
                at = rows(core * 256, 256)
                src[at, :] = src[at, :] + land[0:256, :]
            else:
                take(j - 1)
            for k in peers(j):
                down(j, k).start()

        def take(j):
            d, pos, count, at, length, room = levels[j]
            here = rows(at + pos * length, length)
            all_down(j).wait_recv()
            total = src[here, :].astype(F32)
            for k in peers(j):
                r = room + (k - 1) * length
                total = total + land[r : r + length, :].astype(F32)
            src[here, :] = total.astype(BF)

        def step_turn():
            take(last)
            if extra > 1:
                here = rows(own_at, 16)
                for k in range(1, extra):
                    far_send(k).start()
                total = src[here, :].astype(F32)
                for k in range(1, extra):
                    far_send(k).wait()
                    total = total + far[a, k - 1, :, 0:n].astype(F32)
                src[here, :] = total.astype(BF)
            for k in peers(last):
                up(last, k).start()
            local().start()

        def step_up(j):
            if j == last:
                local().wait()
            all_up(j).wait_recv()
            if j == 0:
                core_up(core).start()
            else:
                for k in peers(j - 1):
                    up(j - 1, k).start()

        def step_last():
            core_up(1 - core).wait_recv()

        def step_sent():
            all_sent(0).wait_send()
            all_sent(1).wait_send()

        steps = [step_core] + [functools.partial(step_down, j) for j in range(last + 1)] + [step_turn]
        return steps + [functools.partial(step_up, j) for j in range(last, -1, -1)] + [step_last, step_sent]

    def together(units):
        return [lambda steps=steps: [step() for step in steps] for steps in zip(*units)]

    wide_units = [sum_unit(a, asum.at[a], rec.at[a], wide_hbm.at[a], ORDERS[a]) for a in range(9)]
    groups = [together(wide_units[2 * i : 2 * i + 2]) for i in range(4)] + [wide_units[8]]
    for p in range(2):
        part_units = []
        for i in range(3):
            place = (pl.ds(512 * (i // 2), 512), pl.ds(256 * (i % 2), 256))
            part_units.append(
                sum_unit(
                    9 + 3 * p + i, act.at[p].at[place], act.at[2 + p].at[place], qkv_hbm.at[p, i],
                    ORDERS[9 + 3 * p + i],
                )
            )
        groups.append(together(part_units))

    def small_steps():
        mine, other = pl.ds(pl.multiple_of(16 * core, 16), 16), pl.ds(pl.multiple_of(16 - 16 * core, 16), 16)

        def copy(src, dst, i, peer):
            return remote(src, dst, s_sm.at[i], r_sm.at[i], peer)

        def core_send():
            return copy(small_s.at[0, other], small_c, 0, core_peer)

        def plane_send(k):
            return copy(small_s.at[1, mine], small_p.at[k - 1], 1, plane_peer(k))

        def z_send(k):
            return copy(small_s.at[2, mine], small_z.at[k - 1], 2, z_peer(k))

        def far_copy(k):
            return copy(small_s.at[3, mine], small_far.at[k - 1], 3 + k, far_peer(k))

        def core_up(rows):
            return copy(small_o.at[rows], small_o.at[rows], 3, core_peer)

        def step0():
            core_send().start()

        def step1():
            core_send().wait_recv()
            small_s[1, mine, :] = small_s[0, mine, :] + small_c[...]
            for k in range(1, 4):
                plane_send(k).start()

        def step2():
            total = small_s[1, mine, :]
            copy(small_p, small_p, 1, core_peer).wait_recv()
            for k in range(3):
                total = total + small_p[k]
            small_s[2, mine, :] = total
            for k in range(1, 4):
                z_send(k).start()

        def step3():
            total = small_s[2, mine, :]
            copy(small_z, small_z, 2, core_peer).wait_recv()
            for k in range(3):
                total = total + small_z[k]
            if extra > 1:
                small_s[3, mine, :] = total
                for k in range(1, extra):
                    far_copy(k).start()
                for k in range(1, extra):
                    far_copy(k).wait()
                    total = total + small_far[k - 1]
            small_o[mine, :] = total
            core_up(mine).start()

        def step4():
            core_up(other).wait_recv()
            small_out[...] = small_o[...]

        def step5():
            core_send().wait_send()
            core_up(mine).wait_send()
            copy(small_p, small_p, 1, core_peer).wait_send()
            copy(small_z, small_z, 2, core_peer).wait_send()

        return [step0, step1, step2, step3, step4, step5]

    groups.append(small_steps())

    def run(name):
        for at, j in SCHEDULE.get(name, ()):
            groups[at][j]()

    def run_in(prefix, i):
        for at in range(8):
            if SCHEDULE.get(f"{prefix}{at}"):

                @pl.when(i == at)
                def _(at=at):
                    run(f"{prefix}{at}")

    for c in range(4):
        asum[c] = tn(act[c], dout[...]).astype(BF)
        run(f"a{c}")

    for w in range(4):
        dmid[w] = flat(to_blocks(cr[w].astype(F32))).reshape(4, 64, 512)

    def dense_back(c, _):
        cols = pl.ds(pl.multiple_of(512 * c, 512), 512)
        dh = (nt(dout[...], wc[cols, :]) * dhid[c].astype(F32)).astype(BF)
        dhid[c] = dh
        acc_s[3 + c] = col_sum(dh.astype(F32))
        dmid[...] += nt(dh, we[:, cols]).reshape(4, 4, 64, 512)
        asum[4 + c] = tn(mlow[...], dh).astype(BF)
        run_in("d", c)
        return 0

    lax.fori_loop(0, 4, dense_back, 0)

    def norm_back(pair, _):
        z1, r1 = first_norm(pair)
        dm = dmid[pl.ds(2 * pair, 2)].reshape(512, 512)
        acc_s[7] += col_sum(dm * z1)
        acc_s[8] += col_sum(dm)
        dn1 = dm * g1[...][None, :]
        db = r1 * (
            dn1 - jnp.mean(dn1, axis=1, keepdims=True) - z1 * jnp.mean(dn1 * z1, axis=1, keepdims=True)
        )
        blk[pl.ds(2 * pair, 2)] = db.astype(BF).reshape(2, 4, 64, 512)
        return 0

    lax.fori_loop(0, 2, norm_back, 0)
    run("nb")

    bias[...] = jnp.zeros_like(bias)

    def gather(o, _):
        for bcol in range(2):
            for br in range(2):
                at = (bcol * 2 + br) * 64
                cr[o, at : at + 64, :] = blk[home(o, bcol, br)]
        return 0

    lax.fori_loop(0, 4, gather, 0)
    asum[8] = tn(mixed[...].reshape(1024, 512), cr[...].reshape(1024, 512)).astype(BF)
    run("gproj")
    head_ones_half = head_ones[0:128, 0:128]
    minus = jnp.full((256, 128), -1.0, BF)
    lane32 = lax.rem(lax.broadcasted_iota(jnp.int32, (256, 128), 1), 32)

    def retreat(it, _):
        p, o = it // 4, lax.rem(it, 4)
        half = pl.ds(pl.multiple_of(256 * p, 256), 256)
        dmx = nt(cr[o], wproj[half, :])
        rows = pl.ds(pl.multiple_of(o * TOK, TOK), TOK)
        scales = scale_lanes(p)
        for gi in range(2):
            g = 2 * p + gi
            lanes = pl.ds(pl.multiple_of(128 * g, 128), 128)
            qg, kg, vg = qs[o, g], kl[o, g], vl[o, g]
            dmg = dmx[:, 128 * gi : 128 * gi + 128] * isum[o, g]
            dmp = dmg.astype(BF)
            mix = mixed[o, :, lanes].astype(F32) + mixlo[o, :, lanes].astype(F32)
            prod = dmp.astype(F32) * mix
            delta = sum(nn(p, head_ones_half) for p in split3(prod)[:2])
            delta_hi, delta_lo, _ = split3(delta)
            prod = jnp.where(lane32 == 0, delta_hi, jnp.where(lane32 == 1, delta_lo, jnp.zeros_like(delta_lo)))
            vw = jnp.concatenate([vg, minus], axis=1)
            dmp4 = jnp.concatenate([dmp * mask for mask in head_mask], axis=0)
            left = jnp.concatenate([dmp4, jnp.concatenate([prod * mask for mask in head_mask], axis=0)], axis=1)
            e4 = ex[o, g].reshape(1024, 256)
            dsf = nt(left, vw) * e4.astype(F32)
            ds = dsf.astype(BF)
            for hh in range(4):
                h, n = 4 * g + hh, 256 * hh
                bias[h, 1] += dsf[n : n + 128, 0:128] + dsf[n + 128 : n + 256, 128:256]
                bias[h, 0] += dsf[n : n + 128, 128:256]
                bias[h, 2] += dsf[n + 128 : n + 256, 0:128]
            dq = nn(
                jnp.concatenate([ds[256 * hh : 256 * hh + 256] for hh in range(4)], axis=1),
                jnp.concatenate([kg * mask for mask in head_mask], axis=0),
            )
            dk = tn(ds, jnp.concatenate([qg * mask for mask in head_mask], axis=0))
            dv = tn(e4, dmp4)
            qf, kf = qg.astype(F32), kg.astype(F32)
            scale = scales[:, 128 * gi : 128 * gi + 128]
            tq = dq * qf
            acc_s[9, :, lanes] += col_sum(tq)
            aq = nn(tq.astype(BF), head_ones_half)
            ak = nn((dk * kf).astype(BF), head_ones_half)
            dhid[0, rows, lanes] = (qinv[o, g].astype(F32) * (scale * dq - (1.0 / scale) * qf * aq)).astype(BF)
            dhid[1, rows, lanes] = (kinv[o, g].astype(F32) * (dk - kf * ak)).astype(BF)
            dhid[2, rows, lanes] = dv.astype(BF)
        run_in("r", it)

        @pl.when(lax.rem(it, 4) == 3)
        def _():
            moved = sum(
                nt(dhid[i, :, half], wqkv[:, pl.ds(pl.multiple_of(512 * i + 256 * p, 256), 256)])
                for i in range(3)
            )
            for w in range(4):
                for bcol in range(2):
                    for br in range(2):
                        at = 256 * w + (bcol * 2 + br) * 64
                        dmid[home(w, bcol, br)] += moved[at : at + 64, :]
            xflat = xroll[...].reshape(1024, 512)
            for i in range(3):
                grad = tn(xflat, dhid[i, :, half]).astype(BF)
                act[p, 512 * (i // 2) : 512 * (i // 2) + 512, 256 * (i % 2) : 256 * (i % 2) + 256] = grad

        run_in("gq", jnp.where(lax.rem(it, 4) == 3, p, -1))
        return 0

    lax.fori_loop(0, 8, retreat, 0)

    def gin_copy(w):
        return remote(slope.at[w], gin_hbm.at[me, 0], s_gin.at[w], r_gin.at[me], (img, w))

    def finish(w, _):
        quads = [[dmid[w, 2 * qr + qc] for qc in range(2)] for qr in range(2)]
        slope[w] = from_blocks(quads).astype(BF)

        @pl.when(w != me)
        def _():
            gin_copy(w).start()

        return 0

    lax.fori_loop(0, 4, finish, 0)
    own_gin = pltpu.make_async_copy(slope.at[me], gin_hbm.at[me, 0], r_gin.at[me])
    own_gin.start()
    run("finish")

    row_ones = jnp.ones((8, 1024), BF)

    def put(row, v):
        small_s[0, row : row + v.shape[0], :] = v

    put(ROW_QB, nn(row_ones, dhid[0])[0:1])
    put(ROW_VB, nn(row_ones, dhid[2])[0:1])
    put(ROW_BP, nn(row_ones, cr[...].reshape(1024, 512))[0:1])
    for row, i in ((ROW_LS, 9), (ROW_G1, 7), (ROW_S1, 8), (ROW_B2, 2), (ROW_G2, 0), (ROW_S2, 1)):
        put(row, jnp.sum(acc_s[i], axis=0, keepdims=True))
    for c in range(4):
        put(ROW_BE + c, jnp.sum(acc_s[3 + c], axis=0, keepdims=True))
    run("puts")
    short = jnp.zeros((384, 256), F32)
    for c in range(4):
        places = one_hot_places(c)
        left = jnp.concatenate(
            [bias[:, :, 8 * r : 8 * r + 8, :].reshape(384, 128) for r in range(4 * c, 4 * c + 4)], axis=1
        )
        for p in split3(left)[:2]:
            short = short + nt(p, places)
    pick = one_hot_pick()
    for i in range(4):
        piece = split3(short[96 * i : 96 * i + 96])[:2]
        part[4 * i : 4 * i + 4] = sum(nt(p, pick) for p in piece).reshape(4, 24, 1024)
    run("bb")
    dtab = jnp.zeros((16, 1024), F32)
    for u in range(24):
        dtab = dtab + pltpu.roll(part[:, u, :], 23 - u, 1)
    tab[...] = dtab * tab[...] * (1.0 - tab[...] * (1.0 / BIAS_RANGE))
    small_s[0, ROW_W1 : ROW_W2 + 16, :] = jnp.zeros((ROW_W2 + 16 - ROW_W1, 512), F32)

    def net_back(c, _):
        cols, pre = net_piece(c)
        cap, low = gelu_parts(pre)
        dlog, dlog_lo, _ = split3(tab[:, cols])
        units, units_lo, _ = split3(pre * cap)
        small_s[0, ROW_W2 : ROW_W2 + 16, :] += nn(dlog, units) + nn(dlog_lo, units) + nn(dlog, units_lo)
        w_hi, w_lo, _ = split3(w2t[...])
        back = tn(dlog, w_hi) + tn(dlog_lo, w_hi) + tn(dlog, w_lo)
        dpre, dpre_lo, _ = split3(back * (cap + pre * low))
        hi, mid, _ = split3(crow[:, cols])
        net = nn(hi, dpre) + nn(mid, dpre) + nn(hi, dpre_lo)
        small_s[0, ROW_W1 : ROW_W1 + 3, :] += net[0:3]
        return 0

    lax.fori_loop(0, 4, net_back, 0)
    run("net")
    for k in (1, 2, 3):
        frm = ring_from(k)
        x_send(k, 0).wait_send()
        x_send(k, 1).wait_send()
        spread(cot_hbm, cr, s_c, r_c, k).wait_send()
        res_copy(lax.rem(me + k, n_win)).wait_send()
        remote(xr.at[frm], res_hbm.at[frm, 0], s_res.at[frm], r_res.at[frm], (img, frm)).wait_recv()
    own_res.wait()
    own_gin.wait()
    last = {at: j for at, j in SCHEDULE["end"]}
    late = [at for at, group in enumerate(groups) if last.get(at) == len(group) - 2]
    for at, group in enumerate(groups):
        if at not in late:
            group[-1]()
    for at, j in SCHEDULE["end"]:
        groups[at][j]()
        if at in late and j == len(groups[at]) - 2:
            groups[at][-1]()

    for k in (1, 2, 3):
        frm, to = ring_from(k), lax.rem(me + k, n_win)
        gin_copy(to).wait_send()
        remote(slope.at[frm], gin_hbm.at[frm, 0], s_gin.at[frm], r_gin.at[frm], (img, frm)).wait_recv()


def widen_kernel(
    res, gin, wide, qkv, small,
    res_out, gin_out, w_qkv, g_qb, g_vb, g_ls, g_w1, g_b1, g_w2, w_proj, g_bp, g_g1, g_s1, w_fc1, g_be,
    w_fc2, g_b2, g_g2, g_s2,
    blocks, wide_in, qkv_in, wide_f, qkv_f, s_in, s_out, s_blocks,
):
    taken = [pltpu.make_async_copy(a, blocks.at[i], s_blocks.at[i]) for i, a in enumerate((res, gin))]
    passed = [pltpu.make_async_copy(blocks.at[i], a, s_blocks.at[2 + i]) for i, a in enumerate((res_out, gin_out))]
    pieces = []
    for i in range(9):
        if i < 4:
            place = w_fc2.at[pl.ds(512 * i, 512), :]
        elif i < 8:
            place = w_fc1.at[:, pl.ds(512 * (i - 4), 512)]
        else:
            place = w_proj
        pieces.append((wide.at[i], wide_in.at[i], wide_f.at[i], place))
    for i in range(6):
        place = w_qkv.at[:, pl.ds(512 * (i % 3) + 256 * (i // 3), 256)]
        pieces.append((qkv.at[i // 3, i % 3], qkv_in.at[i], qkv_f.at[i], place))
    loads = [pltpu.make_async_copy(a, b, s_in.at[i]) for i, (a, b, _, _) in enumerate(pieces)]
    stores = [pltpu.make_async_copy(c, d, s_out.at[i]) for i, (_, _, c, d) in enumerate(pieces)]
    for c in loads:
        c.start()
    for c in taken:
        c.start()
    for i, (_, b, c, _) in enumerate(pieces):
        loads[i].wait()
        c[...] = b[...].astype(F32)
        stores[i].start()
    for a, b in zip(taken, passed):
        a.wait()
        b.start()
    for row, out in (
        (ROW_QB, g_qb), (ROW_VB, g_vb), (ROW_B1, g_b1), (ROW_BP, g_bp), (ROW_G1, g_g1), (ROW_S1, g_s1),
        (ROW_B2, g_b2), (ROW_G2, g_g2), (ROW_S2, g_s2),
    ):
        out[...] = small[row, :]
    for c in range(4):
        g_be[512 * c : 512 * c + 512] = small[ROW_BE + c, :]
    g_w1[...] = small[ROW_W1 : ROW_W1 + 2, :]
    g_w2[...] = small[ROW_W2 : ROW_W2 + 16, :]
    h0 = lax.broadcasted_iota(jnp.int32, (512, 16), 0) // 32
    h1 = lax.broadcasted_iota(jnp.int32, (512, 16), 1)
    heads = jnp.where(h0 == h1, 1.0, 0.0).astype(BF)
    per_head = sum(nn(jnp.broadcast_to(p, (8, 512)), heads) for p in split3(small[ROW_LS : ROW_LS + 1, :]))
    g_ls[...] = per_head[0, :]
    for c in passed + stores:
        c.wait()


def body(n_img, n_win, inputs, wqkv, qb, vb, hls, w1, b1, w2, wproj, bproj, g1, s1, we, be, wc, bc, g2, s2, cot):
    extra = n_img // 8
    crow = table_coords()
    dma = pltpu.SemaphoreType.DMA
    n_sm = 4 + (extra - 1)
    vmem = pl.BlockSpec(memory_space=pltpu.VMEM)
    hbm = pl.BlockSpec(memory_space=pl.ANY)
    smem = pl.BlockSpec(memory_space=pltpu.SMEM)
    scratch = [
        pltpu.VMEM((4, TOK, 512), BF),
        pltpu.VMEM((4, TOK, 512), BF),
        pltpu.VMEM((4, TOK, 512), BF),
        pltpu.VMEM((16, 3, 128, 128), F32),
        pltpu.VMEM((4, 4, 4, TOK, TOK), BF),
        pltpu.VMEM((4, 4, TOK, 128), BF),
        pltpu.VMEM((4, 4, TOK, 128), BF),
        pltpu.VMEM((4, 4, TOK, 128), BF),
        pltpu.VMEM((4, 4, TOK, 128), BF),
        pltpu.VMEM((4, 4, TOK, 128), BF),
        pltpu.VMEM((4, 4, TOK, 128), F32),
        pltpu.VMEM((4, TOK, 512), BF),
        pltpu.VMEM((4, TOK, 512), BF),
        pltpu.VMEM((4, 4, 64, 512), BF),
        pltpu.VMEM((4, 4, 64, 512), F32),
        pltpu.VMEM((4, 1024, 512), BF),
        pltpu.VMEM((4, 1024, 512), BF),
        pltpu.VMEM((1024, 512), BF),
        pltpu.VMEM((1024, 512), BF),
        pltpu.VMEM((4, TOK, 512), BF),
        pltpu.VMEM((16, 1024), F32),
        pltpu.VMEM((16, 24, 1024), F32),
        pltpu.VMEM((10, 8, 512), F32),
        pltpu.VMEM((9, 512, 512), BF),
        pltpu.VMEM((9, 496, 512), BF),
        pltpu.VMEM((15, extra - 1, 16, 512) if extra > 1 else (1, 1, 16, 512), BF),
        pltpu.VMEM((512, 1536), BF),
        pltpu.VMEM((512, 512), BF),
        pltpu.VMEM((512, 2048), BF),
        pltpu.VMEM((2048, 512), BF),
        pltpu.VMEM((512,), F32), pltpu.VMEM((512,), F32),
        pltpu.VMEM((2, 512), F32), pltpu.VMEM((512,), F32), pltpu.VMEM((16, 512), F32),
        pltpu.VMEM((512,), F32), pltpu.VMEM((512,), F32), pltpu.VMEM((512,), F32),
        pltpu.VMEM((2048,), F32), pltpu.VMEM((512,), F32),
        pltpu.VMEM((512,), F32), pltpu.VMEM((512,), F32), pltpu.VMEM((8, 1024), F32),
        pltpu.VMEM((4, SMALL_ROWS, 512), F32),
        pltpu.VMEM((16, 512), F32),
        pltpu.VMEM((3, 16, 512), F32),
        pltpu.VMEM((3, 16, 512), F32),
        pltpu.VMEM((max(extra - 1, 1), 16, 512), F32),
        pltpu.VMEM((SMALL_ROWS, 512), F32),
        dma((2, 4)), dma((2, 4)), dma((4,)), dma((4,)),
        dma((4,)), dma((4,)), dma((4,)), dma((4,)),
        dma((15, 1 + extra)), dma((15, 9 + extra)), dma((15,)),
        dma((n_sm,)), dma((n_sm,)),
        dma((4,)), dma((13,)),
    ]
    block = jax.ShapeDtypeStruct(inputs.shape, BF)
    result, grad_inputs, wide, qkv, small = pl.pallas_call(
        functools.partial(block_kernel, n_img, n_win),
        out_shape=(
            block,
            block,
            jax.ShapeDtypeStruct((9, 512, 512), BF),
            jax.ShapeDtypeStruct((2, 3, 512, 256), BF),
            jax.ShapeDtypeStruct((SMALL_ROWS, 512), F32),
        ),
        in_specs=[hbm] * 6 + [smem] + [hbm] * 13,
        out_specs=(hbm, hbm, hbm, hbm, vmem),
        scratch_shapes=scratch,
        compiler_params=pltpu.CompilerParams(
            collective_id=0, has_side_effects=True, vmem_limit_bytes=64 * 1024 * 1024
        ),
    )(
        inputs, cot, wqkv, wproj, we, wc, hls, qb, vb, w1, b1, w2.T, bproj, g1, s1, be, bc, g2, s2,
        jnp.asarray(crow),
    )
    any_ = lambda shape: jax.ShapeDtypeStruct(shape, F32)
    outs = pl.pallas_call(
        widen_kernel,
        out_shape=(
            block, block, any_((512, 1536)), any_((512,)), any_((512,)), any_((16,)), any_((2, 512)),
            any_((512,)), any_((16, 512)), any_((512, 512)), any_((512,)), any_((512,)), any_((512,)),
            any_((512, 2048)), any_((2048,)), any_((2048, 512)), any_((512,)), any_((512,)), any_((512,)),
        ),
        in_specs=[hbm] * 4 + [vmem],
        out_specs=tuple(hbm if i in (0, 1, 2, 9, 13, 15) else vmem for i in range(19)),
        scratch_shapes=[
            pltpu.VMEM((2,) + inputs.shape, BF),
            pltpu.VMEM((9, 512, 512), BF),
            pltpu.VMEM((6, 512, 256), BF),
            pltpu.VMEM((9, 512, 512), F32),
            pltpu.VMEM((6, 512, 256), F32),
            dma((15,)), dma((15,)), dma((4,)),
        ],
        compiler_params=pltpu.CompilerParams(vmem_limit_bytes=63 * 1024 * 1024),
    )(result, grad_inputs, wide, qkv, small)
    return outs[:8] + (outs[8].T,) + outs[9:]


def solution(mesh):
    n_img, n_win = mesh.shape["img"], mesh.shape["win"]
    block = P("img", "win", None, None)
    return jax.shard_map(
        functools.partial(body, n_img, n_win),
        mesh=mesh,
        in_specs=(block,) + (P(),) * 17 + (block,),
        out_specs=(block, block) + (P(),) * 17,
        check_vma=False,
    )
```

```python
import functools

import jax
import jax.numpy as jnp
import numpy as np
from jax import lax
from jax.experimental import pallas as pl
from jax.experimental.pallas import tpu as pltpu
from jax.sharding import PartitionSpec as P

WIN = 16
TOK = WIN * WIN
EPS_DIR = 1e-06
EPS_NORM = 1e-05
MASK_FILL = -100.0
BIAS_RANGE = 16.0
INV_ROOT_TWO = 0.7071067811865476
INV_ROOT_TWOPI = 0.3989422804014327
LOG2_E = 1.4426950408889634
MESH = pl.DeviceIdType.MESH
BF = jnp.bfloat16
F32 = jnp.float32

(ROW_QB, ROW_VB, ROW_LS, ROW_W1, ROW_B1, ROW_W2, ROW_BP, ROW_G1, ROW_S1, ROW_B2, ROW_G2, ROW_S2,
 ROW_BE, SMALL_ROWS) = (0, 1, 2, 3, 5, 6, 22, 23, 24, 25, 26, 27, 28, 32)

SCHEDULE = {
    "a1": ((0, 0),),
    "a3": ((1, 0), (0, 1)),
    "d0": ((1, 1),),
    "d1": ((2, 0), (0, 2)),
    "d2": ((2, 1), (1, 2)),
    "d3": ((3, 0),),
    "nb": ((0, 3), (3, 1)),
    "gproj": ((4, 0), (2, 2)),
    "r0": ((4, 1), (1, 3), (3, 2)),
    "r1": ((0, 4),),
    "r2": ((2, 3), (4, 2), (1, 4)),
    "r3": ((3, 3), (0, 5), (2, 4)),
    "gq0": ((5, 0), (4, 3)),
    "r4": ((5, 1), (3, 4), (2, 5), (0, 6)),
    "r5": ((4, 4),),
    "r6": ((1, 5), (5, 2), (3, 5)),
    "r7": ((2, 6), (0, 7)),
    "gq1": ((6, 0), (4, 5), (1, 6), (5, 3), (0, 8), (3, 6), (6, 1), (2, 7)),
    "finish": ((4, 6),),
    "puts": ((1, 7), (5, 4)),
    "bb": ((3, 7), (6, 2), (2, 8)),
    "net": ((7, 0), (1, 8), (5, 5), (7, 1), (3, 8)),
    "end": (
        (6, 3), (2, 9), (2, 10), (1, 9), (5, 6), (7, 2), (1, 10), (6, 4), (3, 9), (5, 7), (3, 10), (5, 8), (7, 3),
        (6, 5), (7, 4), (6, 6),
    ),
}
ORDERS = (
    "wpv", "xyz", "wvxy", "xwyv", "wvxy", "xwyv", "xwvy", "yxwv", "pz",
    "pwv", "wpv", "wpv", "pz", "pz", "pz",
)


def nn(a, b):
    return lax.dot_general(a, b, (((1,), (0,)), ((), ())), preferred_element_type=F32)


def nt(a, b):
    return lax.dot_general(a, b, (((1,), (1,)), ((), ())), preferred_element_type=F32)


def tn(a, b):
    return lax.dot_general(a, b, (((0,), (0,)), ((), ())), preferred_element_type=F32)


def split3(v):
    hi = v.astype(BF)
    rest = v - hi.astype(F32)
    mid = rest.astype(BF)
    return hi, mid, (rest - mid.astype(F32)).astype(BF)


def gelu_parts(v):
    cap = 0.5 + 0.5 * lax.erf(v * INV_ROOT_TWO)
    return cap, INV_ROOT_TWOPI * jnp.exp2(v * v * (-0.5 * LOG2_E))


def col_sum(v):
    return jnp.sum(v.reshape(v.shape[0] // 8, 8, v.shape[1]), axis=0)


def to_blocks(v):
    n = v.shape[-1]
    t = v.reshape(2, 8, 2, 8, n)
    return [[t[qr, :, qc].reshape(64, n) for qc in range(2)] for qr in range(2)]


def from_blocks(quads):
    n = quads[0][0].shape[-1]
    rows = []
    for qr in range(2):
        a = quads[qr][0].reshape(8, 1, 8, n)
        b = quads[qr][1].reshape(8, 1, 8, n)
        rows.append(jnp.concatenate([a, b], axis=1).reshape(128, n))
    return jnp.concatenate(rows, axis=0)


def one_hot_places(c):
    l = lax.broadcasted_iota(jnp.int32, (256, 512), 0)
    k = lax.broadcasted_iota(jnp.int32, (256, 512), 1) + 512 * c
    return jnp.where(l == 8 * (15 - k // 128) + k % 128, 1.0, 0.0).astype(BF)


def one_hot_pick():
    k = lax.broadcasted_iota(jnp.int32, (1024, 256), 0)
    l = lax.broadcasted_iota(jnp.int32, (1024, 256), 1)
    return jnp.where(k == 32 * (l // 8) + l % 8, 1.0, 0.0).astype(BF)


def table_coords():
    k = np.arange(1024)
    out = np.zeros((2, 1024), np.float64)
    for i, off in enumerate((15 - k // 32, 15 - k % 32)):
        u = off * (8.0 / 15.0)
        out[i] = np.sign(u) * np.log2(np.abs(u) + 1.0) / 3.0
    rows = np.zeros((8, 1024), np.float32)
    rows[0:2] = out
    rows[2] = 1.0
    return rows


def net_first(cols, w1, b1):
    return cols[:, 0:1] * w1[0:1, :] + cols[:, 1:2] * w1[1:2, :] + b1


def block_kernel(
    n_img, n_win,
    x_hbm, cot_hbm, wqkv_hbm, wproj_hbm, we_hbm, wc_hbm, hls, qb_hbm, vb_hbm, w1_hbm, b1_hbm,
    w2t_hbm, bproj_hbm, g1_hbm, s1_hbm, be_hbm, bc_hbm, g2_hbm, s2_hbm, crow_hbm,
    res_hbm, gin_hbm, wide_hbm, qkv_hbm, small_out,
    xr, cr, xroll, bias, ex, qs, kl, vl, qinv, kinv, isum, mixed, mixlo, blk, dmid, act, dhid, dout,
    mlow, slope, tab, part, acc_s, asum, rec, far, wqkv, wproj, we, wc,
    qb, vb, w1, b1, w2t, bproj, g1, s1, be, bc, g2, s2, crow,
    small_s, small_c, small_p, small_z, small_far, small_o,
    s_x, r_x, s_c, r_c, s_res, r_res, s_gin, r_gin, s_ar, r_ar, l_ar, s_sm, r_sm, s_w, s_v,
):
    img = lax.axis_index("img")
    me = lax.axis_index("win")
    extra = n_img // 8
    core = lax.rem(me, 2)
    ypos = me // 2
    xpos = lax.rem(img, 2)
    zpos = lax.rem(img // 2, 4)
    upper = img // 8

    def ring_to(k):
        return (img, lax.rem(me + k, n_win))

    def ring_from(k):
        return lax.rem(me + n_win - k, n_win)

    core_peer = (img, me + 1 - 2 * core)
    y_peer = (img, lax.rem(me + 2, 4))
    x_peer = (img + 1 - 2 * xpos, me)
    plane_pos = 2 * xpos + ypos

    def z_peer(k):
        return (upper * 8 + lax.rem(zpos + k, 4) * 2 + xpos, me)

    def plane_peer(k):
        to = lax.rem(plane_pos + k, 4)
        return (img + to // 2 - xpos, lax.rem(to, 2) * 2 + core)

    def far_peer(k):
        return (lax.rem(upper + k, extra) * 8 + zpos * 2 + xpos, me)

    weights = [
        pltpu.make_async_copy(a, b, s_w.at[i])
        for i, (a, b) in enumerate(((wqkv_hbm, wqkv), (wproj_hbm, wproj), (we_hbm, we), (wc_hbm, wc)))
    ]

    own_x = pltpu.make_async_copy(x_hbm.at[me, 0], xr.at[me], r_x.at[0, 0])
    own_c = pltpu.make_async_copy(cot_hbm.at[me, 0], cr.at[me], r_c.at[0])
    vectors = [
        pltpu.make_async_copy(a, b, s_v.at[i])
        for i, (a, b) in enumerate(
            (
                (w1_hbm, w1), (b1_hbm, b1), (w2t_hbm, w2t), (crow_hbm, crow), (qb_hbm, qb), (vb_hbm, vb),
                (bproj_hbm, bproj), (g1_hbm, g1), (s1_hbm, s1), (be_hbm, be), (bc_hbm, bc), (g2_hbm, g2),
                (s2_hbm, s2),
            )
        )
    ]
    for c in vectors + [own_x] + weights + [own_c]:
        c.start()

    barrier = pltpu.get_barrier_semaphore()
    others = [ring_to(k) for k in range(1, n_win)] + [x_peer, (img + 1 - 2 * xpos, lax.rem(me + 2, 4))]
    others += [z_peer(k) for k in range(1, 4)] + [far_peer(k) for k in range(1, extra)]
    for peer in others:
        pl.semaphore_signal(barrier, inc=1, device_id=peer, device_id_type=MESH)
    pl.semaphore_wait(barrier, len(others))

    def remote(src, dst, ssem, rsem, peer):
        return pltpu.make_async_remote_copy(
            src_ref=src, dst_ref=dst, send_sem=ssem, recv_sem=rsem, device_id=peer, device_id_type=MESH
        )

    def spread(src_hbm, dst, ssem, rsem, k):
        to = lax.rem(me + k, n_win)
        return remote(src_hbm.at[to, 0], dst.at[me], ssem.at[k], rsem.at[k], ring_to(k))

    def spread_in(src_hbm, dst, ssem, rsem, k):
        frm = ring_from(k)
        return remote(src_hbm.at[frm, 0], dst.at[frm], ssem.at[k], rsem.at[k], ring_to(k))

    def half_rows(w, half):
        return pl.ds(pl.multiple_of(128 * (1 - w // 2 if half == 0 else w // 2), 128), 128)

    def x_send(k, half):
        to, rows = lax.rem(me + k, n_win), half_rows(me, half)
        return remote(
            x_hbm.at[to, 0, rows], xr.at[me, rows], s_x.at[half, k], r_x.at[half, k], ring_to(k)
        )

    def x_arrival(k, half):
        frm = ring_from(k)
        rows = half_rows(frm, half)
        return remote(x_hbm.at[frm, 0, rows], xr.at[frm, rows], s_x.at[half, k], r_x.at[half, k], ring_to(k))

    for half in range(2):
        for k in (2, 1, 3):
            x_send(k, half).start()
    for k in (2, 1, 3):
        spread(cot_hbm, cr, s_c, r_c, k).start()

    for c in vectors:
        c.wait()
    def net_piece(c):
        rows = pl.ds(pl.multiple_of(256 * c, 256), 256)
        return rows, net_first(crow[:, rows].T, w1[...], b1[...][None, :])

    def look_up(c, _):
        cols, pre = net_piece(c)
        logits = lax.dot_general(
            w2t[...], pre * gelu_parts(pre)[0], (((1,), (1,)), ((), ())),
            precision=lax.Precision.HIGHEST, preferred_element_type=F32,
        )
        tab[:, cols] = BIAS_RANGE / (1.0 + jnp.exp(-logits))
        return 0

    lax.fori_loop(0, 4, look_up, 0)
    for u in range(24):
        part[:, u, :] = pltpu.roll(tab[...], 1001 + u, 1)
    pick = one_hot_pick()
    short = jnp.concatenate(
        [sum(nn(p, pick) for p in split3(part[4 * i : 4 * i + 4].reshape(96, 1024))) for i in range(4)], axis=0
    )
    short_parts = split3(short)
    for c in range(4):
        places = one_hot_places(c)
        wide = sum(nn(p, places) for p in short_parts)
        for r in range(4):
            row = 8 * (4 * c + r)
            bias[:, :, row : row + 8, :] = wide[:, 128 * r : 128 * r + 128].reshape(16, 3, 8, 128)

    lane = lax.broadcasted_iota(jnp.int32, (1, 128), 1)
    head_mask = [jnp.where(lane // 32 == hh, 1.0, 0.0).astype(BF) for hh in range(4)]
    l0 = lax.broadcasted_iota(jnp.int32, (256, 256), 0)
    l1 = lax.broadcasted_iota(jnp.int32, (256, 256), 1)
    head_ones = jnp.where(l0 // 32 == l1 // 32, 1.0, 0.0).astype(BF)

    def scale_lanes(p):
        wide = lax.broadcasted_iota(jnp.int32, (1, 256), 1) // 32
        out = jnp.zeros((1, 256), F32)
        for i in range(8):
            out = jnp.where(wide == i, hls[8 * p + i], out)
        return jnp.exp(out)

    def lay(half):
        def one(w, _):
            late = w // 2 if half == 0 else 1 - w // 2
            rows = pl.ds(pl.multiple_of(128 * (1 - late), 128), 128)
            v = xr[w, rows, :].astype(F32).reshape(8, 2, 8, 512)
            for qc in range(2):
                bcol = 1 - qc
                ocol = lax.rem(w, 2) if bcol == 0 else 1 - lax.rem(w, 2)
                at = pl.ds(pl.multiple_of((bcol * 2 + late) * 64, 64), 64)
                xroll[2 * half + ocol, at, :] = v[:, qc].reshape(64, 512).astype(BF)
            return 0

        lax.fori_loop(0, 4, one, 0)

    def project(half):
        xw = xroll[2 * half : 2 * half + 2].reshape(512, 512)

        def one(p, _):
            def cols(i):
                return pl.ds(pl.multiple_of(512 * i + 256 * p, 256), 256)

            q = nn(xw, wqkv[:, cols(0)]) + qb[cols(0)][None, :]
            qi = lax.rsqrt(nn((q * q).astype(BF), head_ones) + EPS_DIR)
            qsc = (q * qi * scale_lanes(p)).astype(BF)
            k = nn(xw, wqkv[:, cols(1)])
            ki = lax.rsqrt(nn((k * k).astype(BF), head_ones) + EPS_DIR)
            kn = (k * ki).astype(BF)
            v = (nn(xw, wqkv[:, cols(2)]) + vb[cols(0)][None, :]).astype(BF)
            for w in range(2):
                rows = slice(256 * w, 256 * w + 256)
                for i in range(2):
                    lanes = slice(128 * i, 128 * i + 128)
                    at = (2 * half + w, 2 * p + i)
                    qs[at] = qsc[rows, lanes]
                    kl[at] = kn[rows, lanes]
                    vl[at] = v[rows, lanes]
                    qinv[at] = qi[rows, lanes].astype(BF)
                    kinv[at] = ki[rows, lanes].astype(BF)
            return 0

        lax.fori_loop(0, 2, one, 0)

    own_x.wait()
    for k in (1, 2, 3):
        x_arrival(k, 0).wait_recv()
    lay(0)
    weights[0].wait()
    project(0)
    weights[1].wait()

    row_half = lax.broadcasted_iota(jnp.int32, (128, 128), 0) // 64
    col_half = lax.broadcasted_iota(jnp.int32, (128, 128), 1) // 64
    apart = jnp.where(row_half == col_half, 0.0, MASK_FILL)

    def home(o, bcol, br):
        row, col = lax.rem(2 * (o // 2) + br + 1, 4), lax.rem(2 * lax.rem(o, 2) + bcol + 1, 4)
        return 2 * (row // 2) + col // 2, 2 * lax.rem(row, 2) + lax.rem(col, 2)

    def attend(o, _):
        @pl.when(o == 2)
        def _():
            for k in (1, 2, 3):
                x_arrival(k, 1).wait_recv()
            lay(1)
            project(1)

        rows_cut = jnp.where(o // 2 == 1, apart, 0.0)
        cols_cut = jnp.where(lax.rem(o, 2) == 1, jnp.full((128, 128), MASK_FILL, F32), rows_cut)

        for g in range(4):
            qg, kg, vg = qs[o, g], kl[o, g], vl[o, g]
            sc = nt(jnp.concatenate([qg * mask for mask in head_mask], axis=0), kg)
            for hh in range(4):
                h, n = 4 * g + hh, 256 * hh
                ex[o, g, hh, 0:128, 0:128] = jnp.exp(sc[n : n + 128, 0:128] + bias[h, 1] + rows_cut).astype(BF)
                ex[o, g, hh, 0:128, 128:256] = jnp.exp(sc[n : n + 128, 128:256] + bias[h, 0] + cols_cut).astype(BF)
                ex[o, g, hh, 128:256, 0:128] = jnp.exp(sc[n + 128 : n + 256, 0:128] + bias[h, 2] + cols_cut).astype(BF)
                ex[o, g, hh, 128:256, 128:256] = jnp.exp(
                    sc[n + 128 : n + 256, 128:256] + bias[h, 1] + rows_cut
                ).astype(BF)
            ones = [jnp.broadcast_to(mask, (256, 128)) for mask in head_mask]
            total = nn(
                jnp.concatenate([ex[o, g, hh] for hh in range(4)], axis=1),
                jnp.concatenate(
                    [jnp.concatenate([vg * mask, one], axis=1) for mask, one in zip(head_mask, ones)], axis=0
                ),
            )
            inv = 1.0 / total[:, 128:256]
            isum[o, g] = inv
            mix = total[:, 0:128] * inv
            mix_hi = mix.astype(BF)
            mixed[o, :, 128 * g : 128 * g + 128] = mix_hi
            mixlo[o, :, 128 * g : 128 * g + 128] = (mix - mix_hi.astype(F32)).astype(BF)

        branch = (nn(mixed[o], wproj[...]) + bproj[...][None, :]).astype(BF)
        for bcol in range(2):
            for br in range(2):
                at = (bcol * 2 + br) * 64
                blk[home(o, bcol, br)] = branch[at : at + 64, :]
        return 0

    lax.fori_loop(0, 4, attend, 0)

    weights[2].wait()
    weights[3].wait()
    acc_s[...] = jnp.zeros_like(acc_s)

    def res_copy(w):
        return remote(xr.at[w], res_hbm.at[me, 0], s_res.at[w], r_res.at[me], (img, w))

    def flat(quads):
        return jnp.concatenate([quads[0][0], quads[0][1], quads[1][0], quads[1][1]], axis=0)

    def first_norm(pair):
        back = blk[pl.ds(2 * pair, 2)].reshape(512, 512).astype(F32)
        ctr = back - jnp.mean(back, axis=1, keepdims=True)
        r1 = lax.rsqrt(jnp.mean(ctr * ctr, axis=1, keepdims=True) + EPS_NORM)
        return ctr * r1, r1

    def laid(ref, pair):
        return jnp.concatenate([flat(to_blocks(ref[2 * pair + i].astype(F32))) for i in range(2)], axis=0)

    def dense(turn, _):
        pair = lax.rem(ypos + turn, 2)
        z1, _ = first_norm(pair)
        middle = laid(xr, pair) + z1 * g1[...][None, :] + s1[...][None, :]
        ml = middle.astype(BF)
        rows = pl.ds(pl.multiple_of(pair * 512, 512), 512)
        mlow[rows, :] = ml
        out = jnp.zeros((512, 512), F32)
        for c in range(8):
            cols = slice(256 * c, 256 * c + 256)
            part_cols = slice(256 * (c % 2), 256 * (c % 2) + 256)
            hid = nn(ml, we[:, cols]) + be[cols][None, :]
            cap, low = gelu_parts(hid)
            a = (hid * cap).astype(BF)
            act[c // 2, rows, part_cols] = a
            dhid[c // 2, rows, part_cols] = (cap + hid * low).astype(BF)
            out = out + nn(a, wc[cols, :])
        out = out + bc[...][None, :]
        ctr2 = out - jnp.mean(out, axis=1, keepdims=True)
        r2 = lax.rsqrt(jnp.mean(ctr2 * ctr2, axis=1, keepdims=True) + EPS_NORM)
        z2 = ctr2 * r2
        result = middle + z2 * g2[...][None, :] + s2[...][None, :]
        for i in range(2):
            quads = [[result[256 * i + 64 * (2 * qr + qc) :][:64] for qc in range(2)] for qr in range(2)]
            w = 2 * pair + i
            xr[w] = from_blocks(quads).astype(BF)

            @pl.when(w != me)
            def _(w=w):
                res_copy(w).start()

        @pl.when(turn == 0)
        def _():
            own_c.wait()
            spread_in(cot_hbm, cr, s_c, r_c, 3 - 2 * core).wait_recv()

        @pl.when(turn == 1)
        def _():
            spread_in(cot_hbm, cr, s_c, r_c, 2).wait_recv()
            spread_in(cot_hbm, cr, s_c, r_c, 1 + 2 * core).wait_recv()

        e = laid(cr, pair)
        acc_s[0] += col_sum(e * z2)
        acc_s[1] += col_sum(e)
        dn = e * g2[...][None, :]
        dv = r2 * (
            dn - jnp.mean(dn, axis=1, keepdims=True) - z2 * jnp.mean(dn * z2, axis=1, keepdims=True)
        )
        do = dv.astype(BF)
        dout[rows, :] = do
        acc_s[2] += col_sum(do.astype(F32))
        return 0

    lax.fori_loop(0, 2, dense, 0)
    own_res = pltpu.make_async_copy(xr.at[me], res_hbm.at[me, 0], r_res.at[me])
    own_res.start()

    digits = {
        "x": (xpos, 2), "y": (ypos, 2), "z": (zpos, 4), "p": (plane_pos, 4),
        "w": (lax.rem(zpos, 2), 2), "v": (zpos // 2, 2),
    }

    def digit_peer(d, k):
        if d == "z":
            return z_peer(k)
        if d == "p":
            return plane_peer(k)
        z_step = {"w": 1 - 2 * lax.rem(zpos, 2), "v": 2 - 4 * (zpos // 2)}
        if d in z_step:
            return (img + 2 * z_step[d], me)
        return x_peer if d == "x" else y_peer

    def sum_unit(a, src, land, out, order):
        n = src.shape[1]
        levels, at, size, room = [], core * 256, 256, 256
        for d in order:
            pos, count = digits[d]
            part_size = size // count
            levels.append((d, pos, count, at, part_size, room))
            at, room = at + pos * part_size, room + (count - 1) * part_size
            size = part_size
        own_at, last = at, len(order) - 1

        def rows(start, length):
            return pl.ds(pl.multiple_of(start, 16), length)

        def copy(src_at, dst, length, i, peer):
            return remote(src.at[rows(src_at, length)], dst, s_ar.at[a, 0], r_ar.at[a, i], peer)

        def core_send():
            return copy((1 - core) * 256, land.at[pl.ds(0, 256)], 256, 0, core_peer)

        def down(j, k):
            d, pos, count, at, length, room = levels[j]
            dst = land.at[pl.ds(room + (k - 1) * length, length)]
            return copy(at + lax.rem(pos + k, count) * length, dst, length, 1 + j, digit_peer(d, k))

        def all_down(j):
            d, _, count, _, length, room = levels[j]
            dst = land.at[pl.ds(room, (count - 1) * length)]
            return copy(0, dst, (count - 1) * length, 1 + j, digit_peer(d, 1))

        def up(j, k):
            d, pos, count, at, length, _ = levels[j]
            here = out.at[rows(at + pos * length, length)]
            from_ = src.at[rows(own_at, length)] if j == last else here
            return remote(from_, here, s_ar.at[a, 1], r_ar.at[a, 5 + j], digit_peer(d, k))

        def all_up(j):
            d, _, count, _, length, _ = levels[j]
            some = out.at[pl.ds(0, (count - 1) * length)]
            return remote(some, some, s_ar.at[a, 1], r_ar.at[a, 5 + j], digit_peer(d, 1))

        def core_up(c):
            here = out.at[rows(c * 256, 256)]
            return remote(here, here, s_ar.at[a, 1], r_ar.at[a, 9], core_peer)

        def all_sent(i):
            some = out.at[pl.ds(0, 496)]
            return remote(some, some, s_ar.at[a, i], r_ar.at[a, 0], core_peer)

        def far_send(k):
            return remote(
                src.at[rows(own_at, 16)], far.at[a, k - 1, :, 0:n], s_ar.at[a, 1 + k], r_ar.at[a, 9 + k],
                far_peer(k),
            )

        def peers(j):
            return range(1, levels[j][2])

        def local():
            here = rows(own_at, 16)
            return pltpu.make_async_copy(src.at[here], out.at[here], l_ar.at[a])

        def step_core():
            core_send().start()

        def step_down(j):
            if j == 0:
                core_send().wait_recv()
                at = rows(core * 256, 256)
                src[at, :] = src[at, :] + land[0:256, :]
            else:
                take(j - 1)
            for k in peers(j):
                down(j, k).start()

        def take(j):
            d, pos, count, at, length, room = levels[j]
            here = rows(at + pos * length, length)
            all_down(j).wait_recv()
            total = src[here, :].astype(F32)
            for k in peers(j):
                r = room + (k - 1) * length
                total = total + land[r : r + length, :].astype(F32)
            src[here, :] = total.astype(BF)

        def step_turn():
            take(last)
            if extra > 1:
                here = rows(own_at, 16)
                for k in range(1, extra):
                    far_send(k).start()
                total = src[here, :].astype(F32)
                for k in range(1, extra):
                    far_send(k).wait()
                    total = total + far[a, k - 1, :, 0:n].astype(F32)
                src[here, :] = total.astype(BF)
            for k in peers(last):
                up(last, k).start()
            local().start()

        def step_up(j):
            if j == last:
                local().wait()
            all_up(j).wait_recv()
            if j == 0:
                core_up(core).start()
            else:
                for k in peers(j - 1):
                    up(j - 1, k).start()

        def step_last():
            core_up(1 - core).wait_recv()

        def step_sent():
            all_sent(0).wait_send()
            all_sent(1).wait_send()

        steps = [step_core] + [functools.partial(step_down, j) for j in range(last + 1)] + [step_turn]
        return steps + [functools.partial(step_up, j) for j in range(last, -1, -1)] + [step_last, step_sent]

    def together(units):
        return [lambda steps=steps: [step() for step in steps] for steps in zip(*units)]

    wide_units = [sum_unit(a, asum.at[a], rec.at[a], wide_hbm.at[a], ORDERS[a]) for a in range(9)]
    groups = [together(wide_units[2 * i : 2 * i + 2]) for i in range(4)] + [wide_units[8]]
    for p in range(2):
        part_units = []
        for i in range(3):
            place = (pl.ds(512 * (i // 2), 512), pl.ds(256 * (i % 2), 256))
            part_units.append(
                sum_unit(
                    9 + 3 * p + i, act.at[p].at[place], act.at[2 + p].at[place], qkv_hbm.at[p, i],
                    ORDERS[9 + 3 * p + i],
                )
            )
        groups.append(together(part_units))

    def small_steps():
        mine, other = pl.ds(pl.multiple_of(16 * core, 16), 16), pl.ds(pl.multiple_of(16 - 16 * core, 16), 16)

        def copy(src, dst, i, peer):
            return remote(src, dst, s_sm.at[i], r_sm.at[i], peer)

        def core_send():
            return copy(small_s.at[0, other], small_c, 0, core_peer)

        def plane_send(k):
            return copy(small_s.at[1, mine], small_p.at[k - 1], 1, plane_peer(k))

        def z_send(k):
            return copy(small_s.at[2, mine], small_z.at[k - 1], 2, z_peer(k))

        def far_copy(k):
            return copy(small_s.at[3, mine], small_far.at[k - 1], 3 + k, far_peer(k))

        def core_up(rows):
            return copy(small_o.at[rows], small_o.at[rows], 3, core_peer)

        def step0():
            core_send().start()

        def step1():
            core_send().wait_recv()
            small_s[1, mine, :] = small_s[0, mine, :] + small_c[...]
            for k in range(1, 4):
                plane_send(k).start()

        def step2():
            total = small_s[1, mine, :]
            copy(small_p, small_p, 1, core_peer).wait_recv()
            for k in range(3):
                total = total + small_p[k]
            small_s[2, mine, :] = total
            for k in range(1, 4):
                z_send(k).start()

        def step3():
            total = small_s[2, mine, :]
            copy(small_z, small_z, 2, core_peer).wait_recv()
            for k in range(3):
                total = total + small_z[k]
            if extra > 1:
                small_s[3, mine, :] = total
                for k in range(1, extra):
                    far_copy(k).start()
                for k in range(1, extra):
                    far_copy(k).wait()
                    total = total + small_far[k - 1]
            small_o[mine, :] = total
            core_up(mine).start()

        def step4():
            core_up(other).wait_recv()
            small_out[...] = small_o[...]

        def step5():
            core_send().wait_send()
            core_up(mine).wait_send()
            copy(small_p, small_p, 1, core_peer).wait_send()
            copy(small_z, small_z, 2, core_peer).wait_send()

        return [step0, step1, step2, step3, step4, step5]

    groups.append(small_steps())

    def run(name):
        for at, j in SCHEDULE.get(name, ()):
            groups[at][j]()

    def run_in(prefix, i):
        for at in range(8):
            if SCHEDULE.get(f"{prefix}{at}"):

                @pl.when(i == at)
                def _(at=at):
                    run(f"{prefix}{at}")

    for c in range(4):
        asum[c] = tn(act[c], dout[...]).astype(BF)
        run(f"a{c}")

    for w in range(4):
        dmid[w] = flat(to_blocks(cr[w].astype(F32))).reshape(4, 64, 512)

    def dense_back(c, _):
        cols = pl.ds(pl.multiple_of(512 * c, 512), 512)
        dh = (nt(dout[...], wc[cols, :]) * dhid[c].astype(F32)).astype(BF)
        dhid[c] = dh
        acc_s[3 + c] = col_sum(dh.astype(F32))
        dmid[...] += nt(dh, we[:, cols]).reshape(4, 4, 64, 512)
        asum[4 + c] = tn(mlow[...], dh).astype(BF)
        run_in("d", c)
        return 0

    lax.fori_loop(0, 4, dense_back, 0)

    def norm_back(pair, _):
        z1, r1 = first_norm(pair)
        dm = dmid[pl.ds(2 * pair, 2)].reshape(512, 512)
        acc_s[7] += col_sum(dm * z1)
        acc_s[8] += col_sum(dm)
        dn1 = dm * g1[...][None, :]
        db = r1 * (
            dn1 - jnp.mean(dn1, axis=1, keepdims=True) - z1 * jnp.mean(dn1 * z1, axis=1, keepdims=True)
        )
        blk[pl.ds(2 * pair, 2)] = db.astype(BF).reshape(2, 4, 64, 512)
        return 0

    lax.fori_loop(0, 2, norm_back, 0)
    run("nb")

    bias[...] = jnp.zeros_like(bias)

    def gather(o, _):
        for bcol in range(2):
            for br in range(2):
                at = (bcol * 2 + br) * 64
                cr[o, at : at + 64, :] = blk[home(o, bcol, br)]
        return 0

    lax.fori_loop(0, 4, gather, 0)
    asum[8] = tn(mixed[...].reshape(1024, 512), cr[...].reshape(1024, 512)).astype(BF)
    run("gproj")
    head_ones_half = head_ones[0:128, 0:128]
    minus = jnp.full((256, 128), -1.0, BF)
    lane32 = lax.rem(lax.broadcasted_iota(jnp.int32, (256, 128), 1), 32)

    def retreat(it, _):
        p, o = it // 4, lax.rem(it, 4)
        half = pl.ds(pl.multiple_of(256 * p, 256), 256)
        dmx = nt(cr[o], wproj[half, :])
        rows = pl.ds(pl.multiple_of(o * TOK, TOK), TOK)
        scales = scale_lanes(p)
        for gi in range(2):
            g = 2 * p + gi
            lanes = pl.ds(pl.multiple_of(128 * g, 128), 128)
            qg, kg, vg = qs[o, g], kl[o, g], vl[o, g]
            dmg = dmx[:, 128 * gi : 128 * gi + 128] * isum[o, g]
            dmp = dmg.astype(BF)
            mix = mixed[o, :, lanes].astype(F32) + mixlo[o, :, lanes].astype(F32)
            prod = dmp.astype(F32) * mix
            delta = sum(nn(p, head_ones_half) for p in split3(prod)[:2])
            delta_hi, delta_lo, _ = split3(delta)
            prod = jnp.where(lane32 == 0, delta_hi, jnp.where(lane32 == 1, delta_lo, jnp.zeros_like(delta_lo)))
            vw = jnp.concatenate([vg, minus], axis=1)
            dmp4 = jnp.concatenate([dmp * mask for mask in head_mask], axis=0)
            left = jnp.concatenate([dmp4, jnp.concatenate([prod * mask for mask in head_mask], axis=0)], axis=1)
            e4 = ex[o, g].reshape(1024, 256)
            dsf = nt(left, vw) * e4.astype(F32)
            ds = dsf.astype(BF)
            for hh in range(4):
                h, n = 4 * g + hh, 256 * hh
                bias[h, 1] += dsf[n : n + 128, 0:128] + dsf[n + 128 : n + 256, 128:256]
                bias[h, 0] += dsf[n : n + 128, 128:256]
                bias[h, 2] += dsf[n + 128 : n + 256, 0:128]
            dq = nn(
                jnp.concatenate([ds[256 * hh : 256 * hh + 256] for hh in range(4)], axis=1),
                jnp.concatenate([kg * mask for mask in head_mask], axis=0),
            )
            dk = tn(ds, jnp.concatenate([qg * mask for mask in head_mask], axis=0))
            dv = tn(e4, dmp4)
            qf, kf = qg.astype(F32), kg.astype(F32)
            scale = scales[:, 128 * gi : 128 * gi + 128]
            tq = dq * qf
            acc_s[9, :, lanes] += col_sum(tq)
            aq = nn(tq.astype(BF), head_ones_half)
            ak = nn((dk * kf).astype(BF), head_ones_half)
            dhid[0, rows, lanes] = (qinv[o, g].astype(F32) * (scale * dq - (1.0 / scale) * qf * aq)).astype(BF)
            dhid[1, rows, lanes] = (kinv[o, g].astype(F32) * (dk - kf * ak)).astype(BF)
            dhid[2, rows, lanes] = dv.astype(BF)
        run_in("r", it)

        @pl.when(lax.rem(it, 4) == 3)
        def _():
            moved = sum(
                nt(dhid[i, :, half], wqkv[:, pl.ds(pl.multiple_of(512 * i + 256 * p, 256), 256)])
                for i in range(3)
            )
            for w in range(4):
                for bcol in range(2):
                    for br in range(2):
                        at = 256 * w + (bcol * 2 + br) * 64
                        dmid[home(w, bcol, br)] += moved[at : at + 64, :]
            xflat = xroll[...].reshape(1024, 512)
            for i in range(3):
                grad = tn(xflat, dhid[i, :, half]).astype(BF)
                act[p, 512 * (i // 2) : 512 * (i // 2) + 512, 256 * (i % 2) : 256 * (i % 2) + 256] = grad

        run_in("gq", jnp.where(lax.rem(it, 4) == 3, p, -1))
        return 0

    lax.fori_loop(0, 8, retreat, 0)

    def gin_copy(w):
        return remote(slope.at[w], gin_hbm.at[me, 0], s_gin.at[w], r_gin.at[me], (img, w))

    def finish(w, _):
        quads = [[dmid[w, 2 * qr + qc] for qc in range(2)] for qr in range(2)]
        slope[w] = from_blocks(quads).astype(BF)

        @pl.when(w != me)
        def _():
            gin_copy(w).start()

        return 0

    lax.fori_loop(0, 4, finish, 0)
    own_gin = pltpu.make_async_copy(slope.at[me], gin_hbm.at[me, 0], r_gin.at[me])
    own_gin.start()
    run("finish")

    row_ones = jnp.ones((8, 1024), BF)

    def put(row, v):
        small_s[0, row : row + v.shape[0], :] = v

    put(ROW_QB, nn(row_ones, dhid[0])[0:1])
    put(ROW_VB, nn(row_ones, dhid[2])[0:1])
    put(ROW_BP, nn(row_ones, cr[...].reshape(1024, 512))[0:1])
    for row, i in ((ROW_LS, 9), (ROW_G1, 7), (ROW_S1, 8), (ROW_B2, 2), (ROW_G2, 0), (ROW_S2, 1)):
        put(row, jnp.sum(acc_s[i], axis=0, keepdims=True))
    for c in range(4):
        put(ROW_BE + c, jnp.sum(acc_s[3 + c], axis=0, keepdims=True))
    run("puts")
    short = jnp.zeros((384, 256), F32)
    for c in range(4):
        places = one_hot_places(c)
        left = jnp.concatenate(
            [bias[:, :, 8 * r : 8 * r + 8, :].reshape(384, 128) for r in range(4 * c, 4 * c + 4)], axis=1
        )
        for p in split3(left)[:2]:
            short = short + nt(p, places)
    pick = one_hot_pick()
    for i in range(4):
        piece = split3(short[96 * i : 96 * i + 96])[:2]
        part[4 * i : 4 * i + 4] = sum(nt(p, pick) for p in piece).reshape(4, 24, 1024)
    run("bb")
    dtab = jnp.zeros((16, 1024), F32)
    for u in range(24):
        dtab = dtab + pltpu.roll(part[:, u, :], 23 - u, 1)
    tab[...] = dtab * tab[...] * (1.0 - tab[...] * (1.0 / BIAS_RANGE))
    small_s[0, ROW_W1 : ROW_W2 + 16, :] = jnp.zeros((ROW_W2 + 16 - ROW_W1, 512), F32)

    def net_back(c, _):
        cols, pre = net_piece(c)
        cap, low = gelu_parts(pre)
        dlog, dlog_lo, _ = split3(tab[:, cols])
        units, units_lo, _ = split3(pre * cap)
        small_s[0, ROW_W2 : ROW_W2 + 16, :] += nn(dlog, units) + nn(dlog_lo, units) + nn(dlog, units_lo)
        w_hi, w_lo, _ = split3(w2t[...])
        back = tn(dlog, w_hi) + tn(dlog_lo, w_hi) + tn(dlog, w_lo)
        dpre, dpre_lo, _ = split3(back * (cap + pre * low))
        hi, mid, _ = split3(crow[:, cols])
        net = nn(hi, dpre) + nn(mid, dpre) + nn(hi, dpre_lo)
        small_s[0, ROW_W1 : ROW_W1 + 3, :] += net[0:3]
        return 0

    lax.fori_loop(0, 4, net_back, 0)
    run("net")
    for k in (1, 2, 3):
        frm = ring_from(k)
        x_send(k, 0).wait_send()
        x_send(k, 1).wait_send()
        spread(cot_hbm, cr, s_c, r_c, k).wait_send()
        res_copy(lax.rem(me + k, n_win)).wait_send()
        remote(xr.at[frm], res_hbm.at[frm, 0], s_res.at[frm], r_res.at[frm], (img, frm)).wait_recv()
    own_res.wait()
    own_gin.wait()
    last = {at: j for at, j in SCHEDULE["end"]}
    late = [at for at, group in enumerate(groups) if last.get(at) == len(group) - 2]
    for at, group in enumerate(groups):
        if at not in late:
            group[-1]()
    for at, j in SCHEDULE["end"]:
        groups[at][j]()
        if at in late and j == len(groups[at]) - 2:
            groups[at][-1]()

    for k in (1, 2, 3):
        frm, to = ring_from(k), lax.rem(me + k, n_win)
        gin_copy(to).wait_send()
        remote(slope.at[frm], gin_hbm.at[frm, 0], s_gin.at[frm], r_gin.at[frm], (img, frm)).wait_recv()


def widen_kernel(
    res, gin, wide, qkv, small,
    res_out, gin_out, w_qkv, g_qb, g_vb, g_ls, g_w1, g_b1, g_w2, w_proj, g_bp, g_g1, g_s1, w_fc1, g_be,
    w_fc2, g_b2, g_g2, g_s2,
    blocks, wide_in, qkv_in, wide_f, qkv_f, s_in, s_out, s_blocks,
):
    taken = [pltpu.make_async_copy(a, blocks.at[i], s_blocks.at[i]) for i, a in enumerate((res, gin))]
    passed = [pltpu.make_async_copy(blocks.at[i], a, s_blocks.at[2 + i]) for i, a in enumerate((res_out, gin_out))]
    pieces = []
    for i in range(9):
        if i < 4:
            place = w_fc2.at[pl.ds(512 * i, 512), :]
        elif i < 8:
            place = w_fc1.at[:, pl.ds(512 * (i - 4), 512)]
        else:
            place = w_proj
        pieces.append((wide.at[i], wide_in.at[i], wide_f.at[i], place))
    for i in range(6):
        place = w_qkv.at[:, pl.ds(512 * (i % 3) + 256 * (i // 3), 256)]
        pieces.append((qkv.at[i // 3, i % 3], qkv_in.at[i], qkv_f.at[i], place))
    loads = [pltpu.make_async_copy(a, b, s_in.at[i]) for i, (a, b, _, _) in enumerate(pieces)]
    stores = [pltpu.make_async_copy(c, d, s_out.at[i]) for i, (_, _, c, d) in enumerate(pieces)]
    for c in loads:
        c.start()
    for c in taken:
        c.start()
    for i, (_, b, c, _) in enumerate(pieces):
        loads[i].wait()
        c[...] = b[...].astype(F32)
        stores[i].start()
    for a, b in zip(taken, passed):
        a.wait()
        b.start()
    for row, out in (
        (ROW_QB, g_qb), (ROW_VB, g_vb), (ROW_B1, g_b1), (ROW_BP, g_bp), (ROW_G1, g_g1), (ROW_S1, g_s1),
        (ROW_B2, g_b2), (ROW_G2, g_g2), (ROW_S2, g_s2),
    ):
        out[...] = small[row, :]
    for c in range(4):
        g_be[512 * c : 512 * c + 512] = small[ROW_BE + c, :]
    g_w1[...] = small[ROW_W1 : ROW_W1 + 2, :]
    g_w2[...] = small[ROW_W2 : ROW_W2 + 16, :]
    h0 = lax.broadcasted_iota(jnp.int32, (512, 16), 0) // 32
    h1 = lax.broadcasted_iota(jnp.int32, (512, 16), 1)
    heads = jnp.where(h0 == h1, 1.0, 0.0).astype(BF)
    per_head = sum(nn(jnp.broadcast_to(p, (8, 512)), heads) for p in split3(small[ROW_LS : ROW_LS + 1, :]))
    g_ls[...] = per_head[0, :]
    for c in passed + stores:
        c.wait()


def body(n_img, n_win, inputs, wqkv, qb, vb, hls, w1, b1, w2, wproj, bproj, g1, s1, we, be, wc, bc, g2, s2, cot):
    extra = n_img // 8
    crow = table_coords()
    dma = pltpu.SemaphoreType.DMA
    n_sm = 4 + (extra - 1)
    vmem = pl.BlockSpec(memory_space=pltpu.VMEM)
    hbm = pl.BlockSpec(memory_space=pl.ANY)
    smem = pl.BlockSpec(memory_space=pltpu.SMEM)
    scratch = [
        pltpu.VMEM((4, TOK, 512), BF),
        pltpu.VMEM((4, TOK, 512), BF),
        pltpu.VMEM((4, TOK, 512), BF),
        pltpu.VMEM((16, 3, 128, 128), F32),
        pltpu.VMEM((4, 4, 4, TOK, TOK), BF),
        pltpu.VMEM((4, 4, TOK, 128), BF),
        pltpu.VMEM((4, 4, TOK, 128), BF),
        pltpu.VMEM((4, 4, TOK, 128), BF),
        pltpu.VMEM((4, 4, TOK, 128), BF),
        pltpu.VMEM((4, 4, TOK, 128), BF),
        pltpu.VMEM((4, 4, TOK, 128), F32),
        pltpu.VMEM((4, TOK, 512), BF),
        pltpu.VMEM((4, TOK, 512), BF),
        pltpu.VMEM((4, 4, 64, 512), BF),
        pltpu.VMEM((4, 4, 64, 512), F32),
        pltpu.VMEM((4, 1024, 512), BF),
        pltpu.VMEM((4, 1024, 512), BF),
        pltpu.VMEM((1024, 512), BF),
        pltpu.VMEM((1024, 512), BF),
        pltpu.VMEM((4, TOK, 512), BF),
        pltpu.VMEM((16, 1024), F32),
        pltpu.VMEM((16, 24, 1024), F32),
        pltpu.VMEM((10, 8, 512), F32),
        pltpu.VMEM((9, 512, 512), BF),
        pltpu.VMEM((9, 496, 512), BF),
        pltpu.VMEM((15, extra - 1, 16, 512) if extra > 1 else (1, 1, 16, 512), BF),
        pltpu.VMEM((512, 1536), BF),
        pltpu.VMEM((512, 512), BF),
        pltpu.VMEM((512, 2048), BF),
        pltpu.VMEM((2048, 512), BF),
        pltpu.VMEM((512,), F32), pltpu.VMEM((512,), F32),
        pltpu.VMEM((2, 512), F32), pltpu.VMEM((512,), F32), pltpu.VMEM((16, 512), F32),
        pltpu.VMEM((512,), F32), pltpu.VMEM((512,), F32), pltpu.VMEM((512,), F32),
        pltpu.VMEM((2048,), F32), pltpu.VMEM((512,), F32),
        pltpu.VMEM((512,), F32), pltpu.VMEM((512,), F32), pltpu.VMEM((8, 1024), F32),
        pltpu.VMEM((4, SMALL_ROWS, 512), F32),
        pltpu.VMEM((16, 512), F32),
        pltpu.VMEM((3, 16, 512), F32),
        pltpu.VMEM((3, 16, 512), F32),
        pltpu.VMEM((max(extra - 1, 1), 16, 512), F32),
        pltpu.VMEM((SMALL_ROWS, 512), F32),
        dma((2, 4)), dma((2, 4)), dma((4,)), dma((4,)),
        dma((4,)), dma((4,)), dma((4,)), dma((4,)),
        dma((15, 1 + extra)), dma((15, 9 + extra)), dma((15,)),
        dma((n_sm,)), dma((n_sm,)),
        dma((4,)), dma((13,)),
    ]
    block = jax.ShapeDtypeStruct(inputs.shape, BF)
    result, grad_inputs, wide, qkv, small = pl.pallas_call(
        functools.partial(block_kernel, n_img, n_win),
        out_shape=(
            block,
            block,
            jax.ShapeDtypeStruct((9, 512, 512), BF),
            jax.ShapeDtypeStruct((2, 3, 512, 256), BF),
            jax.ShapeDtypeStruct((SMALL_ROWS, 512), F32),
        ),
        in_specs=[hbm] * 6 + [smem] + [hbm] * 13,
        out_specs=(hbm, hbm, hbm, hbm, vmem),
        scratch_shapes=scratch,
        compiler_params=pltpu.CompilerParams(
            collective_id=0, has_side_effects=True, vmem_limit_bytes=64 * 1024 * 1024
        ),
    )(
        inputs, cot, wqkv, wproj, we, wc, hls, qb, vb, w1, b1, w2.T, bproj, g1, s1, be, bc, g2, s2,
        jnp.asarray(crow),
    )
    any_ = lambda shape: jax.ShapeDtypeStruct(shape, F32)
    outs = pl.pallas_call(
        widen_kernel,
        out_shape=(
            block, block, any_((512, 1536)), any_((512,)), any_((512,)), any_((16,)), any_((2, 512)),
            any_((512,)), any_((16, 512)), any_((512, 512)), any_((512,)), any_((512,)), any_((512,)),
            any_((512, 2048)), any_((2048,)), any_((2048, 512)), any_((512,)), any_((512,)), any_((512,)),
        ),
        in_specs=[hbm] * 4 + [vmem],
        out_specs=tuple(hbm if i in (0, 1, 2, 9, 13, 15) else vmem for i in range(19)),
        scratch_shapes=[
            pltpu.VMEM((2,) + inputs.shape, BF),
            pltpu.VMEM((9, 512, 512), BF),
            pltpu.VMEM((6, 512, 256), BF),
            pltpu.VMEM((9, 512, 512), F32),
            pltpu.VMEM((6, 512, 256), F32),
            dma((15,)), dma((15,)), dma((4,)),
        ],
        compiler_params=pltpu.CompilerParams(vmem_limit_bytes=63 * 1024 * 1024),
    )(result, grad_inputs, wide, qkv, small)
    return outs[:8] + (outs[8].T,) + outs[9:]


def solution(mesh):
    n_img, n_win = mesh.shape["img"], mesh.shape["win"]
    block = P("img", "win", None, None)
    return jax.shard_map(
        functools.partial(body, n_img, n_win),
        mesh=mesh,
        in_specs=(block,) + (P(),) * 17 + (block,),
        out_specs=(block, block) + (P(),) * 17,
        check_vma=False,
    )
```

```python
import functools

import jax
import jax.numpy as jnp
import numpy as np
from jax import lax
from jax.experimental import pallas as pl
from jax.experimental.pallas import tpu as pltpu
from jax.sharding import PartitionSpec as P

WIN = 16
TOK = WIN * WIN
EPS_DIR = 1e-06
EPS_NORM = 1e-05
MASK_FILL = -100.0
BIAS_RANGE = 16.0
INV_ROOT_TWO = 0.7071067811865476
INV_ROOT_TWOPI = 0.3989422804014327
LOG2_E = 1.4426950408889634
MESH = pl.DeviceIdType.MESH
BF = jnp.bfloat16
F32 = jnp.float32

(ROW_QB, ROW_VB, ROW_LS, ROW_W1, ROW_B1, ROW_W2, ROW_BP, ROW_G1, ROW_S1, ROW_B2, ROW_G2, ROW_S2,
 ROW_BE, SMALL_ROWS) = (0, 1, 2, 3, 5, 6, 22, 23, 24, 25, 26, 27, 28, 32)

SCHEDULE = {
    "a1": ((0, 0),),
    "a3": ((1, 0), (0, 1)),
    "d0": ((1, 1),),
    "d1": ((2, 0), (0, 2)),
    "d2": ((2, 1), (1, 2)),
    "d3": ((3, 0),),
    "nb": ((0, 3), (3, 1)),
    "gproj": ((4, 0), (2, 2)),
    "r0": ((4, 1), (1, 3), (3, 2)),
    "r1": ((0, 4),),
    "r2": ((2, 3), (4, 2), (1, 4)),
    "r3": ((3, 3), (0, 5), (2, 4)),
    "gq0": ((5, 0), (4, 3)),
    "r4": ((5, 1), (3, 4), (2, 5), (0, 6)),
    "r5": ((4, 4),),
    "r6": ((1, 5), (5, 2), (3, 5)),
    "r7": ((2, 6), (0, 7)),
    "gq1": ((6, 0), (4, 5), (1, 6), (5, 3), (0, 8), (3, 6), (6, 1), (2, 7)),
    "finish": ((4, 6),),
    "puts": ((1, 7), (5, 4)),
    "bb": ((3, 7), (6, 2), (2, 8)),
    "net": ((7, 0), (1, 8), (5, 5), (7, 1), (3, 8)),
    "end": (
        (6, 3), (2, 9), (2, 10), (1, 9), (5, 6), (7, 2), (1, 10), (6, 4), (3, 9), (5, 7), (3, 10), (5, 8), (7, 3),
        (6, 5), (7, 4), (6, 6),
    ),
}
ORDERS = (
    "wpv", "xyz", "wvxy", "xwyv", "wvxy", "xwyv", "xwvy", "yxwv", "pz",
    "pwv", "wpv", "wpv", "pz", "pz", "pz",
)


def nn(a, b):
    return lax.dot_general(a, b, (((1,), (0,)), ((), ())), preferred_element_type=F32)


def nt(a, b):
    return lax.dot_general(a, b, (((1,), (1,)), ((), ())), preferred_element_type=F32)


def tn(a, b):
    return lax.dot_general(a, b, (((0,), (0,)), ((), ())), preferred_element_type=F32)


def split3(v):
    hi = v.astype(BF)
    rest = v - hi.astype(F32)
    mid = rest.astype(BF)
    return hi, mid, (rest - mid.astype(F32)).astype(BF)


def gelu_parts(v):
    cap = 0.5 + 0.5 * lax.erf(v * INV_ROOT_TWO)
    return cap, INV_ROOT_TWOPI * jnp.exp2(v * v * (-0.5 * LOG2_E))


def col_sum(v):
    return jnp.sum(v.reshape(v.shape[0] // 8, 8, v.shape[1]), axis=0)


def to_blocks(v):
    n = v.shape[-1]
    t = v.reshape(2, 8, 2, 8, n)
    return [[t[qr, :, qc].reshape(64, n) for qc in range(2)] for qr in range(2)]


def from_blocks(quads):
    n = quads[0][0].shape[-1]
    rows = []
    for qr in range(2):
        a = quads[qr][0].reshape(8, 1, 8, n)
        b = quads[qr][1].reshape(8, 1, 8, n)
        rows.append(jnp.concatenate([a, b], axis=1).reshape(128, n))
    return jnp.concatenate(rows, axis=0)


def one_hot_places(c):
    l = lax.broadcasted_iota(jnp.int32, (256, 512), 0)
    k = lax.broadcasted_iota(jnp.int32, (256, 512), 1) + 512 * c
    return jnp.where(l == 8 * (15 - k // 128) + k % 128, 1.0, 0.0).astype(BF)


def one_hot_pick():
    k = lax.broadcasted_iota(jnp.int32, (1024, 256), 0)
    l = lax.broadcasted_iota(jnp.int32, (1024, 256), 1)
    return jnp.where(k == 32 * (l // 8) + l % 8, 1.0, 0.0).astype(BF)


def table_coords():
    k = np.arange(1024)
    out = np.zeros((2, 1024), np.float64)
    for i, off in enumerate((15 - k // 32, 15 - k % 32)):
        u = off * (8.0 / 15.0)
        out[i] = np.sign(u) * np.log2(np.abs(u) + 1.0) / 3.0
    rows = np.zeros((8, 1024), np.float32)
    rows[0:2] = out
    rows[2] = 1.0
    return rows


def net_first(cols, w1, b1):
    return cols[:, 0:1] * w1[0:1, :] + cols[:, 1:2] * w1[1:2, :] + b1


def block_kernel(
    n_img, n_win,
    x_hbm, cot_hbm, wqkv_hbm, wproj_hbm, we_hbm, wc_hbm, hls, qb_hbm, vb_hbm, w1_hbm, b1_hbm,
    w2t_hbm, bproj_hbm, g1_hbm, s1_hbm, be_hbm, bc_hbm, g2_hbm, s2_hbm, crow_hbm,
    res_hbm, gin_hbm, wide_hbm, qkv_hbm, small_out,
    xr, cr, xroll, bias, ex, qs, kl, vl, qinv, kinv, isum, mixed, mixlo, blk, dmid, act, dhid, dout,
    mlow, slope, tab, part, acc_s, asum, rec, far, wqkv, wproj, we, wc,
    qb, vb, w1, b1, w2t, bproj, g1, s1, be, bc, g2, s2, crow,
    small_s, small_c, small_p, small_z, small_far, small_o,
    s_x, r_x, s_c, r_c, s_res, r_res, s_gin, r_gin, s_ar, r_ar, l_ar, s_sm, r_sm, s_w, s_v,
):
    img = lax.axis_index("img")
    me = lax.axis_index("win")
    extra = n_img // 8
    core = lax.rem(me, 2)
    ypos = me // 2
    xpos = lax.rem(img, 2)
    zpos = lax.rem(img // 2, 4)
    upper = img // 8

    def ring_to(k):
        return (img, lax.rem(me + k, n_win))

    def ring_from(k):
        return lax.rem(me + n_win - k, n_win)

    core_peer = (img, me + 1 - 2 * core)
    y_peer = (img, lax.rem(me + 2, 4))
    x_peer = (img + 1 - 2 * xpos, me)
    plane_pos = 2 * xpos + ypos

    def z_peer(k):
        return (upper * 8 + lax.rem(zpos + k, 4) * 2 + xpos, me)

    def plane_peer(k):
        to = lax.rem(plane_pos + k, 4)
        return (img + to // 2 - xpos, lax.rem(to, 2) * 2 + core)

    def far_peer(k):
        return (lax.rem(upper + k, extra) * 8 + zpos * 2 + xpos, me)

    weights = [
        pltpu.make_async_copy(a, b, s_w.at[i])
        for i, (a, b) in enumerate(((wqkv_hbm, wqkv), (wproj_hbm, wproj), (we_hbm, we), (wc_hbm, wc)))
    ]

    own_x = pltpu.make_async_copy(x_hbm.at[me, 0], xr.at[me], r_x.at[0, 0])
    own_c = pltpu.make_async_copy(cot_hbm.at[me, 0], cr.at[me], r_c.at[0])
    vectors = [
        pltpu.make_async_copy(a, b, s_v.at[i])
        for i, (a, b) in enumerate(
            (
                (w1_hbm, w1), (b1_hbm, b1), (w2t_hbm, w2t), (crow_hbm, crow), (qb_hbm, qb), (vb_hbm, vb),
                (bproj_hbm, bproj), (g1_hbm, g1), (s1_hbm, s1), (be_hbm, be), (bc_hbm, bc), (g2_hbm, g2),
                (s2_hbm, s2),
            )
        )
    ]
    for c in vectors + [own_x] + weights + [own_c]:
        c.start()

    barrier = pltpu.get_barrier_semaphore()
    others = [ring_to(k) for k in range(1, n_win)] + [x_peer, (img + 1 - 2 * xpos, lax.rem(me + 2, 4))]
    others += [z_peer(k) for k in range(1, 4)] + [far_peer(k) for k in range(1, extra)]
    for peer in others:
        pl.semaphore_signal(barrier, inc=1, device_id=peer, device_id_type=MESH)
    pl.semaphore_wait(barrier, len(others))

    def remote(src, dst, ssem, rsem, peer):
        return pltpu.make_async_remote_copy(
            src_ref=src, dst_ref=dst, send_sem=ssem, recv_sem=rsem, device_id=peer, device_id_type=MESH
        )

    def spread(src_hbm, dst, ssem, rsem, k):
        to = lax.rem(me + k, n_win)
        return remote(src_hbm.at[to, 0], dst.at[me], ssem.at[k], rsem.at[k], ring_to(k))

    def spread_in(src_hbm, dst, ssem, rsem, k):
        frm = ring_from(k)
        return remote(src_hbm.at[frm, 0], dst.at[frm], ssem.at[k], rsem.at[k], ring_to(k))

    def half_rows(w, half):
        return pl.ds(pl.multiple_of(128 * (1 - w // 2 if half == 0 else w // 2), 128), 128)

    def x_send(k, half):
        to, rows = lax.rem(me + k, n_win), half_rows(me, half)
        return remote(
            x_hbm.at[to, 0, rows], xr.at[me, rows], s_x.at[half, k], r_x.at[half, k], ring_to(k)
        )

    def x_arrival(k, half):
        frm = ring_from(k)
        rows = half_rows(frm, half)
        return remote(x_hbm.at[frm, 0, rows], xr.at[frm, rows], s_x.at[half, k], r_x.at[half, k], ring_to(k))

    for half in range(2):
        for k in (2, 1, 3):
            x_send(k, half).start()
    for k in (2, 1, 3):
        spread(cot_hbm, cr, s_c, r_c, k).start()

    for c in vectors:
        c.wait()
    def net_piece(c):
        rows = pl.ds(pl.multiple_of(256 * c, 256), 256)
        return rows, net_first(crow[:, rows].T, w1[...], b1[...][None, :])

    def look_up(c, _):
        cols, pre = net_piece(c)
        logits = lax.dot_general(
            w2t[...], pre * gelu_parts(pre)[0], (((1,), (1,)), ((), ())),
            precision=lax.Precision.HIGHEST, preferred_element_type=F32,
        )
        tab[:, cols] = BIAS_RANGE / (1.0 + jnp.exp(-logits))
        return 0

    lax.fori_loop(0, 4, look_up, 0)
    for u in range(24):
        part[:, u, :] = pltpu.roll(tab[...], 1001 + u, 1)
    pick = one_hot_pick()
    short = jnp.concatenate(
        [sum(nn(p, pick) for p in split3(part[4 * i : 4 * i + 4].reshape(96, 1024))[:2]) for i in range(4)], axis=0
    )
    short_parts = split3(short)[:2]
    for c in range(4):
        places = one_hot_places(c)
        wide = sum(nn(p, places) for p in short_parts)
        for r in range(4):
            row = 8 * (4 * c + r)
            bias[:, :, row : row + 8, :] = wide[:, 128 * r : 128 * r + 128].reshape(16, 3, 8, 128)

    lane = lax.broadcasted_iota(jnp.int32, (1, 128), 1)
    head_mask = [jnp.where(lane // 32 == hh, 1.0, 0.0).astype(BF) for hh in range(4)]
    l0 = lax.broadcasted_iota(jnp.int32, (256, 256), 0)
    l1 = lax.broadcasted_iota(jnp.int32, (256, 256), 1)
    head_ones = jnp.where(l0 // 32 == l1 // 32, 1.0, 0.0).astype(BF)

    def scale_lanes(p):
        wide = lax.broadcasted_iota(jnp.int32, (1, 256), 1) // 32
        out = jnp.zeros((1, 256), F32)
        for i in range(8):
            out = jnp.where(wide == i, hls[8 * p + i], out)
        return jnp.exp(out)

    def lay(half):
        def one(w, _):
            late = w // 2 if half == 0 else 1 - w // 2
            rows = pl.ds(pl.multiple_of(128 * (1 - late), 128), 128)
            v = xr[w, rows, :].astype(F32).reshape(8, 2, 8, 512)
            for qc in range(2):
                bcol = 1 - qc
                ocol = lax.rem(w, 2) if bcol == 0 else 1 - lax.rem(w, 2)
                at = pl.ds(pl.multiple_of((bcol * 2 + late) * 64, 64), 64)
                xroll[2 * half + ocol, at, :] = v[:, qc].reshape(64, 512).astype(BF)
            return 0

        lax.fori_loop(0, 4, one, 0)

    def project(half):
        xw = xroll[2 * half : 2 * half + 2].reshape(512, 512)

        def one(p, _):
            def cols(i):
                return pl.ds(pl.multiple_of(512 * i + 256 * p, 256), 256)

            q = nn(xw, wqkv[:, cols(0)]) + qb[cols(0)][None, :]
            qi = lax.rsqrt(nn((q * q).astype(BF), head_ones) + EPS_DIR)
            qsc = (q * qi * scale_lanes(p)).astype(BF)
            k = nn(xw, wqkv[:, cols(1)])
            ki = lax.rsqrt(nn((k * k).astype(BF), head_ones) + EPS_DIR)
            kn = (k * ki).astype(BF)
            v = (nn(xw, wqkv[:, cols(2)]) + vb[cols(0)][None, :]).astype(BF)
            for w in range(2):
                rows = slice(256 * w, 256 * w + 256)
                for i in range(2):
                    lanes = slice(128 * i, 128 * i + 128)
                    at = (2 * half + w, 2 * p + i)
                    qs[at] = qsc[rows, lanes]
                    kl[at] = kn[rows, lanes]
                    vl[at] = v[rows, lanes]
                    qinv[at] = qi[rows, lanes].astype(BF)
                    kinv[at] = ki[rows, lanes].astype(BF)
            return 0

        lax.fori_loop(0, 2, one, 0)

    own_x.wait()
    for k in (1, 2, 3):
        x_arrival(k, 0).wait_recv()
    lay(0)
    weights[0].wait()
    project(0)
    weights[1].wait()

    row_half = lax.broadcasted_iota(jnp.int32, (128, 128), 0) // 64
    col_half = lax.broadcasted_iota(jnp.int32, (128, 128), 1) // 64
    apart = jnp.where(row_half == col_half, 0.0, MASK_FILL)

    def home(o, bcol, br):
        row, col = lax.rem(2 * (o // 2) + br + 1, 4), lax.rem(2 * lax.rem(o, 2) + bcol + 1, 4)
        return 2 * (row // 2) + col // 2, 2 * lax.rem(row, 2) + lax.rem(col, 2)

    def attend(o, _):
        @pl.when(o == 2)
        def _():
            for k in (1, 2, 3):
                x_arrival(k, 1).wait_recv()
            lay(1)
            project(1)

        rows_cut = jnp.where(o // 2 == 1, apart, 0.0)
        cols_cut = jnp.where(lax.rem(o, 2) == 1, jnp.full((128, 128), MASK_FILL, F32), rows_cut)

        for g in range(4):
            qg, kg, vg = qs[o, g], kl[o, g], vl[o, g]
            sc = nt(jnp.concatenate([qg * mask for mask in head_mask], axis=0), kg)
            for hh in range(4):
                h, n = 4 * g + hh, 256 * hh
                ex[o, g, hh, 0:128, 0:128] = jnp.exp(sc[n : n + 128, 0:128] + bias[h, 1] + rows_cut).astype(BF)
                ex[o, g, hh, 0:128, 128:256] = jnp.exp(sc[n : n + 128, 128:256] + bias[h, 0] + cols_cut).astype(BF)
                ex[o, g, hh, 128:256, 0:128] = jnp.exp(sc[n + 128 : n + 256, 0:128] + bias[h, 2] + cols_cut).astype(BF)
                ex[o, g, hh, 128:256, 128:256] = jnp.exp(
                    sc[n + 128 : n + 256, 128:256] + bias[h, 1] + rows_cut
                ).astype(BF)
            ones = [jnp.broadcast_to(mask, (256, 128)) for mask in head_mask]
            total = nn(
                jnp.concatenate([ex[o, g, hh] for hh in range(4)], axis=1),
                jnp.concatenate(
                    [jnp.concatenate([vg * mask, one], axis=1) for mask, one in zip(head_mask, ones)], axis=0
                ),
            )
            inv = 1.0 / total[:, 128:256]
            isum[o, g] = inv
            mix = total[:, 0:128] * inv
            mix_hi = mix.astype(BF)
            mixed[o, :, 128 * g : 128 * g + 128] = mix_hi
            mixlo[o, :, 128 * g : 128 * g + 128] = (mix - mix_hi.astype(F32)).astype(BF)

        branch = (nn(mixed[o], wproj[...]) + bproj[...][None, :]).astype(BF)
        for bcol in range(2):
            for br in range(2):
                at = (bcol * 2 + br) * 64
                blk[home(o, bcol, br)] = branch[at : at + 64, :]
        return 0

    lax.fori_loop(0, 4, attend, 0)

    weights[2].wait()
    weights[3].wait()
    acc_s[...] = jnp.zeros_like(acc_s)

    def res_copy(w):
        return remote(xr.at[w], res_hbm.at[me, 0], s_res.at[w], r_res.at[me], (img, w))

    def flat(quads):
        return jnp.concatenate([quads[0][0], quads[0][1], quads[1][0], quads[1][1]], axis=0)

    def first_norm(pair):
        back = blk[pl.ds(2 * pair, 2)].reshape(512, 512).astype(F32)
        ctr = back - jnp.mean(back, axis=1, keepdims=True)
        r1 = lax.rsqrt(jnp.mean(ctr * ctr, axis=1, keepdims=True) + EPS_NORM)
        return ctr * r1, r1

    def laid(ref, pair):
        return jnp.concatenate([flat(to_blocks(ref[2 * pair + i].astype(F32))) for i in range(2)], axis=0)

    def dense(turn, _):
        pair = lax.rem(ypos + turn, 2)
        z1, _ = first_norm(pair)
        middle = laid(xr, pair) + z1 * g1[...][None, :] + s1[...][None, :]
        ml = middle.astype(BF)
        rows = pl.ds(pl.multiple_of(pair * 512, 512), 512)
        mlow[rows, :] = ml
        out = jnp.zeros((512, 512), F32)
        for c in range(8):
            cols = slice(256 * c, 256 * c + 256)
            part_cols = slice(256 * (c % 2), 256 * (c % 2) + 256)
            hid = nn(ml, we[:, cols]) + be[cols][None, :]
            cap, low = gelu_parts(hid)
            a = (hid * cap).astype(BF)
            act[c // 2, rows, part_cols] = a
            dhid[c // 2, rows, part_cols] = (cap + hid * low).astype(BF)
            out = out + nn(a, wc[cols, :])
        out = out + bc[...][None, :]
        ctr2 = out - jnp.mean(out, axis=1, keepdims=True)
        r2 = lax.rsqrt(jnp.mean(ctr2 * ctr2, axis=1, keepdims=True) + EPS_NORM)
        z2 = ctr2 * r2
        result = middle + z2 * g2[...][None, :] + s2[...][None, :]
        for i in range(2):
            quads = [[result[256 * i + 64 * (2 * qr + qc) :][:64] for qc in range(2)] for qr in range(2)]
            w = 2 * pair + i
            xr[w] = from_blocks(quads).astype(BF)

            @pl.when(w != me)
            def _(w=w):
                res_copy(w).start()

        @pl.when(turn == 0)
        def _():
            own_c.wait()
            spread_in(cot_hbm, cr, s_c, r_c, 3 - 2 * core).wait_recv()

        @pl.when(turn == 1)
        def _():
            spread_in(cot_hbm, cr, s_c, r_c, 2).wait_recv()
            spread_in(cot_hbm, cr, s_c, r_c, 1 + 2 * core).wait_recv()

        e = laid(cr, pair)
        acc_s[0] += col_sum(e * z2)
        acc_s[1] += col_sum(e)
        dn = e * g2[...][None, :]
        dv = r2 * (
            dn - jnp.mean(dn, axis=1, keepdims=True) - z2 * jnp.mean(dn * z2, axis=1, keepdims=True)
        )
        do = dv.astype(BF)
        dout[rows, :] = do
        acc_s[2] += col_sum(do.astype(F32))
        return 0

    lax.fori_loop(0, 2, dense, 0)
    own_res = pltpu.make_async_copy(xr.at[me], res_hbm.at[me, 0], r_res.at[me])
    own_res.start()

    digits = {
        "x": (xpos, 2), "y": (ypos, 2), "z": (zpos, 4), "p": (plane_pos, 4),
        "w": (lax.rem(zpos, 2), 2), "v": (zpos // 2, 2),
    }

    def digit_peer(d, k):
        if d == "z":
            return z_peer(k)
        if d == "p":
            return plane_peer(k)
        z_step = {"w": 1 - 2 * lax.rem(zpos, 2), "v": 2 - 4 * (zpos // 2)}
        if d in z_step:
            return (img + 2 * z_step[d], me)
        return x_peer if d == "x" else y_peer

    def sum_unit(a, src, land, out, order):
        n = src.shape[1]
        levels, at, size, room = [], core * 256, 256, 256
        for d in order:
            pos, count = digits[d]
            part_size = size // count
            levels.append((d, pos, count, at, part_size, room))
            at, room = at + pos * part_size, room + (count - 1) * part_size
            size = part_size
        own_at, last = at, len(order) - 1

        def rows(start, length):
            return pl.ds(pl.multiple_of(start, 16), length)

        def copy(src_at, dst, length, i, peer):
            return remote(src.at[rows(src_at, length)], dst, s_ar.at[a, 0], r_ar.at[a, i], peer)

        def core_send():
            return copy((1 - core) * 256, land.at[pl.ds(0, 256)], 256, 0, core_peer)

        def down(j, k):
            d, pos, count, at, length, room = levels[j]
            dst = land.at[pl.ds(room + (k - 1) * length, length)]
            return copy(at + lax.rem(pos + k, count) * length, dst, length, 1 + j, digit_peer(d, k))

        def all_down(j):
            d, _, count, _, length, room = levels[j]
            dst = land.at[pl.ds(room, (count - 1) * length)]
            return copy(0, dst, (count - 1) * length, 1 + j, digit_peer(d, 1))

        def up(j, k):
            d, pos, count, at, length, _ = levels[j]
            here = out.at[rows(at + pos * length, length)]
            from_ = src.at[rows(own_at, length)] if j == last else here
            return remote(from_, here, s_ar.at[a, 1], r_ar.at[a, 5 + j], digit_peer(d, k))

        def all_up(j):
            d, _, count, _, length, _ = levels[j]
            some = out.at[pl.ds(0, (count - 1) * length)]
            return remote(some, some, s_ar.at[a, 1], r_ar.at[a, 5 + j], digit_peer(d, 1))

        def core_up(c):
            here = out.at[rows(c * 256, 256)]
            return remote(here, here, s_ar.at[a, 1], r_ar.at[a, 9], core_peer)

        def all_sent(i):
            some = out.at[pl.ds(0, 496)]
            return remote(some, some, s_ar.at[a, i], r_ar.at[a, 0], core_peer)

        def far_send(k):
            return remote(
                src.at[rows(own_at, 16)], far.at[a, k - 1, :, 0:n], s_ar.at[a, 1 + k], r_ar.at[a, 9 + k],
                far_peer(k),
            )

        def peers(j):
            return range(1, levels[j][2])

        def local():
            here = rows(own_at, 16)
            return pltpu.make_async_copy(src.at[here], out.at[here], l_ar.at[a])

        def step_core():
            core_send().start()

        def step_down(j):
            if j == 0:
                core_send().wait_recv()
                at = rows(core * 256, 256)
                src[at, :] = src[at, :] + land[0:256, :]
            else:
                take(j - 1)
            for k in peers(j):
                down(j, k).start()

        def take(j):
            d, pos, count, at, length, room = levels[j]
            here = rows(at + pos * length, length)
            all_down(j).wait_recv()
            total = src[here, :].astype(F32)
            for k in peers(j):
                r = room + (k - 1) * length
                total = total + land[r : r + length, :].astype(F32)
            src[here, :] = total.astype(BF)

        def step_turn():
            take(last)
            if extra > 1:
                here = rows(own_at, 16)
                for k in range(1, extra):
                    far_send(k).start()
                total = src[here, :].astype(F32)
                for k in range(1, extra):
                    far_send(k).wait()
                    total = total + far[a, k - 1, :, 0:n].astype(F32)
                src[here, :] = total.astype(BF)
            for k in peers(last):
                up(last, k).start()
            local().start()

        def step_up(j):
            if j == last:
                local().wait()
            all_up(j).wait_recv()
            if j == 0:
                core_up(core).start()
            else:
                for k in peers(j - 1):
                    up(j - 1, k).start()

        def step_last():
            core_up(1 - core).wait_recv()

        def step_sent():
            all_sent(0).wait_send()
            all_sent(1).wait_send()

        steps = [step_core] + [functools.partial(step_down, j) for j in range(last + 1)] + [step_turn]
        return steps + [functools.partial(step_up, j) for j in range(last, -1, -1)] + [step_last, step_sent]

    def together(units):
        return [lambda steps=steps: [step() for step in steps] for steps in zip(*units)]

    wide_units = [sum_unit(a, asum.at[a], rec.at[a], wide_hbm.at[a], ORDERS[a]) for a in range(9)]
    groups = [together(wide_units[2 * i : 2 * i + 2]) for i in range(4)] + [wide_units[8]]
    for p in range(2):
        part_units = []
        for i in range(3):
            place = (pl.ds(512 * (i // 2), 512), pl.ds(256 * (i % 2), 256))
            part_units.append(
                sum_unit(
                    9 + 3 * p + i, act.at[p].at[place], act.at[2 + p].at[place], qkv_hbm.at[p, i],
                    ORDERS[9 + 3 * p + i],
                )
            )
        groups.append(together(part_units))

    def small_steps():
        mine, other = pl.ds(pl.multiple_of(16 * core, 16), 16), pl.ds(pl.multiple_of(16 - 16 * core, 16), 16)

        def copy(src, dst, i, peer):
            return remote(src, dst, s_sm.at[i], r_sm.at[i], peer)

        def core_send():
            return copy(small_s.at[0, other], small_c, 0, core_peer)

        def plane_send(k):
            return copy(small_s.at[1, mine], small_p.at[k - 1], 1, plane_peer(k))

        def z_send(k):
            return copy(small_s.at[2, mine], small_z.at[k - 1], 2, z_peer(k))

        def far_copy(k):
            return copy(small_s.at[3, mine], small_far.at[k - 1], 3 + k, far_peer(k))

        def core_up(rows):
            return copy(small_o.at[rows], small_o.at[rows], 3, core_peer)

        def step0():
            core_send().start()

        def step1():
            core_send().wait_recv()
            small_s[1, mine, :] = small_s[0, mine, :] + small_c[...]
            for k in range(1, 4):
                plane_send(k).start()

        def step2():
            total = small_s[1, mine, :]
            copy(small_p, small_p, 1, core_peer).wait_recv()
            for k in range(3):
                total = total + small_p[k]
            small_s[2, mine, :] = total
            for k in range(1, 4):
                z_send(k).start()

        def step3():
            total = small_s[2, mine, :]
            copy(small_z, small_z, 2, core_peer).wait_recv()
            for k in range(3):
                total = total + small_z[k]
            if extra > 1:
                small_s[3, mine, :] = total
                for k in range(1, extra):
                    far_copy(k).start()
                for k in range(1, extra):
                    far_copy(k).wait()
                    total = total + small_far[k - 1]
            small_o[mine, :] = total
            core_up(mine).start()

        def step4():
            core_up(other).wait_recv()
            small_out[...] = small_o[...]

        def step5():
            core_send().wait_send()
            core_up(mine).wait_send()
            copy(small_p, small_p, 1, core_peer).wait_send()
            copy(small_z, small_z, 2, core_peer).wait_send()

        return [step0, step1, step2, step3, step4, step5]

    groups.append(small_steps())

    def run(name):
        for at, j in SCHEDULE.get(name, ()):
            groups[at][j]()

    def run_in(prefix, i):
        for at in range(8):
            if SCHEDULE.get(f"{prefix}{at}"):

                @pl.when(i == at)
                def _(at=at):
                    run(f"{prefix}{at}")

    for c in range(4):
        asum[c] = tn(act[c], dout[...]).astype(BF)
        run(f"a{c}")

    for w in range(4):
        dmid[w] = flat(to_blocks(cr[w].astype(F32))).reshape(4, 64, 512)

    def dense_back(c, _):
        cols = pl.ds(pl.multiple_of(512 * c, 512), 512)
        dh = (nt(dout[...], wc[cols, :]) * dhid[c].astype(F32)).astype(BF)
        dhid[c] = dh
        acc_s[3 + c] = col_sum(dh.astype(F32))
        dmid[...] += nt(dh, we[:, cols]).reshape(4, 4, 64, 512)
        asum[4 + c] = tn(mlow[...], dh).astype(BF)
        run_in("d", c)
        return 0

    lax.fori_loop(0, 4, dense_back, 0)

    def norm_back(pair, _):
        z1, r1 = first_norm(pair)
        dm = dmid[pl.ds(2 * pair, 2)].reshape(512, 512)
        acc_s[7] += col_sum(dm * z1)
        acc_s[8] += col_sum(dm)
        dn1 = dm * g1[...][None, :]
        db = r1 * (
            dn1 - jnp.mean(dn1, axis=1, keepdims=True) - z1 * jnp.mean(dn1 * z1, axis=1, keepdims=True)
        )
        blk[pl.ds(2 * pair, 2)] = db.astype(BF).reshape(2, 4, 64, 512)
        return 0

    lax.fori_loop(0, 2, norm_back, 0)
    run("nb")

    bias[...] = jnp.zeros_like(bias)

    def gather(o, _):
        for bcol in range(2):
            for br in range(2):
                at = (bcol * 2 + br) * 64
                cr[o, at : at + 64, :] = blk[home(o, bcol, br)]
        return 0

    lax.fori_loop(0, 4, gather, 0)
    asum[8] = tn(mixed[...].reshape(1024, 512), cr[...].reshape(1024, 512)).astype(BF)
    run("gproj")
    head_ones_half = head_ones[0:128, 0:128]
    minus = jnp.full((256, 128), -1.0, BF)
    lane32 = lax.rem(lax.broadcasted_iota(jnp.int32, (256, 128), 1), 32)

    def retreat(it, _):
        p, o = it // 4, lax.rem(it, 4)
        half = pl.ds(pl.multiple_of(256 * p, 256), 256)
        dmx = nt(cr[o], wproj[half, :])
        rows = pl.ds(pl.multiple_of(o * TOK, TOK), TOK)
        scales = scale_lanes(p)
        for gi in range(2):
            g = 2 * p + gi
            lanes = pl.ds(pl.multiple_of(128 * g, 128), 128)
            qg, kg, vg = qs[o, g], kl[o, g], vl[o, g]
            dmg = dmx[:, 128 * gi : 128 * gi + 128] * isum[o, g]
            dmp = dmg.astype(BF)
            mix = mixed[o, :, lanes].astype(F32) + mixlo[o, :, lanes].astype(F32)
            prod = dmp.astype(F32) * mix
            delta = sum(nn(p, head_ones_half) for p in split3(prod)[:2])
            delta_hi, delta_lo, _ = split3(delta)
            prod = jnp.where(lane32 == 0, delta_hi, jnp.where(lane32 == 1, delta_lo, jnp.zeros_like(delta_lo)))
            vw = jnp.concatenate([vg, minus], axis=1)
            dmp4 = jnp.concatenate([dmp * mask for mask in head_mask], axis=0)
            left = jnp.concatenate([dmp4, jnp.concatenate([prod * mask for mask in head_mask], axis=0)], axis=1)
            e4 = ex[o, g].reshape(1024, 256)
            dsf = nt(left, vw) * e4.astype(F32)
            ds = dsf.astype(BF)
            for hh in range(4):
                h, n = 4 * g + hh, 256 * hh
                bias[h, 1] += dsf[n : n + 128, 0:128] + dsf[n + 128 : n + 256, 128:256]
                bias[h, 0] += dsf[n : n + 128, 128:256]
                bias[h, 2] += dsf[n + 128 : n + 256, 0:128]
            dq = nn(
                jnp.concatenate([ds[256 * hh : 256 * hh + 256] for hh in range(4)], axis=1),
                jnp.concatenate([kg * mask for mask in head_mask], axis=0),
            )
            dk = tn(ds, jnp.concatenate([qg * mask for mask in head_mask], axis=0))
            dv = tn(e4, dmp4)
            qf, kf = qg.astype(F32), kg.astype(F32)
            scale = scales[:, 128 * gi : 128 * gi + 128]
            tq = dq * qf
            acc_s[9, :, lanes] += col_sum(tq)
            aq = nn(tq.astype(BF), head_ones_half)
            ak = nn((dk * kf).astype(BF), head_ones_half)
            dhid[0, rows, lanes] = (qinv[o, g].astype(F32) * (scale * dq - (1.0 / scale) * qf * aq)).astype(BF)
            dhid[1, rows, lanes] = (kinv[o, g].astype(F32) * (dk - kf * ak)).astype(BF)
            dhid[2, rows, lanes] = dv.astype(BF)
        run_in("r", it)

        @pl.when(lax.rem(it, 4) == 3)
        def _():
            moved = sum(
                nt(dhid[i, :, half], wqkv[:, pl.ds(pl.multiple_of(512 * i + 256 * p, 256), 256)])
                for i in range(3)
            )
            for w in range(4):
                for bcol in range(2):
                    for br in range(2):
                        at = 256 * w + (bcol * 2 + br) * 64
                        dmid[home(w, bcol, br)] += moved[at : at + 64, :]
            xflat = xroll[...].reshape(1024, 512)
            for i in range(3):
                grad = tn(xflat, dhid[i, :, half]).astype(BF)
                act[p, 512 * (i // 2) : 512 * (i // 2) + 512, 256 * (i % 2) : 256 * (i % 2) + 256] = grad

        run_in("gq", jnp.where(lax.rem(it, 4) == 3, p, -1))
        return 0

    lax.fori_loop(0, 8, retreat, 0)

    def gin_copy(w):
        return remote(slope.at[w], gin_hbm.at[me, 0], s_gin.at[w], r_gin.at[me], (img, w))

    def finish(w, _):
        quads = [[dmid[w, 2 * qr + qc] for qc in range(2)] for qr in range(2)]
        slope[w] = from_blocks(quads).astype(BF)

        @pl.when(w != me)
        def _():
            gin_copy(w).start()

        return 0

    lax.fori_loop(0, 4, finish, 0)
    own_gin = pltpu.make_async_copy(slope.at[me], gin_hbm.at[me, 0], r_gin.at[me])
    own_gin.start()
    run("finish")

    row_ones = jnp.ones((8, 1024), BF)

    def put(row, v):
        small_s[0, row : row + v.shape[0], :] = v

    put(ROW_QB, nn(row_ones, dhid[0])[0:1])
    put(ROW_VB, nn(row_ones, dhid[2])[0:1])
    put(ROW_BP, nn(row_ones, cr[...].reshape(1024, 512))[0:1])
    for row, i in ((ROW_LS, 9), (ROW_G1, 7), (ROW_S1, 8), (ROW_B2, 2), (ROW_G2, 0), (ROW_S2, 1)):
        put(row, jnp.sum(acc_s[i], axis=0, keepdims=True))
    for c in range(4):
        put(ROW_BE + c, jnp.sum(acc_s[3 + c], axis=0, keepdims=True))
    run("puts")
    short = jnp.zeros((384, 256), F32)
    for c in range(4):
        places = one_hot_places(c)
        left = jnp.concatenate(
            [bias[:, :, 8 * r : 8 * r + 8, :].reshape(384, 128) for r in range(4 * c, 4 * c + 4)], axis=1
        )
        for p in split3(left)[:2]:
            short = short + nt(p, places)
    pick = one_hot_pick()
    for i in range(4):
        piece = split3(short[96 * i : 96 * i + 96])[:2]
        part[4 * i : 4 * i + 4] = sum(nt(p, pick) for p in piece).reshape(4, 24, 1024)
    run("bb")
    dtab = jnp.zeros((16, 1024), F32)
    for u in range(24):
        dtab = dtab + pltpu.roll(part[:, u, :], 23 - u, 1)
    tab[...] = dtab * tab[...] * (1.0 - tab[...] * (1.0 / BIAS_RANGE))
    small_s[0, ROW_W1 : ROW_W2 + 16, :] = jnp.zeros((ROW_W2 + 16 - ROW_W1, 512), F32)

    def net_back(c, _):
        cols, pre = net_piece(c)
        cap, low = gelu_parts(pre)
        dlog, dlog_lo, _ = split3(tab[:, cols])
        units, units_lo, _ = split3(pre * cap)
        small_s[0, ROW_W2 : ROW_W2 + 16, :] += nn(dlog, units) + nn(dlog_lo, units) + nn(dlog, units_lo)
        w_hi, w_lo, _ = split3(w2t[...])
        back = tn(dlog, w_hi) + tn(dlog_lo, w_hi) + tn(dlog, w_lo)
        dpre, dpre_lo, _ = split3(back * (cap + pre * low))
        hi, mid, _ = split3(crow[:, cols])
        net = nn(hi, dpre) + nn(mid, dpre) + nn(hi, dpre_lo)
        small_s[0, ROW_W1 : ROW_W1 + 3, :] += net[0:3]
        return 0

    lax.fori_loop(0, 4, net_back, 0)
    run("net")
    for k in (1, 2, 3):
        frm = ring_from(k)
        x_send(k, 0).wait_send()
        x_send(k, 1).wait_send()
        spread(cot_hbm, cr, s_c, r_c, k).wait_send()
        res_copy(lax.rem(me + k, n_win)).wait_send()
        remote(xr.at[frm], res_hbm.at[frm, 0], s_res.at[frm], r_res.at[frm], (img, frm)).wait_recv()
    own_res.wait()
    own_gin.wait()
    last = {at: j for at, j in SCHEDULE["end"]}
    late = [at for at, group in enumerate(groups) if last.get(at) == len(group) - 2]
    for at, group in enumerate(groups):
        if at not in late:
            group[-1]()
    for at, j in SCHEDULE["end"]:
        groups[at][j]()
        if at in late and j == len(groups[at]) - 2:
            groups[at][-1]()

    for k in (1, 2, 3):
        frm, to = ring_from(k), lax.rem(me + k, n_win)
        gin_copy(to).wait_send()
        remote(slope.at[frm], gin_hbm.at[frm, 0], s_gin.at[frm], r_gin.at[frm], (img, frm)).wait_recv()


def widen_kernel(
    res, gin, wide, qkv, small,
    res_out, gin_out, w_qkv, g_qb, g_vb, g_ls, g_w1, g_b1, g_w2, w_proj, g_bp, g_g1, g_s1, w_fc1, g_be,
    w_fc2, g_b2, g_g2, g_s2,
    blocks, wide_in, qkv_in, wide_f, qkv_f, s_in, s_out, s_blocks,
):
    taken = [pltpu.make_async_copy(a, blocks.at[i], s_blocks.at[i]) for i, a in enumerate((res, gin))]
    passed = [pltpu.make_async_copy(blocks.at[i], a, s_blocks.at[2 + i]) for i, a in enumerate((res_out, gin_out))]
    pieces = []
    for i in range(9):
        if i < 4:
            place = w_fc2.at[pl.ds(512 * i, 512), :]
        elif i < 8:
            place = w_fc1.at[:, pl.ds(512 * (i - 4), 512)]
        else:
            place = w_proj
        pieces.append((wide.at[i], wide_in.at[i], wide_f.at[i], place))
    for i in range(6):
        place = w_qkv.at[:, pl.ds(512 * (i % 3) + 256 * (i // 3), 256)]
        pieces.append((qkv.at[i // 3, i % 3], qkv_in.at[i], qkv_f.at[i], place))
    loads = [pltpu.make_async_copy(a, b, s_in.at[i]) for i, (a, b, _, _) in enumerate(pieces)]
    stores = [pltpu.make_async_copy(c, d, s_out.at[i]) for i, (_, _, c, d) in enumerate(pieces)]
    for c in loads:
        c.start()
    for c in taken:
        c.start()
    for i, (_, b, c, _) in enumerate(pieces):
        loads[i].wait()
        c[...] = b[...].astype(F32)
        stores[i].start()
    for a, b in zip(taken, passed):
        a.wait()
        b.start()
    for row, out in (
        (ROW_QB, g_qb), (ROW_VB, g_vb), (ROW_B1, g_b1), (ROW_BP, g_bp), (ROW_G1, g_g1), (ROW_S1, g_s1),
        (ROW_B2, g_b2), (ROW_G2, g_g2), (ROW_S2, g_s2),
    ):
        out[...] = small[row, :]
    for c in range(4):
        g_be[512 * c : 512 * c + 512] = small[ROW_BE + c, :]
    g_w1[...] = small[ROW_W1 : ROW_W1 + 2, :]
    g_w2[...] = small[ROW_W2 : ROW_W2 + 16, :]
    h0 = lax.broadcasted_iota(jnp.int32, (512, 16), 0) // 32
    h1 = lax.broadcasted_iota(jnp.int32, (512, 16), 1)
    heads = jnp.where(h0 == h1, 1.0, 0.0).astype(BF)
    per_head = sum(nn(jnp.broadcast_to(p, (8, 512)), heads) for p in split3(small[ROW_LS : ROW_LS + 1, :]))
    g_ls[...] = per_head[0, :]
    for c in passed + stores:
        c.wait()


def body(n_img, n_win, inputs, wqkv, qb, vb, hls, w1, b1, w2, wproj, bproj, g1, s1, we, be, wc, bc, g2, s2, cot):
    extra = n_img // 8
    crow = table_coords()
    dma = pltpu.SemaphoreType.DMA
    n_sm = 4 + (extra - 1)
    vmem = pl.BlockSpec(memory_space=pltpu.VMEM)
    hbm = pl.BlockSpec(memory_space=pl.ANY)
    smem = pl.BlockSpec(memory_space=pltpu.SMEM)
    scratch = [
        pltpu.VMEM((4, TOK, 512), BF),
        pltpu.VMEM((4, TOK, 512), BF),
        pltpu.VMEM((4, TOK, 512), BF),
        pltpu.VMEM((16, 3, 128, 128), F32),
        pltpu.VMEM((4, 4, 4, TOK, TOK), BF),
        pltpu.VMEM((4, 4, TOK, 128), BF),
        pltpu.VMEM((4, 4, TOK, 128), BF),
        pltpu.VMEM((4, 4, TOK, 128), BF),
        pltpu.VMEM((4, 4, TOK, 128), BF),
        pltpu.VMEM((4, 4, TOK, 128), BF),
        pltpu.VMEM((4, 4, TOK, 128), F32),
        pltpu.VMEM((4, TOK, 512), BF),
        pltpu.VMEM((4, TOK, 512), BF),
        pltpu.VMEM((4, 4, 64, 512), BF),
        pltpu.VMEM((4, 4, 64, 512), F32),
        pltpu.VMEM((4, 1024, 512), BF),
        pltpu.VMEM((4, 1024, 512), BF),
        pltpu.VMEM((1024, 512), BF),
        pltpu.VMEM((1024, 512), BF),
        pltpu.VMEM((4, TOK, 512), BF),
        pltpu.VMEM((16, 1024), F32),
        pltpu.VMEM((16, 24, 1024), F32),
        pltpu.VMEM((10, 8, 512), F32),
        pltpu.VMEM((9, 512, 512), BF),
        pltpu.VMEM((9, 496, 512), BF),
        pltpu.VMEM((15, extra - 1, 16, 512) if extra > 1 else (1, 1, 16, 512), BF),
        pltpu.VMEM((512, 1536), BF),
        pltpu.VMEM((512, 512), BF),
        pltpu.VMEM((512, 2048), BF),
        pltpu.VMEM((2048, 512), BF),
        pltpu.VMEM((512,), F32), pltpu.VMEM((512,), F32),
        pltpu.VMEM((2, 512), F32), pltpu.VMEM((512,), F32), pltpu.VMEM((16, 512), F32),
        pltpu.VMEM((512,), F32), pltpu.VMEM((512,), F32), pltpu.VMEM((512,), F32),
        pltpu.VMEM((2048,), F32), pltpu.VMEM((512,), F32),
        pltpu.VMEM((512,), F32), pltpu.VMEM((512,), F32), pltpu.VMEM((8, 1024), F32),
        pltpu.VMEM((4, SMALL_ROWS, 512), F32),
        pltpu.VMEM((16, 512), F32),
        pltpu.VMEM((3, 16, 512), F32),
        pltpu.VMEM((3, 16, 512), F32),
        pltpu.VMEM((max(extra - 1, 1), 16, 512), F32),
        pltpu.VMEM((SMALL_ROWS, 512), F32),
        dma((2, 4)), dma((2, 4)), dma((4,)), dma((4,)),
        dma((4,)), dma((4,)), dma((4,)), dma((4,)),
        dma((15, 1 + extra)), dma((15, 9 + extra)), dma((15,)),
        dma((n_sm,)), dma((n_sm,)),
        dma((4,)), dma((13,)),
    ]
    block = jax.ShapeDtypeStruct(inputs.shape, BF)
    result, grad_inputs, wide, qkv, small = pl.pallas_call(
        functools.partial(block_kernel, n_img, n_win),
        out_shape=(
            block,
            block,
            jax.ShapeDtypeStruct((9, 512, 512), BF),
            jax.ShapeDtypeStruct((2, 3, 512, 256), BF),
            jax.ShapeDtypeStruct((SMALL_ROWS, 512), F32),
        ),
        in_specs=[hbm] * 6 + [smem] + [hbm] * 13,
        out_specs=(hbm, hbm, hbm, hbm, vmem),
        scratch_shapes=scratch,
        compiler_params=pltpu.CompilerParams(
            collective_id=0, has_side_effects=True, vmem_limit_bytes=64 * 1024 * 1024
        ),
    )(
        inputs, cot, wqkv, wproj, we, wc, hls, qb, vb, w1, b1, w2.T, bproj, g1, s1, be, bc, g2, s2,
        jnp.asarray(crow),
    )
    any_ = lambda shape: jax.ShapeDtypeStruct(shape, F32)
    outs = pl.pallas_call(
        widen_kernel,
        out_shape=(
            block, block, any_((512, 1536)), any_((512,)), any_((512,)), any_((16,)), any_((2, 512)),
            any_((512,)), any_((16, 512)), any_((512, 512)), any_((512,)), any_((512,)), any_((512,)),
            any_((512, 2048)), any_((2048,)), any_((2048, 512)), any_((512,)), any_((512,)), any_((512,)),
        ),
        in_specs=[hbm] * 4 + [vmem],
        out_specs=tuple(hbm if i in (0, 1, 2, 9, 13, 15) else vmem for i in range(19)),
        scratch_shapes=[
            pltpu.VMEM((2,) + inputs.shape, BF),
            pltpu.VMEM((9, 512, 512), BF),
            pltpu.VMEM((6, 512, 256), BF),
            pltpu.VMEM((9, 512, 512), F32),
            pltpu.VMEM((6, 512, 256), F32),
            dma((15,)), dma((15,)), dma((4,)),
        ],
        compiler_params=pltpu.CompilerParams(vmem_limit_bytes=63 * 1024 * 1024),
    )(result, grad_inputs, wide, qkv, small)
    return outs[:8] + (outs[8].T,) + outs[9:]


def solution(mesh):
    n_img, n_win = mesh.shape["img"], mesh.shape["win"]
    block = P("img", "win", None, None)
    return jax.shard_map(
        functools.partial(body, n_img, n_win),
        mesh=mesh,
        in_specs=(block,) + (P(),) * 17 + (block,),
        out_specs=(block, block) + (P(),) * 17,
        check_vma=False,
    )
```
